32 devices in a mesh: dp: 8 (over z, x), expert: 4 (over y, core).
Axes of the slice: x: 2, y: 2, z: 4, core: 2. Of those that a mesh axis runs over, the one named last changes fastest.
Arguments:
- tokens: bfloat16 [128, 4096], P(('dp', 'expert')), may hold values from -6 to 6
- expert_ids: int32 [128, 2], P(('dp', 'expert')), may hold values from 0 to 3, all different within a row; in each aligned block of 16 rows (0 to 15, 16 to 31, ...) at most 16 rows name the same one
- route_weights: bfloat16 [128, 2], P(('dp', 'expert')), may hold values from 0.099609375 to 1
- out_grad: bfloat16 [128, 4096], P(('dp', 'expert')), may hold values from -6 to 6
- gate_weight: bfloat16 [4, 1536, 4096], P('expert', 'dp'), may hold values from -0.09375 to 0.09375
- up_weight: bfloat16 [4, 1536, 4096], P('expert', 'dp'), may hold values from -0.09375 to 0.09375
- down_weight: bfloat16 [4, 1536, 4096], P('expert', 'dp'), may hold values from -0.15625 to 0.15625
Outputs:
- mixed: bfloat16 [128, 4096], P(('dp', 'expert'))
- input_grad: bfloat16 [128, 4096], P(('dp', 'expert'))
- gate_grad: bfloat16 [4, 1536, 4096], P('expert', 'dp')
- up_grad: bfloat16 [4, 1536, 4096], P('expert', 'dp')
- down_grad: bfloat16 [4, 1536, 4096], P('expert', 'dp')
The draws below stay inside these ranges and needn't reach their ends.
Inputs may be any that keep to these rules, and one draw needn't show every extreme that they name: `expert_ids`: each row names 2 different experts. In each aligned block of 16 rows (the tokens of one index of dp) no expert is named by more than 16 rows, a bound that some block reaches.
All inputs are finite; a program needn't handle non-finite values.
Results may differ from the reference program's by a relative error of at most 0.024.
Values may be sent and summed in bfloat16 or wider, within the bound.
No kernel may reach another device: no remote copies, remote signals or barrier semaphores. Data moves between devices by JAX's collectives and lax.ppermute only.
A program may use at most 64 MiB of HBM per device.

```python
import math
import jax
import jax.numpy as jnp
import numpy as np
from jax import lax

D = 4096
FF = 1536
TOP = 2
EXPERTS = 4
GROUP_TOK = 16
ROW_CAP = 16
TOKENS = 128
N_DP = 8


def level_of(stream_key, extent, cuts, smallest, largest):
    level = 1.0
    for axis_at, parts in cuts:
        draws = jax.random.uniform(jax.random.fold_in(jax.random.fold_in(stream_key, 6), axis_at), (parts,), jnp.float32, smallest / len(cuts), largest / len(cuts))
        level = level * jnp.repeat(jnp.exp(draws), extent[axis_at] // parts).reshape((-1,) + (1,) * (len(extent) - 1 - axis_at))
    return level


def shared_out(stream_key, own, number, rows, amount, top, most, skew):
    sequence = jax.random.permutation(stream_key, amount)
    packed, ordinary = portions_of(amount, rows * top, most, skew, True), portions_of(amount, rows * top, most, skew, False)
    places = jnp.arange(amount)

    def named(tallies, turn):
        used = int((tallies > 0).sum())
        fixed = max(1, used // 4)
        moved = fixed + (places - fixed + turn * (used - fixed)) % max(1, amount - fixed)
        return jnp.zeros((amount,), jnp.int32).at[sequence[jnp.where(places < fixed, places, moved)]].set(jnp.asarray(tallies, jnp.int32))

    tallies = jnp.where(number % 4 == 0, named(packed, number // 4), named(ordinary, number - number // 4 - 1))
    mixed = jax.random.permutation(jax.random.fold_in(own, 3), amount)
    giver, sink = mixed[0:amount // 2 * 2:2], mixed[1:amount // 2 * 2:2]
    margin = jnp.minimum(tallies[giver] - 1, most - tallies[sink]) // 2
    margin = jnp.where((giver == sequence[0]) | (sink == sequence[0]) | (tallies[sink] == 0), 0, jnp.maximum(margin, 0))
    moved = jax.random.randint(jax.random.fold_in(own, 4), (amount // 2,), 0, 1 << 20) % (margin + 1)
    tallies = tallies.at[giver].add(-moved).at[sink].add(moved)
    labels = jnp.searchsorted(jnp.cumsum(tallies), jnp.arange(rows * top), side="right").astype(jnp.int32)
    listing = labels.reshape(top, rows).T
    listing = listing[jax.random.permutation(jax.random.fold_in(own, 1), rows)]
    turn = jax.random.randint(jax.random.fold_in(own, 2), (rows, 1), 0, top)
    return jnp.take_along_axis(listing, (jnp.arange(top)[None, :] + turn) % top, axis=1)


def portions_of(number_of, total, bound, skew, full):
    loads = [(1 << 20) // math.isqrt(standing ** skew) + 1 for standing in range(1, number_of + 1)]
    largest = bound if full else min(bound, max(-(-total // number_of), total * loads[0] // sum(loads)))
    least = 1 if total - largest >= number_of - 1 else 0
    given, rest = [largest] + [least] * (number_of - 1), total - largest - least * (number_of - 1)
    while rest > 0:
        free = [i for i in range(1, number_of) if given[i] < largest] or [i for i in range(1, number_of) if given[i] < bound]
        mass, remaining = sum([loads[i] for i in free]), rest
        for i in free:
            more = min(bound - given[i], max(1, remaining * loads[i] // mass), rest)
            given[i] = given[i] + more
            rest = rest - more
    return np.array(given)


def noise(key, shape, scale, reach, shards=(), held_as=jnp.bfloat16):
    values = jax.random.normal(key, shape, jnp.float32) * scale
    if len(shards) > 0:
        values = level_of(key, shape, shards, -0.22, 0.18) * values
    return jnp.clip(values, min=-reach, max=reach).astype(held_as)


def setup_inputs(seed: int = 0) -> dict:
    seeds = jax.random.split(jax.random.key(seed), 8)
    tokens = noise(seeds[0], (TOKENS, D), 1.0, 6.0, ((0, 32),))
    expert_ids_keys = jax.random.split(jax.random.fold_in(seeds[1], 1), TOKENS // GROUP_TOK)
    expert_ids_turns = jax.random.permutation(jax.random.fold_in(seeds[1], 3), TOKENS // GROUP_TOK)
    expert_ids = jax.vmap(lambda own, number: shared_out(jax.random.fold_in(seeds[1], 2), own, number, GROUP_TOK, EXPERTS, TOP, ROW_CAP, 2))(expert_ids_keys, expert_ids_turns).reshape((TOKENS, TOP))
    route_weights = jnp.clip(jnp.exp(math.log(1.0) - 2.306499 * jax.random.uniform(seeds[2], (TOKENS, TOP), jnp.float32) ** level_of(seeds[2], (TOKENS, TOP), ((0, 32),), -0.2, 0.2)), 0.099609375, 1.0).astype(jnp.bfloat16)
    out_grad = noise(seeds[3], (TOKENS, D), 1.0, 6.0, ((0, 32),))
    gate_weight = noise(seeds[4], (EXPERTS, FF, D), D ** -0.5, 0.09375, ((0, 4), (1, 8)))
    up_weight = noise(seeds[5], (EXPERTS, FF, D), D ** -0.5, 0.09375, ((0, 4), (1, 8)))
    down_weight = noise(seeds[6], (EXPERTS, FF, D), FF ** -0.5, 0.15625, ((0, 4), (1, 8)))
    return {"tokens": tokens, "expert_ids": expert_ids, "route_weights": route_weights, "out_grad": out_grad, "gate_weight": gate_weight, "up_weight": up_weight, "down_weight": down_weight}


def contract_rows(left, right):
    return lax.dot_general(left, right, (((1,), (1,)), ((), ())), preferred_element_type=jnp.float32)


def contract_first(left, right):
    return lax.dot_general(left, right, (((0,), (0,)), ((), ())), preferred_element_type=jnp.float32)


def grouped_sum(acts, weights):
    slot_total = acts.shape[0]
    group_width = FF // N_DP
    act_groups = acts.reshape(slot_total, N_DP, group_width).astype(jnp.float32)
    weight_groups = weights.reshape(N_DP, group_width, weights.shape[1]).astype(jnp.float32)
    partial_value = jnp.einsum("snf,nfd->nsd", act_groups, weight_groups)
    rounded = lax.optimization_barrier(partial_value.astype(jnp.bfloat16))
    return jnp.sum(rounded.astype(jnp.float32), axis=0)


def grouped_pair(first_acts, first_weights, second_acts, second_weights):
    slot_total = first_acts.shape[0]
    group_width = FF // N_DP
    width = first_weights.shape[1]
    first_groups = first_acts.reshape(slot_total, N_DP, group_width).astype(jnp.float32)
    second_groups = second_acts.reshape(slot_total, N_DP, group_width).astype(jnp.float32)
    partial_value = jnp.einsum("snf,nfd->nsd", first_groups, first_weights.reshape(N_DP, group_width, width).astype(jnp.float32))
    partial_value = partial_value + jnp.einsum("snf,nfd->nsd", second_groups, second_weights.reshape(N_DP, group_width, width).astype(jnp.float32))
    rounded = lax.optimization_barrier(partial_value.astype(jnp.bfloat16))
    return jnp.sum(rounded.astype(jnp.float32), axis=0)


def reference(tokens, expert_ids, route_weights, out_grad, gate_weight, up_weight, down_weight):
    token_count = tokens.shape[0]
    slot_total = N_DP * ROW_CAP
    positions = jnp.arange(token_count, dtype=jnp.int32)
    route_float = route_weights.astype(jnp.float32)
    grad_float = out_grad.astype(jnp.float32)

    def per_expert(totals, inputs):
        mixed_total, input_total = totals
        w_gate, w_up, w_down, expert = inputs
        matches = expert_ids == expert
        routed = jnp.any(matches, axis=1)
        weight = jnp.sum(jnp.where(matches, route_float, 0.0), axis=1)
        order_key = jnp.where(routed, positions, positions + token_count).astype(jnp.int32)
        slot_order = jnp.argsort(order_key)[:slot_total].astype(jnp.int32)
        slot_valid = routed[slot_order]
        slot_weight = jnp.where(slot_valid, weight[slot_order], 0.0)
        rows_x = jnp.where(slot_valid[:, None], tokens[slot_order], jnp.zeros((), jnp.bfloat16))
        rows_dy = (slot_weight[:, None] * grad_float[slot_order]).astype(jnp.bfloat16)
        gate_pre = contract_rows(rows_x, w_gate)
        up_pre = contract_rows(rows_x, w_up)
        gate_sig = jax.nn.sigmoid(gate_pre)
        silu_gate = gate_pre * gate_sig
        hidden = (silu_gate * up_pre).astype(jnp.bfloat16)
        expert_out = grouped_sum(hidden, w_down).astype(jnp.bfloat16)
        hidden_grad = contract_rows(rows_dy, w_down)
        silu_slope = gate_sig * (1.0 + gate_pre * (1.0 - gate_sig))
        gate_act = (hidden_grad * up_pre * silu_slope).astype(jnp.bfloat16)
        up_act = (hidden_grad * silu_gate).astype(jnp.bfloat16)
        grad_down = contract_first(hidden, rows_dy).astype(jnp.bfloat16)
        grad_gate = contract_first(gate_act, rows_x).astype(jnp.bfloat16)
        grad_up = contract_first(up_act, rows_x).astype(jnp.bfloat16)
        expert_in = grouped_pair(gate_act, w_gate, up_act, w_up).astype(jnp.bfloat16)
        mixed_total = mixed_total.at[slot_order].add(slot_weight[:, None] * expert_out.astype(jnp.float32))
        input_total = input_total.at[slot_order].add(jnp.where(slot_valid[:, None], expert_in.astype(jnp.float32), 0.0))
        return (mixed_total, input_total), (grad_gate, grad_up, grad_down)

    start_totals = (jnp.zeros(tokens.shape, jnp.float32), jnp.zeros(tokens.shape, jnp.float32))
    experts_all = jnp.arange(gate_weight.shape[0], dtype=jnp.int32)
    totals, grads = lax.scan(per_expert, start_totals, (gate_weight, up_weight, down_weight, experts_all))
    mixed = totals[0].astype(jnp.bfloat16)
    input_grad = totals[1].astype(jnp.bfloat16)
    return mixed, input_grad, grads[0], grads[1], grads[2]
```

```python
import jax
import jax.numpy as jnp
from jax import lax
from jax.sharding import PartitionSpec as P

ROW_CAP = 16
AXES = ("dp", "expert")


def contract_rows(left, right):
    return lax.dot_general(
        left, right, (((1,), (1,)), ((), ())), preferred_element_type=jnp.float32
    )


def contract_first(left, right):
    return lax.dot_general(
        left, right, (((0,), (0,)), ((), ())), preferred_element_type=jnp.float32
    )


def slotted(tokens, expert_ids, route_weights, out_grad, gate_weight, up_weight, down_weight):
    expert = lax.axis_index("expert")
    width = tokens.shape[1]
    local_tokens = tokens.shape[0]
    group_x, group_dy, group_w = (
        lax.all_gather(tokens, "expert", axis=0, tiled=True),
        lax.all_gather(out_grad, "expert", axis=0, tiled=True),
        lax.all_gather(route_weights, "expert", axis=0, tiled=True),
    )
    group_ids = lax.all_gather(expert_ids, "expert", axis=0, tiled=True)
    matches = group_ids == expert
    routed = jnp.any(matches, axis=1)
    weight = jnp.sum(jnp.where(matches, group_w.astype(jnp.float32), 0.0), axis=1)
    slot_rank = jnp.cumsum(routed.astype(jnp.int32)) - 1
    slot_index = jnp.arange(ROW_CAP, dtype=jnp.int32)
    picker = ((slot_rank[None, :] == slot_index[:, None]) & routed[None, :]).astype(jnp.bfloat16)
    slot_x = jnp.dot(picker, group_x, preferred_element_type=jnp.float32).astype(jnp.bfloat16)
    scaled = (weight[:, None] * group_dy.astype(jnp.float32)).astype(jnp.bfloat16)
    slot_dy = jnp.dot(picker, scaled, preferred_element_type=jnp.float32).astype(jnp.bfloat16)
    w_gate = gate_weight[0]
    w_up = up_weight[0]
    w_down = down_weight[0]
    all_x = lax.all_gather(slot_x, "dp", axis=0, tiled=True)
    gate_pre = contract_rows(w_gate, all_x)
    up_pre = contract_rows(w_up, all_x)
    gate_sig = jax.nn.sigmoid(gate_pre)
    silu_gate = gate_pre * gate_sig
    hidden = (silu_gate * up_pre).astype(jnp.bfloat16)
    expert_out = lax.psum_scatter(
        contract_first(hidden, w_down).astype(jnp.bfloat16), "dp", scatter_dimension=0, tiled=True
    )
    all_dy = lax.all_gather(slot_dy, "dp", axis=0, tiled=True)
    hidden_grad = contract_rows(w_down, all_dy)
    silu_slope = gate_sig * (1.0 + gate_pre * (1.0 - gate_sig))
    gate_act = (hidden_grad * up_pre * silu_slope).astype(jnp.bfloat16)
    up_act = (hidden_grad * silu_gate).astype(jnp.bfloat16)
    grad_down = jnp.dot(hidden, all_dy, preferred_element_type=jnp.float32).astype(jnp.bfloat16)
    grad_gate = jnp.dot(gate_act, all_x, preferred_element_type=jnp.float32).astype(jnp.bfloat16)
    grad_up = jnp.dot(up_act, all_x, preferred_element_type=jnp.float32).astype(jnp.bfloat16)
    expert_in = lax.psum_scatter(
        (contract_first(gate_act, w_gate) + contract_first(up_act, w_up)).astype(jnp.bfloat16),
        "dp",
        scatter_dimension=0,
        tiled=True,
    )
    back_out = contract_first(picker, expert_out).astype(jnp.bfloat16)
    back_in = contract_first(picker, expert_in).astype(jnp.bfloat16)
    got_out, got_in = (
        lax.all_to_all(back_out, "expert", split_axis=0, concat_axis=0, tiled=True),
        lax.all_to_all(back_in, "expert", split_axis=0, concat_axis=0, tiled=True),
    )
    expert_count = lax.axis_size("expert")
    got_out = got_out.reshape(expert_count, local_tokens, width)
    got_in = got_in.reshape(expert_count, local_tokens, width)
    expert_range = jnp.arange(expert_count, dtype=jnp.int32)
    own_match = expert_ids[:, :, None] == expert_range[None, None, :]
    mix_weight = jnp.sum(
        jnp.where(own_match, route_weights.astype(jnp.float32)[:, :, None], 0.0), axis=1
    )
    mixed_out = jnp.sum(jnp.transpose(mix_weight)[:, :, None] * got_out.astype(jnp.float32), axis=0)
    input_total = jnp.sum(got_in.astype(jnp.float32), axis=0)
    return (
        mixed_out.astype(jnp.bfloat16),
        input_total.astype(jnp.bfloat16),
        grad_gate[None],
        grad_up[None],
        grad_down[None],
    )


def bit_stages(devices):
    bits = devices.bit_length() - 1
    stages, high = [], bits - 1
    while high > 0:
        low = max(high - 1, 1)
        stages.append(tuple(k << low for k in range(1, 1 << (high - low + 1))))
        high = low - 1
    stages.append((1,))
    return stages


def from_xor(value, mask, devices):
    return lax.ppermute(value, AXES, [(i, i ^ mask) for i in range(devices)])


def route_columns(expert_ids, route_weights, experts):
    named = expert_ids[:, :, None] == jnp.arange(experts, dtype=jnp.int32)[None, None, :]
    return jnp.sum(jnp.where(named, route_weights.astype(jnp.float32)[:, :, None], 0.0), axis=1)


def dense(tokens, expert_ids, route_weights, out_grad, gate_weight, up_weight, down_weight):
    experts = lax.axis_size("expert")
    devices = lax.axis_size("dp") * experts
    expert = lax.axis_index("expert")
    rows, width = tokens.shape
    w_gate, w_up, w_down = gate_weight[0], up_weight[0], down_weight[0]
    stages = bit_stages(devices)

    route = route_columns(expert_ids, route_weights, experts).astype(jnp.bfloat16)
    route = jnp.pad(route, ((0, 0), (0, -experts % 128)))
    have = jnp.concatenate([tokens, out_grad, route], axis=1)
    for masks in stages:
        have = jnp.concatenate([have] + [from_xor(have, m, devices) for m in masks], axis=0)
    all_x, all_dy, all_route = have[:, :width], have[:, width : 2 * width], have[:, 2 * width :]
    mine = jnp.arange(all_route.shape[1]) == expert
    weight = jnp.sum(jnp.where(mine[None, :], all_route.astype(jnp.float32), 0.0), axis=1)[:, None]

    gate_pre = contract_rows(all_x, w_gate)
    up_pre = contract_rows(all_x, w_up)
    hidden_grad = weight * contract_rows(all_dy, w_down)
    gate_sig = jax.nn.sigmoid(gate_pre)
    silu_gate = gate_pre * gate_sig
    hidden = (weight * (silu_gate * up_pre)).astype(jnp.bfloat16)
    silu_slope = gate_sig * (1.0 + gate_pre * (1.0 - gate_sig))
    gate_act = (hidden_grad * up_pre * silu_slope).astype(jnp.bfloat16)
    up_act = (hidden_grad * silu_gate).astype(jnp.bfloat16)

    out = jnp.dot(hidden, w_down, preferred_element_type=jnp.float32)
    into = jnp.dot(gate_act, w_gate, preferred_element_type=jnp.float32) + jnp.dot(
        up_act, w_up, preferred_element_type=jnp.float32
    )
    total = jnp.concatenate([out.astype(jnp.bfloat16), into.astype(jnp.bfloat16)], axis=1)
    for masks in reversed(stages):
        part = total.shape[0] // (len(masks) + 1)
        pieces = [total[k * part : (k + 1) * part] for k in range(len(masks) + 1)]
        summed = pieces[0].astype(jnp.float32)
        for m, piece in zip(masks, pieces[1:]):
            summed = summed + from_xor(piece, m, devices).astype(jnp.float32)
        total = summed.astype(jnp.bfloat16)

    grad_down = contract_first(hidden, all_dy).astype(jnp.bfloat16)
    grad_gate = contract_first(gate_act, all_x).astype(jnp.bfloat16)
    grad_up = contract_first(up_act, all_x).astype(jnp.bfloat16)
    return total[:, :width], total[:, width:], grad_gate[None], grad_up[None], grad_down[None]


def shards(tokens, *others):
    experts = lax.axis_size("expert")
    devices = lax.axis_size("dp") * experts
    whole_group = tokens.shape[0] * experts <= ROW_CAP
    if whole_group and devices & (devices - 1) == 0:
        return dense(tokens, *others)
    return slotted(tokens, *others)


def solution(mesh):
    return jax.shard_map(
        shards,
        mesh=mesh,
        in_specs=(
            P(("dp", "expert"), None),
            P(("dp", "expert"), None),
            P(("dp", "expert"), None),
            P(("dp", "expert"), None),
            P("expert", "dp", None),
            P("expert", "dp", None),
            P("expert", "dp", None),
        ),
        out_specs=(
            P(("dp", "expert"), None),
            P(("dp", "expert"), None),
            P("expert", "dp", None),
            P("expert", "dp", None),
            P("expert", "dp", None),
        ),
        check_vma=False,
    )
```

```python
import functools

import jax
import jax.numpy as jnp
from jax import lax
from jax.experimental import pallas as pl
from jax.experimental.pallas import tpu as pltpu
from jax.sharding import PartitionSpec as P

ROW_CAP = 16
AXES = ("dp", "expert")


def contract_rows(left, right):
    return lax.dot_general(
        left, right, (((1,), (1,)), ((), ())), preferred_element_type=jnp.float32
    )


def contract_first(left, right):
    return lax.dot_general(
        left, right, (((0,), (0,)), ((), ())), preferred_element_type=jnp.float32
    )


def slotted(tokens, expert_ids, route_weights, out_grad, gate_weight, up_weight, down_weight):
    expert = lax.axis_index("expert")
    width = tokens.shape[1]
    local_tokens = tokens.shape[0]
    group_x, group_dy, group_w = (
        lax.all_gather(tokens, "expert", axis=0, tiled=True),
        lax.all_gather(out_grad, "expert", axis=0, tiled=True),
        lax.all_gather(route_weights, "expert", axis=0, tiled=True),
    )
    group_ids = lax.all_gather(expert_ids, "expert", axis=0, tiled=True)
    matches = group_ids == expert
    routed = jnp.any(matches, axis=1)
    weight = jnp.sum(jnp.where(matches, group_w.astype(jnp.float32), 0.0), axis=1)
    slot_rank = jnp.cumsum(routed.astype(jnp.int32)) - 1
    slot_index = jnp.arange(ROW_CAP, dtype=jnp.int32)
    picker = ((slot_rank[None, :] == slot_index[:, None]) & routed[None, :]).astype(jnp.bfloat16)
    slot_x = jnp.dot(picker, group_x, preferred_element_type=jnp.float32).astype(jnp.bfloat16)
    scaled = (weight[:, None] * group_dy.astype(jnp.float32)).astype(jnp.bfloat16)
    slot_dy = jnp.dot(picker, scaled, preferred_element_type=jnp.float32).astype(jnp.bfloat16)
    w_gate = gate_weight[0]
    w_up = up_weight[0]
    w_down = down_weight[0]
    all_x = lax.all_gather(slot_x, "dp", axis=0, tiled=True)
    gate_pre = contract_rows(w_gate, all_x)
    up_pre = contract_rows(w_up, all_x)
    gate_sig = jax.nn.sigmoid(gate_pre)
    silu_gate = gate_pre * gate_sig
    hidden = (silu_gate * up_pre).astype(jnp.bfloat16)
    expert_out = lax.psum_scatter(
        contract_first(hidden, w_down).astype(jnp.bfloat16), "dp", scatter_dimension=0, tiled=True
    )
    all_dy = lax.all_gather(slot_dy, "dp", axis=0, tiled=True)
    hidden_grad = contract_rows(w_down, all_dy)
    silu_slope = gate_sig * (1.0 + gate_pre * (1.0 - gate_sig))
    gate_act = (hidden_grad * up_pre * silu_slope).astype(jnp.bfloat16)
    up_act = (hidden_grad * silu_gate).astype(jnp.bfloat16)
    grad_down = jnp.dot(hidden, all_dy, preferred_element_type=jnp.float32).astype(jnp.bfloat16)
    grad_gate = jnp.dot(gate_act, all_x, preferred_element_type=jnp.float32).astype(jnp.bfloat16)
    grad_up = jnp.dot(up_act, all_x, preferred_element_type=jnp.float32).astype(jnp.bfloat16)
    expert_in = lax.psum_scatter(
        (contract_first(gate_act, w_gate) + contract_first(up_act, w_up)).astype(jnp.bfloat16),
        "dp",
        scatter_dimension=0,
        tiled=True,
    )
    back_out = contract_first(picker, expert_out).astype(jnp.bfloat16)
    back_in = contract_first(picker, expert_in).astype(jnp.bfloat16)
    got_out, got_in = (
        lax.all_to_all(back_out, "expert", split_axis=0, concat_axis=0, tiled=True),
        lax.all_to_all(back_in, "expert", split_axis=0, concat_axis=0, tiled=True),
    )
    expert_count = lax.axis_size("expert")
    got_out = got_out.reshape(expert_count, local_tokens, width)
    got_in = got_in.reshape(expert_count, local_tokens, width)
    expert_range = jnp.arange(expert_count, dtype=jnp.int32)
    own_match = expert_ids[:, :, None] == expert_range[None, None, :]
    mix_weight = jnp.sum(
        jnp.where(own_match, route_weights.astype(jnp.float32)[:, :, None], 0.0), axis=1
    )
    mixed_out = jnp.sum(jnp.transpose(mix_weight)[:, :, None] * got_out.astype(jnp.float32), axis=0)
    input_total = jnp.sum(got_in.astype(jnp.float32), axis=0)
    return (
        mixed_out.astype(jnp.bfloat16),
        input_total.astype(jnp.bfloat16),
        grad_gate[None],
        grad_up[None],
        grad_down[None],
    )


def split_masks(devices):
    far = tuple(k << 1 for k in range(1, 4))
    near = tuple(k << 3 for k in range(1, devices >> 3))
    return near, far


def from_xor(value, mask, devices):
    return lax.ppermute(value, AXES, [(i, i ^ mask) for i in range(devices)])


def kernel_call(body, out_shape, scratch, cost, *operands):
    vmem, smem = pl.BlockSpec(memory_space=pltpu.VMEM), pl.BlockSpec(memory_space=pltpu.SMEM)
    specs = [smem if o.ndim == 1 else vmem for o in operands]
    return pl.pallas_call(
        body,
        out_shape=out_shape,
        in_specs=specs,
        out_specs=jax.tree.map(lambda _: vmem, out_shape),
        scratch_shapes=scratch,
        compiler_params=pltpu.CompilerParams(vmem_limit_bytes=24 << 20),
        cost_estimate=pl.CostEstimate(flops=cost, bytes_accessed=4 << 20, transcendentals=0),
    )(*operands)


def pack_body(x_ref, dy_ref, ids_ref, w_ref, msg_ref):
    rows, width = x_ref.shape
    top = ids_ref.shape[0]
    lanes = msg_ref.shape[1] - 2 * width
    msg_ref[:, :width] = x_ref[...]
    msg_ref[:, width : 2 * width] = dy_ref[...]
    diagonal = lax.broadcasted_iota(jnp.int32, (rows, rows), 0) == lax.broadcasted_iota(
        jnp.int32, (rows, rows), 1
    )
    expert = lax.broadcasted_iota(jnp.int32, (rows, lanes), 1)
    route = jnp.zeros((rows, lanes), jnp.float32)
    for k in range(top):
        named = jnp.sum(jnp.where(diagonal, ids_ref[k : k + 1, :], 0), axis=1, keepdims=True)
        weight = jnp.sum(jnp.where(diagonal, w_ref[k : k + 1, :], 0.0), axis=1, keepdims=True)
        route = route + jnp.where(expert == named, weight, 0.0)
    msg_ref[:, 2 * width :] = route.astype(jnp.bfloat16)


def gathered(pieces, into):
    rows = pieces[0].shape[0]
    for i, piece in enumerate(pieces):
        into[i * rows : (i + 1) * rows, :] = piece[...]


def projections(x, dy, wg_ref, wu_ref, wd_ref):
    return (
        contract_rows(x, wg_ref[0]),
        contract_rows(x, wu_ref[0]),
        contract_rows(dy, wd_ref[0]),
    )


def pre_body(count, width, *refs):
    pieces, (wg_ref, wu_ref, wd_ref, pre_ref, have) = refs[:count], refs[count:]
    gathered(pieces, have)
    ff = wg_ref.shape[1]
    pre = projections(have[:, :width], have[:, width : 2 * width], wg_ref, wu_ref, wd_ref)
    for i, value in enumerate(pre):
        pre_ref[:, i * ff : (i + 1) * ff] = value


def activations(pre, route, expert):
    gate_pre, up_pre, hidden_grad = pre
    lane = lax.broadcasted_iota(jnp.int32, route.shape, 1)
    weight = jnp.sum(jnp.where(lane == expert, route.astype(jnp.float32), 0.0), axis=1, keepdims=True)
    hidden_grad = weight * hidden_grad
    gate_sig = 1.0 / (1.0 + jnp.exp(-gate_pre))
    silu_gate = gate_pre * gate_sig
    hidden = weight * (silu_gate * up_pre)
    silu_slope = gate_sig * (1.0 + gate_pre * (1.0 - gate_sig))
    gate_act = hidden_grad * up_pre * silu_slope
    up_act = hidden_grad * silu_gate
    return [v.astype(jnp.bfloat16) for v in (gate_act, up_act, hidden)]


def outputs(acts, wg_ref, wu_ref, wd_ref):
    gate_act, up_act, hidden = acts
    out = jnp.dot(hidden, wd_ref[0], preferred_element_type=jnp.float32)
    into = jnp.dot(gate_act, wg_ref[0], preferred_element_type=jnp.float32) + jnp.dot(
        up_act, wu_ref[0], preferred_element_type=jnp.float32
    )
    return out, into


def act_body(count, width, *refs):
    own, other = refs[:count], refs[count : 2 * count]
    pre_ref, wg_ref, wu_ref, wd_ref, expert_ref, acts_ref, msg_ref, have = refs[2 * count :]
    half, ff, expert = have.shape[0], wg_ref.shape[1], expert_ref[0]
    gathered(other, have)
    pre = projections(have[:, :width], have[:, width : 2 * width], wg_ref, wu_ref, wd_ref)
    acts = activations(pre, have[:, 2 * width :], expert)
    for i, value in enumerate(acts):
        acts_ref[half:, i * ff : (i + 1) * ff] = value
    out, into = outputs(acts, wg_ref, wu_ref, wd_ref)
    msg_ref[:, :width] = out.astype(jnp.bfloat16)
    msg_ref[:, width:] = into.astype(jnp.bfloat16)
    route = jnp.concatenate([piece[:, 2 * width :] for piece in own], axis=0)
    pre = [pre_ref[:, i * ff : (i + 1) * ff] for i in range(3)]
    for i, value in enumerate(activations(pre, route, expert)):
        acts_ref[:half, i * ff : (i + 1) * ff] = value


def own_body(acts_ref, wg_ref, wu_ref, wd_ref, own_ref):
    half, ff = own_ref.shape[0], wg_ref.shape[1]
    width = own_ref.shape[1] // 2
    acts = [acts_ref[:half, i * ff : (i + 1) * ff] for i in range(3)]
    out, into = outputs(acts, wg_ref, wu_ref, wd_ref)
    own_ref[:, :width] = out
    own_ref[:, width:] = into


def grad_body(count, width, *refs):
    pieces, (acts_ref, gg_ref, gu_ref, gd_ref, have) = refs[:count], refs[count:]
    gathered(pieces, have)
    ff = gg_ref.shape[1]
    for i, (ref, side) in enumerate(((gg_ref, 0), (gu_ref, 0), (gd_ref, width))):
        ref[0] = contract_first(
            acts_ref[:, i * ff : (i + 1) * ff], have[:, side : side + width]
        ).astype(jnp.bfloat16)


def dense(tokens, expert_ids, route_weights, out_grad, gate_weight, up_weight, down_weight):
    experts = lax.axis_size("expert")
    devices = lax.axis_size("dp") * experts
    expert = lax.axis_index("expert").astype(jnp.int32).reshape(1)
    rows, width = tokens.shape
    ff = gate_weight.shape[1]
    near, far = split_masks(devices)
    weights = (gate_weight, up_weight, down_weight)
    shape = jax.ShapeDtypeStruct
    bf16, f32 = jnp.bfloat16, jnp.float32
    columns = 2 * width + experts + -experts % 128
    half = rows * devices // 2

    message = kernel_call(
        pack_body,
        shape((rows, columns), bf16),
        [],
        0,
        tokens,
        out_grad,
        expert_ids.T,
        route_weights.astype(f32).T,
    )
    block = jnp.concatenate([message] + [from_xor(message, m, devices) for m in near], axis=0)
    own = [block] + [from_xor(block, m, devices) for m in far]
    other = [from_xor(piece, 1, devices) for piece in own]
    count = len(own)

    held = pltpu.VMEM((half, columns), bf16)
    pre = kernel_call(
        functools.partial(pre_body, count, width),
        shape((half, 3 * ff), f32),
        [held],
        6 * half * ff * width,
        *own,
        *weights,
    )
    acts, message = kernel_call(
        functools.partial(act_body, count, width),
        (shape((2 * half, 3 * ff), bf16), shape((half, 2 * width), bf16)),
        [held],
        12 * half * ff * width,
        *own,
        *other,
        pre,
        *weights,
        expert,
    )
    passed = from_xor(message, 1, devices)
    mine = kernel_call(
        own_body, shape((half, 2 * width), f32), [], 6 * half * ff * width, acts, *weights
    )
    total = (mine + passed.astype(f32)).astype(bf16)
    for masks in (far, near):
        part = total.shape[0] // (len(masks) + 1)
        pieces = [total[k * part : (k + 1) * part] for k in range(len(masks) + 1)]
        summed = pieces[0].astype(f32)
        for m, piece in zip(masks, pieces[1:]):
            summed = summed + from_xor(piece, m, devices).astype(f32)
        total = summed.astype(bf16)

    grads = kernel_call(
        functools.partial(grad_body, 2 * count, width),
        (shape(gate_weight.shape, bf16),) * 3,
        [pltpu.VMEM((2 * half, columns), bf16)],
        12 * half * ff * width,
        *own,
        *other,
        acts,
    )
    return total[:, :width], total[:, width:], *grads


def shards(tokens, *others):
    experts = lax.axis_size("expert")
    devices = lax.axis_size("dp") * experts
    whole_group = tokens.shape[0] * experts <= ROW_CAP
    if whole_group and devices >= 16 and devices & (devices - 1) == 0:
        return dense(tokens, *others)
    return slotted(tokens, *others)


def solution(mesh):
    return jax.shard_map(
        shards,
        mesh=mesh,
        in_specs=(
            P(("dp", "expert"), None),
            P(("dp", "expert"), None),
            P(("dp", "expert"), None),
            P(("dp", "expert"), None),
            P("expert", "dp", None),
            P("expert", "dp", None),
            P("expert", "dp", None),
        ),
        out_specs=(
            P(("dp", "expert"), None),
            P(("dp", "expert"), None),
            P("expert", "dp", None),
            P("expert", "dp", None),
            P("expert", "dp", None),
        ),
        check_vma=False,
    )
```

```python
import functools

import jax
import jax.numpy as jnp
from jax import lax
from jax.experimental import pallas as pl
from jax.experimental.pallas import tpu as pltpu
from jax.sharding import PartitionSpec as P

ROW_CAP = 16
AXES = ("dp", "expert")


def contract_rows(left, right):
    return lax.dot_general(
        left, right, (((1,), (1,)), ((), ())), preferred_element_type=jnp.float32
    )


def contract_first(left, right):
    return lax.dot_general(
        left, right, (((0,), (0,)), ((), ())), preferred_element_type=jnp.float32
    )


def slotted(tokens, expert_ids, route_weights, out_grad, gate_weight, up_weight, down_weight):
    expert = lax.axis_index("expert")
    width = tokens.shape[1]
    local_tokens = tokens.shape[0]
    group_x, group_dy, group_w = (
        lax.all_gather(tokens, "expert", axis=0, tiled=True),
        lax.all_gather(out_grad, "expert", axis=0, tiled=True),
        lax.all_gather(route_weights, "expert", axis=0, tiled=True),
    )
    group_ids = lax.all_gather(expert_ids, "expert", axis=0, tiled=True)
    matches = group_ids == expert
    routed = jnp.any(matches, axis=1)
    weight = jnp.sum(jnp.where(matches, group_w.astype(jnp.float32), 0.0), axis=1)
    slot_rank = jnp.cumsum(routed.astype(jnp.int32)) - 1
    slot_index = jnp.arange(ROW_CAP, dtype=jnp.int32)
    picker = ((slot_rank[None, :] == slot_index[:, None]) & routed[None, :]).astype(jnp.bfloat16)
    slot_x = jnp.dot(picker, group_x, preferred_element_type=jnp.float32).astype(jnp.bfloat16)
    scaled = (weight[:, None] * group_dy.astype(jnp.float32)).astype(jnp.bfloat16)
    slot_dy = jnp.dot(picker, scaled, preferred_element_type=jnp.float32).astype(jnp.bfloat16)
    w_gate = gate_weight[0]
    w_up = up_weight[0]
    w_down = down_weight[0]
    all_x = lax.all_gather(slot_x, "dp", axis=0, tiled=True)
    gate_pre = contract_rows(w_gate, all_x)
    up_pre = contract_rows(w_up, all_x)
    gate_sig = jax.nn.sigmoid(gate_pre)
    silu_gate = gate_pre * gate_sig
    hidden = (silu_gate * up_pre).astype(jnp.bfloat16)
    expert_out = lax.psum_scatter(
        contract_first(hidden, w_down).astype(jnp.bfloat16), "dp", scatter_dimension=0, tiled=True
    )
    all_dy = lax.all_gather(slot_dy, "dp", axis=0, tiled=True)
    hidden_grad = contract_rows(w_down, all_dy)
    silu_slope = gate_sig * (1.0 + gate_pre * (1.0 - gate_sig))
    gate_act = (hidden_grad * up_pre * silu_slope).astype(jnp.bfloat16)
    up_act = (hidden_grad * silu_gate).astype(jnp.bfloat16)
    grad_down = jnp.dot(hidden, all_dy, preferred_element_type=jnp.float32).astype(jnp.bfloat16)
    grad_gate = jnp.dot(gate_act, all_x, preferred_element_type=jnp.float32).astype(jnp.bfloat16)
    grad_up = jnp.dot(up_act, all_x, preferred_element_type=jnp.float32).astype(jnp.bfloat16)
    expert_in = lax.psum_scatter(
        (contract_first(gate_act, w_gate) + contract_first(up_act, w_up)).astype(jnp.bfloat16),
        "dp",
        scatter_dimension=0,
        tiled=True,
    )
    back_out = contract_first(picker, expert_out).astype(jnp.bfloat16)
    back_in = contract_first(picker, expert_in).astype(jnp.bfloat16)
    got_out, got_in = (
        lax.all_to_all(back_out, "expert", split_axis=0, concat_axis=0, tiled=True),
        lax.all_to_all(back_in, "expert", split_axis=0, concat_axis=0, tiled=True),
    )
    expert_count = lax.axis_size("expert")
    got_out = got_out.reshape(expert_count, local_tokens, width)
    got_in = got_in.reshape(expert_count, local_tokens, width)
    expert_range = jnp.arange(expert_count, dtype=jnp.int32)
    own_match = expert_ids[:, :, None] == expert_range[None, None, :]
    mix_weight = jnp.sum(
        jnp.where(own_match, route_weights.astype(jnp.float32)[:, :, None], 0.0), axis=1
    )
    mixed_out = jnp.sum(jnp.transpose(mix_weight)[:, :, None] * got_out.astype(jnp.float32), axis=0)
    input_total = jnp.sum(got_in.astype(jnp.float32), axis=0)
    return (
        mixed_out.astype(jnp.bfloat16),
        input_total.astype(jnp.bfloat16),
        grad_gate[None],
        grad_up[None],
        grad_down[None],
    )


def split_masks(devices):
    far = tuple(k << 1 for k in range(1, 4))
    near = tuple(k << 3 for k in range(1, devices >> 3))
    return near, far


def from_xor(value, mask, devices):
    return lax.ppermute(value, AXES, [(i, i ^ mask) for i in range(devices)])


def kernel_call(body, out_shape, cost, *operands, scratch=(), hbm=(), vmem_mib=24):
    vmem, smem = pl.BlockSpec(memory_space=pltpu.VMEM), pl.BlockSpec(memory_space=pltpu.SMEM)
    stay = pl.BlockSpec(memory_space=pltpu.HBM)
    specs = [stay if i in hbm else smem if o.ndim == 1 else vmem for i, o in enumerate(operands)]
    return pl.pallas_call(
        body,
        out_shape=out_shape,
        in_specs=specs,
        out_specs=jax.tree.map(lambda _: vmem, out_shape),
        scratch_shapes=scratch,
        compiler_params=pltpu.CompilerParams(vmem_limit_bytes=vmem_mib << 20),
        cost_estimate=pl.CostEstimate(flops=cost, bytes_accessed=4 << 20, transcendentals=0),
    )(*operands)


def load_body(*refs):
    count = len(refs) // 2
    sems = refs[-1]
    copies = [
        pltpu.make_async_copy(refs[i], refs[count + i], sems.at[i]) for i in range(count)
    ]
    for copy in copies:
        copy.start()
    for copy in copies:
        copy.wait()


def pack_body(dy_ref, ids_ref, w_ref, msg_ref):
    rows, width = dy_ref.shape
    top = ids_ref.shape[0]
    lanes = msg_ref.shape[1] - width
    msg_ref[:, :width] = dy_ref[...]
    diagonal = lax.broadcasted_iota(jnp.int32, (rows, rows), 0) == lax.broadcasted_iota(
        jnp.int32, (rows, rows), 1
    )
    expert = lax.broadcasted_iota(jnp.int32, (rows, lanes), 1)
    route = jnp.zeros((rows, lanes), jnp.float32)
    for k in range(top):
        named = jnp.sum(jnp.where(diagonal, ids_ref[k : k + 1, :], 0), axis=1, keepdims=True)
        weight = jnp.sum(jnp.where(diagonal, w_ref[k : k + 1, :], 0.0), axis=1, keepdims=True)
        route = route + jnp.where(expert == named, weight, 0.0)
    msg_ref[:, width:] = route.astype(jnp.bfloat16)


def gathered(pieces, into):
    rows = pieces[0].shape[0]
    for i, piece in enumerate(pieces):
        into[i * rows : (i + 1) * rows, :] = piece[...]


def forward_body(count, *refs):
    pieces, (wg_ref, wu_ref, x_ref, hidden_ref, gate_ref, up_ref) = refs[:count], refs[count:]
    gathered(pieces, x_ref)
    x = x_ref[...]
    gate_pre = contract_rows(x, wg_ref[0])
    up_pre = contract_rows(x, wu_ref[0])
    gate_sig = 1.0 / (1.0 + jnp.exp(-gate_pre))
    silu_gate = gate_pre * gate_sig
    hidden_ref[...] = silu_gate * up_pre
    gate_ref[...] = up_pre * (gate_sig * (1.0 + gate_pre * (1.0 - gate_sig)))
    up_ref[...] = silu_gate


def back_body(count, *refs):
    pieces, (wd_ref, dy_ref, grad_ref) = refs[:count], refs[count:]
    gathered(pieces, dy_ref)
    grad_ref[...] = contract_rows(dy_ref[:, : wd_ref.shape[2]], wd_ref[0])


def out_body(count, *refs):
    pieces, rest = refs[:count], refs[count:]
    own_ref, hidden_ref, wd_ref, expert_ref, dy_ref, weight_ref, scaled_ref, msg_ref = rest
    gathered(pieces, dy_ref)
    half, width = msg_ref.shape
    lane = lax.broadcasted_iota(jnp.int32, (half, dy_ref.shape[1] - width), 1)
    for i, ref in enumerate((own_ref, dy_ref)):
        route = jnp.where(lane == expert_ref[0], ref[:, width:].astype(jnp.float32), 0.0)
        weight = jnp.sum(route, axis=1, keepdims=True)
        here = slice(i * half, (i + 1) * half)
        weight_ref[here, :] = jnp.broadcast_to(weight, (half, weight_ref.shape[1]))
        scaled_ref[here, :] = (weight * hidden_ref[here, :]).astype(jnp.bfloat16)
    msg_ref[...] = jnp.dot(
        scaled_ref[half:, :], wd_ref[0], preferred_element_type=jnp.float32
    ).astype(jnp.bfloat16)


def into_sum(gate_act, up_act, wg_ref, wu_ref):
    return jnp.dot(gate_act, wg_ref[0], preferred_element_type=jnp.float32) + jnp.dot(
        up_act, wu_ref[0], preferred_element_type=jnp.float32
    )


def into_body(dy_ref, own_ref, weight_ref, gate_ref, up_ref, wg_ref, wu_ref, wd_ref, *outs):
    gate_act_ref, up_act_ref, msg_ref = outs
    half, width = msg_ref.shape
    other = contract_rows(dy_ref[:, :width], wd_ref[0])
    for i, grad in enumerate((own_ref[...], other)):
        here = slice(i * half, (i + 1) * half)
        grad = weight_ref[here, :1] * grad
        gate_act_ref[here, :] = (grad * gate_ref[here, :]).astype(jnp.bfloat16)
        up_act_ref[here, :] = (grad * up_ref[here, :]).astype(jnp.bfloat16)
    msg_ref[...] = into_sum(gate_act_ref[half:, :], up_act_ref[half:, :], wg_ref, wu_ref).astype(
        jnp.bfloat16
    )


def scattered(total, outs):
    rows = outs[0].shape[0]
    for i, ref in enumerate(outs):
        ref[...] = total[i * rows : (i + 1) * rows, :].astype(ref.dtype)


def own_out_body(scaled_ref, wd_ref, passed_ref, *outs):
    half = passed_ref.shape[0]
    total = jnp.dot(scaled_ref[:half, :], wd_ref[0], preferred_element_type=jnp.float32)
    scattered(total + passed_ref[...].astype(jnp.float32), outs)


def own_into_body(gate_act_ref, up_act_ref, wg_ref, wu_ref, passed_ref, *outs):
    half = passed_ref.shape[0]
    total = into_sum(gate_act_ref[:half, :], up_act_ref[:half, :], wg_ref, wu_ref)
    scattered(total + passed_ref[...].astype(jnp.float32), outs)


def pair_grad_body(gate_act_ref, up_act_ref, x_ref, gg_ref, gu_ref):
    gg_ref[0] = contract_first(gate_act_ref[...], x_ref[...]).astype(jnp.bfloat16)
    gu_ref[0] = contract_first(up_act_ref[...], x_ref[...]).astype(jnp.bfloat16)


def down_grad_body(scaled_ref, own_ref, other_ref, gd_ref):
    half, width = own_ref.shape[0], gd_ref.shape[2]
    gd_ref[0] = (
        contract_first(scaled_ref[:half, :], own_ref[:, :width])
        + contract_first(scaled_ref[half:, :], other_ref[:, :width])
    ).astype(jnp.bfloat16)


def dense(tokens, expert_ids, route_weights, out_grad, gate_weight, up_weight, down_weight):
    experts = lax.axis_size("expert")
    devices = lax.axis_size("dp") * experts
    expert = lax.axis_index("expert").astype(jnp.int32).reshape(1)
    rows, width = tokens.shape
    ff = gate_weight.shape[1]
    near, far = split_masks(devices)
    bf16, f32 = jnp.bfloat16, jnp.float32
    lanes = experts + -experts % 128
    half = rows * devices // 2
    unit = 2 * half * ff * width

    def shape(*dims, dtype=bf16):
        return jax.ShapeDtypeStruct(dims, dtype)

    def near_block(value):
        return jnp.concatenate([value] + [from_xor(value, m, devices) for m in near], axis=0)

    def far_pieces(block):
        own = [block] + [from_xor(block, m, devices) for m in far]
        return own, [from_xor(piece, 1, devices) for piece in own]

    block_x = near_block(tokens)
    message = kernel_call(
        pack_body,
        shape(rows, width + lanes),
        0,
        out_grad,
        expert_ids.T,
        route_weights.astype(f32).T,
    )
    w_gate, w_up, w_down = kernel_call(
        load_body,
        (shape(*gate_weight.shape),) * 3,
        0,
        gate_weight,
        up_weight,
        down_weight,
        scratch=[pltpu.SemaphoreType.DMA((3,))],
        hbm=(0, 1, 2),
        vmem_mib=8,
    )
    block_x, w_gate, w_up, w_down = lax.optimization_barrier((block_x, w_gate, w_up, w_down))
    own_x, other_x = far_pieces(block_x)
    own_dy, other_dy = far_pieces(near_block(message))
    count = len(own_x)

    all_x, hidden, gate_part, up_part = kernel_call(
        functools.partial(forward_body, 2 * count),
        (shape(2 * half, width),) + (shape(2 * half, ff, dtype=f32),) * 3,
        4 * unit,
        *own_x,
        *other_x,
        w_gate,
        w_up,
    )
    dy_own, grad_own = kernel_call(
        functools.partial(back_body, count),
        (shape(half, width + lanes), shape(half, ff, dtype=f32)),
        unit,
        *own_dy,
        w_down,
    )
    dy_other, weight, scaled, message = kernel_call(
        functools.partial(out_body, count),
        (
            shape(half, width + lanes),
            shape(2 * half, lanes, dtype=f32),
            shape(2 * half, ff),
            shape(half, width),
        ),
        unit,
        *other_dy,
        dy_own,
        hidden,
        w_down,
        expert,
    )
    passed_out = from_xor(message, 1, devices)
    gate_act, up_act, message = kernel_call(
        into_body,
        (shape(2 * half, ff), shape(2 * half, ff), shape(half, width)),
        3 * unit,
        dy_other,
        grad_own,
        weight,
        gate_part,
        up_part,
        w_gate,
        w_up,
        w_down,
    )
    passed_into = from_xor(message, 1, devices)

    quarter = half // count
    piece_shapes = (shape(quarter, width, dtype=f32),) + (shape(quarter, width),) * (count - 1)
    out_pieces = kernel_call(own_out_body, piece_shapes, unit, scaled, w_down, passed_out)
    into_pieces = kernel_call(
        own_into_body, piece_shapes, 2 * unit, gate_act, up_act, w_gate, w_up, passed_into
    )

    def reduced(pieces):
        total = pieces[0]
        for m, piece in zip(far, pieces[1:]):
            total = total + from_xor(piece, m, devices).astype(f32)
        total = total.astype(bf16)
        pieces = [total[k * rows : (k + 1) * rows] for k in range(len(near) + 1)]
        total = pieces[0].astype(f32)
        for m, piece in zip(near, pieces[1:]):
            total = total + from_xor(piece, m, devices).astype(f32)
        return total.astype(bf16)

    mixed, input_grad = reduced(out_pieces), reduced(into_pieces)
    grad_down = kernel_call(
        down_grad_body, shape(*down_weight.shape), 2 * unit, scaled, dy_own, dy_other
    )
    grad_gate, grad_up = kernel_call(
        pair_grad_body, (shape(*gate_weight.shape),) * 2, 4 * unit, gate_act, up_act, all_x
    )
    return mixed, input_grad, grad_gate, grad_up, grad_down


def shards(tokens, *others):
    experts = lax.axis_size("expert")
    devices = lax.axis_size("dp") * experts
    whole_group = tokens.shape[0] * experts <= ROW_CAP
    if whole_group and devices >= 16 and devices & (devices - 1) == 0:
        return dense(tokens, *others)
    return slotted(tokens, *others)


def solution(mesh):
    return jax.shard_map(
        shards,
        mesh=mesh,
        in_specs=(
            P(("dp", "expert"), None),
            P(("dp", "expert"), None),
            P(("dp", "expert"), None),
            P(("dp", "expert"), None),
            P("expert", "dp", None),
            P("expert", "dp", None),
            P("expert", "dp", None),
        ),
        out_specs=(
            P(("dp", "expert"), None),
            P(("dp", "expert"), None),
            P("expert", "dp", None),
            P("expert", "dp", None),
            P("expert", "dp", None),
        ),
        check_vma=False,
    )
```

```python
import functools

import jax
import jax.numpy as jnp
from jax import lax
from jax.experimental import pallas as pl
from jax.experimental.pallas import tpu as pltpu
from jax.sharding import PartitionSpec as P

ROW_CAP = 16
AXES = ("dp", "expert")


def contract_rows(left, right):
    return lax.dot_general(
        left, right, (((1,), (1,)), ((), ())), preferred_element_type=jnp.float32
    )


def contract_first(left, right):
    return lax.dot_general(
        left, right, (((0,), (0,)), ((), ())), preferred_element_type=jnp.float32
    )


def slotted(tokens, expert_ids, route_weights, out_grad, gate_weight, up_weight, down_weight):
    expert = lax.axis_index("expert")
    width = tokens.shape[1]
    local_tokens = tokens.shape[0]
    group_x, group_dy, group_w = (
        lax.all_gather(tokens, "expert", axis=0, tiled=True),
        lax.all_gather(out_grad, "expert", axis=0, tiled=True),
        lax.all_gather(route_weights, "expert", axis=0, tiled=True),
    )
    group_ids = lax.all_gather(expert_ids, "expert", axis=0, tiled=True)
    matches = group_ids == expert
    routed = jnp.any(matches, axis=1)
    weight = jnp.sum(jnp.where(matches, group_w.astype(jnp.float32), 0.0), axis=1)
    slot_rank = jnp.cumsum(routed.astype(jnp.int32)) - 1
    slot_index = jnp.arange(ROW_CAP, dtype=jnp.int32)
    picker = ((slot_rank[None, :] == slot_index[:, None]) & routed[None, :]).astype(jnp.bfloat16)
    slot_x = jnp.dot(picker, group_x, preferred_element_type=jnp.float32).astype(jnp.bfloat16)
    scaled = (weight[:, None] * group_dy.astype(jnp.float32)).astype(jnp.bfloat16)
    slot_dy = jnp.dot(picker, scaled, preferred_element_type=jnp.float32).astype(jnp.bfloat16)
    w_gate = gate_weight[0]
    w_up = up_weight[0]
    w_down = down_weight[0]
    all_x = lax.all_gather(slot_x, "dp", axis=0, tiled=True)
    gate_pre = contract_rows(w_gate, all_x)
    up_pre = contract_rows(w_up, all_x)
    gate_sig = jax.nn.sigmoid(gate_pre)
    silu_gate = gate_pre * gate_sig
    hidden = (silu_gate * up_pre).astype(jnp.bfloat16)
    expert_out = lax.psum_scatter(
        contract_first(hidden, w_down).astype(jnp.bfloat16), "dp", scatter_dimension=0, tiled=True
    )
    all_dy = lax.all_gather(slot_dy, "dp", axis=0, tiled=True)
    hidden_grad = contract_rows(w_down, all_dy)
    silu_slope = gate_sig * (1.0 + gate_pre * (1.0 - gate_sig))
    gate_act = (hidden_grad * up_pre * silu_slope).astype(jnp.bfloat16)
    up_act = (hidden_grad * silu_gate).astype(jnp.bfloat16)
    grad_down = jnp.dot(hidden, all_dy, preferred_element_type=jnp.float32).astype(jnp.bfloat16)
    grad_gate = jnp.dot(gate_act, all_x, preferred_element_type=jnp.float32).astype(jnp.bfloat16)
    grad_up = jnp.dot(up_act, all_x, preferred_element_type=jnp.float32).astype(jnp.bfloat16)
    expert_in = lax.psum_scatter(
        (contract_first(gate_act, w_gate) + contract_first(up_act, w_up)).astype(jnp.bfloat16),
        "dp",
        scatter_dimension=0,
        tiled=True,
    )
    back_out = contract_first(picker, expert_out).astype(jnp.bfloat16)
    back_in = contract_first(picker, expert_in).astype(jnp.bfloat16)
    got_out, got_in = (
        lax.all_to_all(back_out, "expert", split_axis=0, concat_axis=0, tiled=True),
        lax.all_to_all(back_in, "expert", split_axis=0, concat_axis=0, tiled=True),
    )
    expert_count = lax.axis_size("expert")
    got_out = got_out.reshape(expert_count, local_tokens, width)
    got_in = got_in.reshape(expert_count, local_tokens, width)
    expert_range = jnp.arange(expert_count, dtype=jnp.int32)
    own_match = expert_ids[:, :, None] == expert_range[None, None, :]
    mix_weight = jnp.sum(
        jnp.where(own_match, route_weights.astype(jnp.float32)[:, :, None], 0.0), axis=1
    )
    mixed_out = jnp.sum(jnp.transpose(mix_weight)[:, :, None] * got_out.astype(jnp.float32), axis=0)
    input_total = jnp.sum(got_in.astype(jnp.float32), axis=0)
    return (
        mixed_out.astype(jnp.bfloat16),
        input_total.astype(jnp.bfloat16),
        grad_gate[None],
        grad_up[None],
        grad_down[None],
    )


CORE, FIRST, SECOND = 1, 2, 4


def from_xor(value, mask, devices):
    return lax.ppermute(value, AXES, [(i, i ^ mask) for i in range(devices)])


def kernel_call(body, out_shape, cost, *operands, scratch=(), hbm=()):
    vmem, smem = pl.BlockSpec(memory_space=pltpu.VMEM), pl.BlockSpec(memory_space=pltpu.SMEM)
    stay = pl.BlockSpec(memory_space=pltpu.HBM)
    specs = [stay if i in hbm else smem if o.ndim == 1 else vmem for i, o in enumerate(operands)]
    operands = [
        pltpu.with_memory_space_constraint(o, pltpu.HBM) if i in hbm else o
        for i, o in enumerate(operands)
    ]
    return pl.pallas_call(
        body,
        out_shape=out_shape,
        in_specs=specs,
        out_specs=jax.tree.map(lambda _: vmem, out_shape),
        scratch_shapes=scratch,
        compiler_params=pltpu.CompilerParams(vmem_limit_bytes=24 << 20),
        cost_estimate=pl.CostEstimate(flops=cost, bytes_accessed=4 << 20, transcendentals=0),
    )(*operands)


def copy_all(pairs, sems):
    copies = [pltpu.make_async_copy(src, dst, sems.at[i]) for i, (src, dst) in enumerate(pairs)]
    for copy in copies:
        copy.start()
    for copy in copies:
        copy.wait()


def load_body(*refs):
    count = len(refs) // 2
    copy_all(list(zip(refs[:count], refs[count:-1])), refs[-1])


def pack_body(x_ref, dy_ref, ids_ref, w_ref, msg_ref, x_buf, dy_buf, sems):
    rows, width = x_ref.shape
    top = ids_ref.shape[0]
    lanes = msg_ref.shape[1] - 2 * width
    copy_all([(x_ref, x_buf), (dy_ref, dy_buf)], sems)
    msg_ref[:, :width] = x_buf[...]
    msg_ref[:, width : 2 * width] = dy_buf[...]
    diagonal = lax.broadcasted_iota(jnp.int32, (rows, rows), 0) == lax.broadcasted_iota(
        jnp.int32, (rows, rows), 1
    )
    expert = lax.broadcasted_iota(jnp.int32, (rows, lanes), 1)
    route = jnp.zeros((rows, lanes), jnp.float32)
    for k in range(top):
        named = jnp.sum(jnp.where(diagonal, ids_ref[k : k + 1, :], 0), axis=1, keepdims=True)
        weight = jnp.sum(jnp.where(diagonal, w_ref[k : k + 1, :], 0.0), axis=1, keepdims=True)
        route = route + jnp.where(expert == named, weight, 0.0)
    msg_ref[:, 2 * width :] = route.astype(jnp.bfloat16)


def passes(have, wg_ref, wu_ref, wd_ref, expert_ref, acts_ref):
    width, ff = wg_ref.shape[2], wg_ref.shape[1]
    x, dy, route = have[:, :width], have[:, width : 2 * width], have[:, 2 * width :]
    lanes = route.shape[1]
    mine = lax.broadcasted_iota(jnp.int32, (8, lanes), 1) == expert_ref[0]
    weight = contract_rows(mine.astype(jnp.float32).astype(jnp.bfloat16), route)[:1, :]
    gate_pre = contract_rows(wg_ref[0], x)
    up_pre = contract_rows(wu_ref[0], x)
    hidden_grad = weight * contract_rows(wd_ref[0], dy)
    gate_sig = 1.0 / (1.0 + jnp.exp(-gate_pre))
    silu_gate = gate_pre * gate_sig
    silu_slope = gate_sig * (1.0 + gate_pre * (1.0 - gate_sig))
    acts_ref[:ff, :] = (hidden_grad * up_pre * silu_slope).astype(jnp.bfloat16)
    acts_ref[ff : 2 * ff, :] = (hidden_grad * silu_gate).astype(jnp.bfloat16)
    acts_ref[2 * ff :, :] = (weight * (silu_gate * up_pre)).astype(jnp.bfloat16)
    out = contract_first(acts_ref[2 * ff :, :], wd_ref[0])
    into = contract_first(acts_ref[:ff, :], wg_ref[0]) + contract_first(
        acts_ref[ff : 2 * ff, :], wu_ref[0]
    )
    return out, into


def give(out, into, own_ref, msg_ref):
    half, width = own_ref.shape[0], out.shape[1]
    for i, value in enumerate((out, into)):
        own_ref[:, i * width : (i + 1) * width] = value[:half, :]
        msg_ref[:, i * width : (i + 1) * width] = value[half:, :].astype(jnp.bfloat16)


def early_body(count, *refs):
    pieces, rest = refs[:count], refs[count:]
    wg_ref, wu_ref, wd_ref, expert_ref, have, acts_ref, own_ref, msg_ref = rest
    rows = pieces[0].shape[0]
    for i, piece in enumerate(pieces):
        have[i * rows : (i + 1) * rows, :] = piece[...]
    out, into = passes(have, wg_ref, wu_ref, wd_ref, expert_ref, acts_ref)
    give(out, into, own_ref, msg_ref)


def late_body(*refs):
    pieces, rest = refs[:4], refs[4:]
    wg_ref, wu_ref, wd_ref, expert_ref, have, acts_ref, own_ref, msg_ref = rest
    rows, width = pieces[0].shape
    for i in range(2):
        have[i * rows : (i + 1) * rows, :width] = pieces[2 * i][...]
        have[i * rows : (i + 1) * rows, width:] = pieces[2 * i + 1][...]
    out, into = passes(have, wg_ref, wu_ref, wd_ref, expert_ref, acts_ref)
    give(out, into, own_ref, msg_ref)


def late_sum_body(own_ref, passed_ref, out_ref, into_ref):
    width = out_ref.shape[1]
    total = own_ref[...] + passed_ref[...].astype(jnp.float32)
    out_ref[...] = total[:, :width].astype(jnp.bfloat16)
    into_ref[...] = total[:, width:].astype(jnp.bfloat16)


def early_sum_body(own_ref, passed_ref, into_ref, out_ref, here_ref, first_ref, second_ref):
    rows, width = into_ref.shape

    def total(i, side):
        at = (slice(i * rows, (i + 1) * rows), slice(side * width, (side + 1) * width))
        return own_ref[at] + passed_ref[at].astype(jnp.float32)

    here_ref[:, :width], here_ref[:, width:] = total(0, 0), total(0, 1)
    second_ref[:, :width] = total(1, 0).astype(jnp.bfloat16)
    second_ref[:, width:] = (total(1, 1) + into_ref[...].astype(jnp.float32)).astype(jnp.bfloat16)
    first_ref[:, :width] = (total(2, 0) + out_ref[...].astype(jnp.float32)).astype(jnp.bfloat16)
    first_ref[:, width:] = total(2, 1).astype(jnp.bfloat16)


def grad_body(early_ref, late_ref, early_acts_ref, late_acts_ref, *grads):
    width = grads[0].shape[2]
    ff = grads[0].shape[1]
    for i, ref in enumerate(grads):
        first = early_acts_ref.shape[0] // ff - len(grads) if len(grads) == 1 else 0
        here = slice((first + i) * ff, (first + i + 1) * ff)
        side = slice(width, 2 * width) if len(grads) == 1 else slice(0, width)
        ref[0] = (
            jnp.dot(early_acts_ref[here, :], early_ref[:, side], preferred_element_type=jnp.float32)
            + jnp.dot(late_acts_ref[here, :], late_ref[:, side], preferred_element_type=jnp.float32)
        ).astype(jnp.bfloat16)


def dense(tokens, expert_ids, route_weights, out_grad, gate_weight, up_weight, down_weight):
    experts = lax.axis_size("expert")
    devices = lax.axis_size("dp") * experts
    expert = lax.axis_index("expert").astype(jnp.int32).reshape(1)
    rows, width = tokens.shape
    ff = gate_weight.shape[1]
    near = tuple(k << 3 for k in range(1, devices >> 3))
    block_rows = rows * (len(near) + 1)
    bf16, f32 = jnp.bfloat16, jnp.float32
    columns = 2 * width + experts + -experts % 128
    unit = 2 * block_rows * ff * width

    def shape(*dims, dtype=bf16):
        return jax.ShapeDtypeStruct(dims, dtype)

    def passed(value, mask):
        return from_xor(value, mask, devices)

    message = kernel_call(
        pack_body,
        shape(rows, columns),
        0,
        tokens,
        out_grad,
        expert_ids.T,
        route_weights.astype(f32).T,
        scratch=[
            pltpu.VMEM((rows, width), bf16),
            pltpu.VMEM((rows, width), bf16),
            pltpu.SemaphoreType.DMA((2,)),
        ],
        hbm=(0, 1),
    )
    weights = kernel_call(
        load_body,
        (shape(*gate_weight.shape),) * 3,
        0,
        gate_weight,
        up_weight,
        down_weight,
        scratch=[pltpu.SemaphoreType.DMA((3,))],
        hbm=(0, 1, 2),
    )
    block = jnp.concatenate([message] + [passed(message, m) for m in near], axis=0)
    block, *weights = lax.optimization_barrier((block, *weights))

    by_second, by_first = passed(block, SECOND), passed(block, FIRST)
    corner_x = passed(by_second[:, :width], FIRST)
    corner_dy = passed(by_first[:, width:], SECOND)
    own = [block, by_second, by_first]
    other = [passed(piece, CORE) for piece in own]
    corner = [corner_x, corner_dy, passed(corner_x, CORE), passed(corner_dy, CORE)]

    early_rows = len(own) * block_rows
    early, early_acts, early_own, message = kernel_call(
        functools.partial(early_body, 2 * len(own)),
        (
            shape(2 * early_rows, columns),
            shape(3 * ff, 2 * early_rows),
            shape(early_rows, 2 * width, dtype=f32),
            shape(early_rows, 2 * width),
        ),
        36 * unit,
        *own,
        *other,
        *weights,
        expert,
    )
    early_passed = passed(message, CORE)
    late, late_acts, late_own, message = kernel_call(
        late_body,
        (
            shape(2 * block_rows, columns),
            shape(3 * ff, 2 * block_rows),
            shape(block_rows, 2 * width, dtype=f32),
            shape(block_rows, 2 * width),
        ),
        12 * unit,
        *corner,
        *weights,
        expert,
    )
    late_passed = passed(message, CORE)

    corner_out, corner_into = kernel_call(
        late_sum_body, (shape(block_rows, width),) * 2, 0, late_own, late_passed
    )
    turned_out, turned_into = passed(corner_out, SECOND), passed(corner_into, FIRST)
    here, for_first, for_second = kernel_call(
        early_sum_body,
        (
            shape(block_rows, 2 * width, dtype=f32),
            shape(block_rows, 2 * width),
            shape(block_rows, 2 * width),
        ),
        0,
        early_own,
        early_passed,
        turned_into,
        turned_out,
    )
    total = here + passed(for_second, SECOND).astype(f32) + passed(for_first, FIRST).astype(f32)
    total = total.astype(bf16)
    pieces = [total[k * rows : (k + 1) * rows] for k in range(len(near) + 1)]
    total = pieces[0].astype(f32)
    for m, piece in zip(near, pieces[1:]):
        total = total + passed(piece, m).astype(f32)
    total = total.astype(bf16)

    (grad_down,) = kernel_call(
        grad_body, (shape(*down_weight.shape),), 8 * unit, early, late, early_acts, late_acts
    )
    grad_gate, grad_up = kernel_call(
        grad_body, (shape(*gate_weight.shape),) * 2, 16 * unit, early, late, early_acts, late_acts
    )
    return total[:, :width], total[:, width:], grad_gate, grad_up, grad_down


def shards(tokens, *others):
    experts = lax.axis_size("expert")
    devices = lax.axis_size("dp") * experts
    whole_group = tokens.shape[0] * experts <= ROW_CAP
    if whole_group and devices >= 16 and devices & (devices - 1) == 0:
        return dense(tokens, *others)
    return slotted(tokens, *others)


def solution(mesh):
    return jax.shard_map(
        shards,
        mesh=mesh,
        in_specs=(
            P(("dp", "expert"), None),
            P(("dp", "expert"), None),
            P(("dp", "expert"), None),
            P(("dp", "expert"), None),
            P("expert", "dp", None),
            P("expert", "dp", None),
            P("expert", "dp", None),
        ),
        out_specs=(
            P(("dp", "expert"), None),
            P(("dp", "expert"), None),
            P("expert", "dp", None),
            P("expert", "dp", None),
            P("expert", "dp", None),
        ),
        check_vma=False,
    )
```

```python
import functools

import jax
import jax.numpy as jnp
from jax import lax
from jax.experimental import pallas as pl
from jax.experimental.pallas import tpu as pltpu
from jax.sharding import PartitionSpec as P

ROW_CAP = 16
AXES = ("dp", "expert")


def contract_rows(left, right):
    return lax.dot_general(
        left, right, (((1,), (1,)), ((), ())), preferred_element_type=jnp.float32
    )


def contract_first(left, right):
    return lax.dot_general(
        left, right, (((0,), (0,)), ((), ())), preferred_element_type=jnp.float32
    )


def slotted(tokens, expert_ids, route_weights, out_grad, gate_weight, up_weight, down_weight):
    expert = lax.axis_index("expert")
    width = tokens.shape[1]
    local_tokens = tokens.shape[0]
    group_x, group_dy, group_w = (
        lax.all_gather(tokens, "expert", axis=0, tiled=True),
        lax.all_gather(out_grad, "expert", axis=0, tiled=True),
        lax.all_gather(route_weights, "expert", axis=0, tiled=True),
    )
    group_ids = lax.all_gather(expert_ids, "expert", axis=0, tiled=True)
    matches = group_ids == expert
    routed = jnp.any(matches, axis=1)
    weight = jnp.sum(jnp.where(matches, group_w.astype(jnp.float32), 0.0), axis=1)
    slot_rank = jnp.cumsum(routed.astype(jnp.int32)) - 1
    slot_index = jnp.arange(ROW_CAP, dtype=jnp.int32)
    picker = ((slot_rank[None, :] == slot_index[:, None]) & routed[None, :]).astype(jnp.bfloat16)
    slot_x = jnp.dot(picker, group_x, preferred_element_type=jnp.float32).astype(jnp.bfloat16)
    scaled = (weight[:, None] * group_dy.astype(jnp.float32)).astype(jnp.bfloat16)
    slot_dy = jnp.dot(picker, scaled, preferred_element_type=jnp.float32).astype(jnp.bfloat16)
    w_gate = gate_weight[0]
    w_up = up_weight[0]
    w_down = down_weight[0]
    all_x = lax.all_gather(slot_x, "dp", axis=0, tiled=True)
    gate_pre = contract_rows(w_gate, all_x)
    up_pre = contract_rows(w_up, all_x)
    gate_sig = jax.nn.sigmoid(gate_pre)
    silu_gate = gate_pre * gate_sig
    hidden = (silu_gate * up_pre).astype(jnp.bfloat16)
    expert_out = lax.psum_scatter(
        contract_first(hidden, w_down).astype(jnp.bfloat16), "dp", scatter_dimension=0, tiled=True
    )
    all_dy = lax.all_gather(slot_dy, "dp", axis=0, tiled=True)
    hidden_grad = contract_rows(w_down, all_dy)
    silu_slope = gate_sig * (1.0 + gate_pre * (1.0 - gate_sig))
    gate_act = (hidden_grad * up_pre * silu_slope).astype(jnp.bfloat16)
    up_act = (hidden_grad * silu_gate).astype(jnp.bfloat16)
    grad_down = jnp.dot(hidden, all_dy, preferred_element_type=jnp.float32).astype(jnp.bfloat16)
    grad_gate = jnp.dot(gate_act, all_x, preferred_element_type=jnp.float32).astype(jnp.bfloat16)
    grad_up = jnp.dot(up_act, all_x, preferred_element_type=jnp.float32).astype(jnp.bfloat16)
    expert_in = lax.psum_scatter(
        (contract_first(gate_act, w_gate) + contract_first(up_act, w_up)).astype(jnp.bfloat16),
        "dp",
        scatter_dimension=0,
        tiled=True,
    )
    back_out = contract_first(picker, expert_out).astype(jnp.bfloat16)
    back_in = contract_first(picker, expert_in).astype(jnp.bfloat16)
    got_out, got_in = (
        lax.all_to_all(back_out, "expert", split_axis=0, concat_axis=0, tiled=True),
        lax.all_to_all(back_in, "expert", split_axis=0, concat_axis=0, tiled=True),
    )
    expert_count = lax.axis_size("expert")
    got_out = got_out.reshape(expert_count, local_tokens, width)
    got_in = got_in.reshape(expert_count, local_tokens, width)
    expert_range = jnp.arange(expert_count, dtype=jnp.int32)
    own_match = expert_ids[:, :, None] == expert_range[None, None, :]
    mix_weight = jnp.sum(
        jnp.where(own_match, route_weights.astype(jnp.float32)[:, :, None], 0.0), axis=1
    )
    mixed_out = jnp.sum(jnp.transpose(mix_weight)[:, :, None] * got_out.astype(jnp.float32), axis=0)
    input_total = jnp.sum(got_in.astype(jnp.float32), axis=0)
    return (
        mixed_out.astype(jnp.bfloat16),
        input_total.astype(jnp.bfloat16),
        grad_gate[None],
        grad_up[None],
        grad_down[None],
    )


CORE, FIRST, SECOND = 1, 2, 4


def from_xor(value, mask, devices):
    return lax.ppermute(value, AXES, [(i, i ^ mask) for i in range(devices)])


def kernel_call(body, out_shape, cost, *operands, scratch=(), hbm=()):
    vmem, smem = pl.BlockSpec(memory_space=pltpu.VMEM), pl.BlockSpec(memory_space=pltpu.SMEM)
    stay = pl.BlockSpec(memory_space=pltpu.HBM)
    specs = [stay if i in hbm else smem if o.ndim == 1 else vmem for i, o in enumerate(operands)]
    operands = [
        pltpu.with_memory_space_constraint(o, pltpu.HBM) if i in hbm else o
        for i, o in enumerate(operands)
    ]
    return pl.pallas_call(
        body,
        out_shape=out_shape,
        in_specs=specs,
        out_specs=jax.tree.map(lambda _: vmem, out_shape),
        scratch_shapes=scratch,
        compiler_params=pltpu.CompilerParams(vmem_limit_bytes=16 << 20),
        cost_estimate=pl.CostEstimate(flops=cost, bytes_accessed=4 << 20, transcendentals=0),
    )(*operands)


def copy_all(pairs, sems):
    copies = [pltpu.make_async_copy(src, dst, sems.at[i]) for i, (src, dst) in enumerate(pairs)]
    for copy in copies:
        copy.start()
    for copy in copies:
        copy.wait()


def load_body(*refs):
    count = len(refs) // 2
    copy_all(list(zip(refs[:count], refs[count:-1])), refs[-1])


def pack_body(x_ref, dy_ref, ids_ref, w_ref, expert_ref, msg_ref, mine_ref, *scratch):
    x_buf, dy_buf, ids_buf, w_buf, sems = scratch
    rows, width = x_ref.shape
    top = ids_ref.shape[0]
    lanes = msg_ref.shape[1] - 2 * width
    copy_all([(x_ref, x_buf), (dy_ref, dy_buf), (ids_ref, ids_buf), (w_ref, w_buf)], sems)
    msg_ref[:, :width] = x_buf[...]
    msg_ref[:, width : 2 * width] = dy_buf[...]
    diagonal = lax.broadcasted_iota(jnp.int32, (rows, rows), 0) == lax.broadcasted_iota(
        jnp.int32, (rows, rows), 1
    )
    expert = lax.broadcasted_iota(jnp.int32, (rows, lanes), 1)
    route = jnp.zeros((rows, lanes), jnp.float32)
    for k in range(top):
        named = jnp.sum(jnp.where(diagonal, ids_buf[k : k + 1, :], 0), axis=1, keepdims=True)
        weight = jnp.sum(jnp.where(diagonal, w_buf[k : k + 1, :], 0.0), axis=1, keepdims=True)
        route = route + jnp.where(expert == named, weight, 0.0)
    msg_ref[:, 2 * width :] = route.astype(jnp.bfloat16)
    lane = lax.broadcasted_iota(jnp.int32, mine_ref.shape, 1)
    mine_ref[...] = jnp.where(lane == expert_ref[0], 1.0, 0.0)


def half_body(start, from_ref, to_ref):
    to_ref[...] = from_ref[:, start : start + to_ref.shape[1]]


def passes(have, wg_ref, wu_ref, wd_ref, mine_ref, acts_ref):
    width, ff = wg_ref.shape[2], wg_ref.shape[1]
    x, dy, route = have[:, :width], have[:, width : 2 * width], have[:, 2 * width :]
    weight = contract_rows(mine_ref[...].astype(jnp.bfloat16), route)[:1, :]
    gate_pre = contract_rows(wg_ref[0], x)
    up_pre = contract_rows(wu_ref[0], x)
    hidden_grad = weight * contract_rows(wd_ref[0], dy)
    gate_sig = 1.0 / (1.0 + jnp.exp(-gate_pre))
    silu_gate = gate_pre * gate_sig
    silu_slope = gate_sig * (1.0 + gate_pre * (1.0 - gate_sig))
    acts_ref[:ff, :] = (hidden_grad * up_pre * silu_slope).astype(jnp.bfloat16)
    acts_ref[ff : 2 * ff, :] = (hidden_grad * silu_gate).astype(jnp.bfloat16)
    acts_ref[2 * ff :, :] = (weight * (silu_gate * up_pre)).astype(jnp.bfloat16)
    out = contract_first(acts_ref[2 * ff :, :], wd_ref[0])
    into = contract_first(acts_ref[:ff, :], wg_ref[0]) + contract_first(
        acts_ref[ff : 2 * ff, :], wu_ref[0]
    )
    return out, into


def give(out, into, own_ref, msg_ref):
    half, width = own_ref.shape[0], out.shape[1]
    for i, value in enumerate((out, into)):
        own_ref[:, i * width : (i + 1) * width] = value[:half, :]
        msg_ref[:, i * width : (i + 1) * width] = value[half:, :].astype(jnp.bfloat16)


def early_body(count, *refs):
    pieces, rest = refs[:count], refs[count:]
    wg_ref, wu_ref, wd_ref, mine_ref, have, acts_ref, own_ref, msg_ref = rest
    rows = pieces[0].shape[0]
    for i, piece in enumerate(pieces):
        have[i * rows : (i + 1) * rows, :] = piece[...]
    out, into = passes(have, wg_ref, wu_ref, wd_ref, mine_ref, acts_ref)
    give(out, into, own_ref, msg_ref)


def late_body(*refs):
    pieces, rest = refs[:4], refs[4:]
    wg_ref, wu_ref, wd_ref, mine_ref, have, acts_ref, own_ref, msg_ref = rest
    rows, width = pieces[0].shape
    for i in range(2):
        have[i * rows : (i + 1) * rows, :width] = pieces[2 * i][...]
        have[i * rows : (i + 1) * rows, width:] = pieces[2 * i + 1][...]
    out, into = passes(have, wg_ref, wu_ref, wd_ref, mine_ref, acts_ref)
    give(out, into, own_ref, msg_ref)


def late_sum_body(own_ref, passed_ref, out_ref, into_ref):
    width = out_ref.shape[1]
    total = own_ref[...] + passed_ref[...].astype(jnp.float32)
    out_ref[...] = total[:, :width].astype(jnp.bfloat16)
    into_ref[...] = total[:, width:].astype(jnp.bfloat16)


def early_sum_body(own_ref, passed_ref, into_ref, out_ref, here_ref, first_ref, second_ref):
    rows, width = into_ref.shape

    def total(i, side):
        at = (slice(i * rows, (i + 1) * rows), slice(side * width, (side + 1) * width))
        return own_ref[at] + passed_ref[at].astype(jnp.float32)

    here_ref[:, :width], here_ref[:, width:] = total(0, 0), total(0, 1)
    second_ref[:, :width] = total(1, 0).astype(jnp.bfloat16)
    second_ref[:, width:] = (total(1, 1) + into_ref[...].astype(jnp.float32)).astype(jnp.bfloat16)
    first_ref[:, :width] = (total(2, 0) + out_ref[...].astype(jnp.float32)).astype(jnp.bfloat16)
    first_ref[:, width:] = total(2, 1).astype(jnp.bfloat16)


def grad_body(early_ref, late_ref, early_acts_ref, late_acts_ref, *grads):
    width = grads[0].shape[2]
    ff = grads[0].shape[1]
    for i, ref in enumerate(grads):
        first = early_acts_ref.shape[0] // ff - len(grads) if len(grads) == 1 else 0
        here = slice((first + i) * ff, (first + i + 1) * ff)
        side = slice(width, 2 * width) if len(grads) == 1 else slice(0, width)
        ref[0] = (
            jnp.dot(early_acts_ref[here, :], early_ref[:, side], preferred_element_type=jnp.float32)
            + jnp.dot(late_acts_ref[here, :], late_ref[:, side], preferred_element_type=jnp.float32)
        ).astype(jnp.bfloat16)


def dense(tokens, expert_ids, route_weights, out_grad, gate_weight, up_weight, down_weight):
    experts = lax.axis_size("expert")
    devices = lax.axis_size("dp") * experts
    expert = lax.axis_index("expert").astype(jnp.int32).reshape(1)
    rows, width = tokens.shape
    ff = gate_weight.shape[1]
    near = tuple(k << 3 for k in range(1, devices >> 3))
    block_rows = rows * (len(near) + 1)
    bf16, f32 = jnp.bfloat16, jnp.float32
    columns = 2 * width + experts + -experts % 128
    unit = 2 * block_rows * ff * width

    def shape(*dims, dtype=bf16):
        return jax.ShapeDtypeStruct(dims, dtype)

    def passed(value, mask):
        return from_xor(value, mask, devices)

    message, mine = kernel_call(
        pack_body,
        (shape(rows, columns), shape(8, columns - 2 * width, dtype=f32)),
        0,
        tokens,
        out_grad,
        expert_ids.T,
        route_weights.astype(f32).T,
        expert,
        scratch=[
            pltpu.VMEM((rows, width), bf16),
            pltpu.VMEM((rows, width), bf16),
            pltpu.VMEM(expert_ids.shape[::-1], jnp.int32),
            pltpu.VMEM(expert_ids.shape[::-1], f32),
            pltpu.SemaphoreType.DMA((4,)),
        ],
        hbm=(0, 1, 2, 3),
    )
    weights = kernel_call(
        load_body,
        (shape(*gate_weight.shape),) * 3,
        0,
        gate_weight,
        up_weight,
        down_weight,
        scratch=[pltpu.SemaphoreType.DMA((3,))],
        hbm=(0, 1, 2),
    )
    block = jnp.concatenate([message] + [passed(message, m) for m in near], axis=0)
    block, *weights = lax.optimization_barrier((block, *weights))

    by_second, by_first = passed(block, SECOND), passed(block, FIRST)
    half_x = kernel_call(
        functools.partial(half_body, 0), shape(block_rows, width), 0, by_second
    )
    half_dy = kernel_call(
        functools.partial(half_body, width), shape(block_rows, columns - width), 0, by_first
    )
    by_second, by_first, half_x, half_dy = lax.optimization_barrier(
        (by_second, by_first, half_x, half_dy)
    )
    corner_x, corner_dy = passed(half_x, FIRST), passed(half_dy, SECOND)
    own = [block, by_second, by_first]
    other = [passed(piece, CORE) for piece in own]

    early_rows = len(own) * block_rows
    early, early_acts, early_own, message = kernel_call(
        functools.partial(early_body, 2 * len(own)),
        (
            shape(2 * early_rows, columns),
            shape(3 * ff, 2 * early_rows),
            shape(early_rows, 2 * width, dtype=f32),
            shape(early_rows, 2 * width),
        ),
        36 * unit,
        *own,
        *other,
        *weights,
        mine,
    )
    corner_x, corner_dy, message = lax.optimization_barrier((corner_x, corner_dy, message))
    corner = [corner_x, corner_dy, passed(corner_x, CORE), passed(corner_dy, CORE)]
    early_passed = passed(message, CORE)
    late, late_acts, late_own, message = kernel_call(
        late_body,
        (
            shape(2 * block_rows, columns),
            shape(3 * ff, 2 * block_rows),
            shape(block_rows, 2 * width, dtype=f32),
            shape(block_rows, 2 * width),
        ),
        12 * unit,
        *corner,
        *weights,
        mine,
    )
    late_passed = passed(message, CORE)

    corner_out, corner_into = kernel_call(
        late_sum_body, (shape(block_rows, width),) * 2, 0, late_own, late_passed
    )
    turned_out, turned_into = passed(corner_out, SECOND), passed(corner_into, FIRST)
    (grad_down,) = kernel_call(
        grad_body, (shape(*down_weight.shape),), 8 * unit, early, late, early_acts, late_acts
    )
    grad_gate, grad_up = kernel_call(
        grad_body, (shape(*gate_weight.shape),) * 2, 16 * unit, early, late, early_acts, late_acts
    )
    turned_out, turned_into, grad_down = lax.optimization_barrier(
        (turned_out, turned_into, grad_down)
    )
    here, for_first, for_second = kernel_call(
        early_sum_body,
        (
            shape(block_rows, 2 * width, dtype=f32),
            shape(block_rows, 2 * width),
            shape(block_rows, 2 * width),
        ),
        0,
        early_own,
        early_passed,
        turned_into,
        turned_out,
    )
    from_second, from_first = passed(for_second, SECOND), passed(for_first, FIRST)
    from_second, from_first, grad_gate, grad_up = lax.optimization_barrier(
        (from_second, from_first, grad_gate, grad_up)
    )
    total = here + from_second.astype(f32) + from_first.astype(f32)
    total = total.astype(bf16)
    pieces = [total[k * rows : (k + 1) * rows] for k in range(len(near) + 1)]
    total = pieces[0].astype(f32)
    for m, piece in zip(near, pieces[1:]):
        total = total + passed(piece, m).astype(f32)
    total = total.astype(bf16)

    return total[:, :width], total[:, width:], grad_gate, grad_up, grad_down


def shards(tokens, *others):
    experts = lax.axis_size("expert")
    devices = lax.axis_size("dp") * experts
    whole_group = tokens.shape[0] * experts <= ROW_CAP
    if whole_group and devices >= 16 and devices & (devices - 1) == 0:
        return dense(tokens, *others)
    return slotted(tokens, *others)


def solution(mesh):
    return jax.shard_map(
        shards,
        mesh=mesh,
        in_specs=(
            P(("dp", "expert"), None),
            P(("dp", "expert"), None),
            P(("dp", "expert"), None),
            P(("dp", "expert"), None),
            P("expert", "dp", None),
            P("expert", "dp", None),
            P("expert", "dp", None),
        ),
        out_specs=(
            P(("dp", "expert"), None),
            P(("dp", "expert"), None),
            P("expert", "dp", None),
            P("expert", "dp", None),
            P("expert", "dp", None),
        ),
        check_vma=False,
    )
```

```python
import functools

import jax
import jax.numpy as jnp
from jax import lax
from jax.experimental import pallas as pl
from jax.experimental.pallas import tpu as pltpu
from jax.sharding import PartitionSpec as P

ROW_CAP = 16
AXES = ("dp", "expert")


def contract_rows(left, right):
    return lax.dot_general(
        left, right, (((1,), (1,)), ((), ())), preferred_element_type=jnp.float32
    )


def contract_first(left, right):
    return lax.dot_general(
        left, right, (((0,), (0,)), ((), ())), preferred_element_type=jnp.float32
    )


def slotted(tokens, expert_ids, route_weights, out_grad, gate_weight, up_weight, down_weight):
    expert = lax.axis_index("expert")
    width = tokens.shape[1]
    local_tokens = tokens.shape[0]
    group_x, group_dy, group_w = (
        lax.all_gather(tokens, "expert", axis=0, tiled=True),
        lax.all_gather(out_grad, "expert", axis=0, tiled=True),
        lax.all_gather(route_weights, "expert", axis=0, tiled=True),
    )
    group_ids = lax.all_gather(expert_ids, "expert", axis=0, tiled=True)
    matches = group_ids == expert
    routed = jnp.any(matches, axis=1)
    weight = jnp.sum(jnp.where(matches, group_w.astype(jnp.float32), 0.0), axis=1)
    slot_rank = jnp.cumsum(routed.astype(jnp.int32)) - 1
    slot_index = jnp.arange(ROW_CAP, dtype=jnp.int32)
    picker = ((slot_rank[None, :] == slot_index[:, None]) & routed[None, :]).astype(jnp.bfloat16)
    slot_x = jnp.dot(picker, group_x, preferred_element_type=jnp.float32).astype(jnp.bfloat16)
    scaled = (weight[:, None] * group_dy.astype(jnp.float32)).astype(jnp.bfloat16)
    slot_dy = jnp.dot(picker, scaled, preferred_element_type=jnp.float32).astype(jnp.bfloat16)
    w_gate = gate_weight[0]
    w_up = up_weight[0]
    w_down = down_weight[0]
    all_x = lax.all_gather(slot_x, "dp", axis=0, tiled=True)
    gate_pre = contract_rows(w_gate, all_x)
    up_pre = contract_rows(w_up, all_x)
    gate_sig = jax.nn.sigmoid(gate_pre)
    silu_gate = gate_pre * gate_sig
    hidden = (silu_gate * up_pre).astype(jnp.bfloat16)
    expert_out = lax.psum_scatter(
        contract_first(hidden, w_down).astype(jnp.bfloat16), "dp", scatter_dimension=0, tiled=True
    )
    all_dy = lax.all_gather(slot_dy, "dp", axis=0, tiled=True)
    hidden_grad = contract_rows(w_down, all_dy)
    silu_slope = gate_sig * (1.0 + gate_pre * (1.0 - gate_sig))
    gate_act = (hidden_grad * up_pre * silu_slope).astype(jnp.bfloat16)
    up_act = (hidden_grad * silu_gate).astype(jnp.bfloat16)
    grad_down = jnp.dot(hidden, all_dy, preferred_element_type=jnp.float32).astype(jnp.bfloat16)
    grad_gate = jnp.dot(gate_act, all_x, preferred_element_type=jnp.float32).astype(jnp.bfloat16)
    grad_up = jnp.dot(up_act, all_x, preferred_element_type=jnp.float32).astype(jnp.bfloat16)
    expert_in = lax.psum_scatter(
        (contract_first(gate_act, w_gate) + contract_first(up_act, w_up)).astype(jnp.bfloat16),
        "dp",
        scatter_dimension=0,
        tiled=True,
    )
    back_out = contract_first(picker, expert_out).astype(jnp.bfloat16)
    back_in = contract_first(picker, expert_in).astype(jnp.bfloat16)
    got_out, got_in = (
        lax.all_to_all(back_out, "expert", split_axis=0, concat_axis=0, tiled=True),
        lax.all_to_all(back_in, "expert", split_axis=0, concat_axis=0, tiled=True),
    )
    expert_count = lax.axis_size("expert")
    got_out = got_out.reshape(expert_count, local_tokens, width)
    got_in = got_in.reshape(expert_count, local_tokens, width)
    expert_range = jnp.arange(expert_count, dtype=jnp.int32)
    own_match = expert_ids[:, :, None] == expert_range[None, None, :]
    mix_weight = jnp.sum(
        jnp.where(own_match, route_weights.astype(jnp.float32)[:, :, None], 0.0), axis=1
    )
    mixed_out = jnp.sum(jnp.transpose(mix_weight)[:, :, None] * got_out.astype(jnp.float32), axis=0)
    input_total = jnp.sum(got_in.astype(jnp.float32), axis=0)
    return (
        mixed_out.astype(jnp.bfloat16),
        input_total.astype(jnp.bfloat16),
        grad_gate[None],
        grad_up[None],
        grad_down[None],
    )


CORE, FAR = 1, (2, 4, 6)


def from_xor(value, mask, devices):
    return lax.ppermute(value, AXES, [(i, i ^ mask) for i in range(devices)])


def kernel_call(body, out_shape, cost, *operands, scratch=(), hbm=()):
    vmem, smem = pl.BlockSpec(memory_space=pltpu.VMEM), pl.BlockSpec(memory_space=pltpu.SMEM)
    stay = pl.BlockSpec(memory_space=pltpu.HBM)
    specs = [stay if i in hbm else smem if o.ndim == 1 else vmem for i, o in enumerate(operands)]
    operands = [
        pltpu.with_memory_space_constraint(o, pltpu.HBM) if i in hbm else o
        for i, o in enumerate(operands)
    ]
    return pl.pallas_call(
        body,
        out_shape=out_shape,
        in_specs=specs,
        out_specs=jax.tree.map(lambda _: vmem, out_shape),
        scratch_shapes=scratch,
        compiler_params=pltpu.CompilerParams(vmem_limit_bytes=16 << 20),
        cost_estimate=pl.CostEstimate(flops=cost, bytes_accessed=4 << 20, transcendentals=0),
    )(*operands)


def copy_all(pairs, sems):
    copies = [pltpu.make_async_copy(src, dst, sems.at[i]) for i, (src, dst) in enumerate(pairs)]
    for copy in copies:
        copy.start()
    for copy in copies:
        copy.wait()


def load_body(*refs):
    count = len(refs) // 2
    copy_all(list(zip(refs[:count], refs[count:-1])), refs[-1])


def pack_body(x_ref, dy_ref, ids_ref, w_ref, expert_ref, msg_ref, mine_ref, *scratch):
    x_buf, dy_buf, ids_buf, w_buf, sems = scratch
    rows, width = x_ref.shape
    top = ids_ref.shape[0]
    lanes = msg_ref.shape[1] - 2 * width
    copy_all([(x_ref, x_buf), (dy_ref, dy_buf), (ids_ref, ids_buf), (w_ref, w_buf)], sems)
    msg_ref[:, :width] = x_buf[...]
    msg_ref[:, width : 2 * width] = dy_buf[...]
    diagonal = lax.broadcasted_iota(jnp.int32, (rows, rows), 0) == lax.broadcasted_iota(
        jnp.int32, (rows, rows), 1
    )
    expert = lax.broadcasted_iota(jnp.int32, (rows, lanes), 1)
    top_weights = w_buf[...].astype(jnp.float32)
    route = jnp.zeros((rows, lanes), jnp.float32)
    for k in range(top):
        named = jnp.sum(jnp.where(diagonal, ids_buf[k : k + 1, :], 0), axis=1, keepdims=True)
        weight = jnp.sum(jnp.where(diagonal, top_weights[k : k + 1, :], 0.0), axis=1, keepdims=True)
        route = route + jnp.where(expert == named, weight, 0.0)
    msg_ref[:, 2 * width :] = route.astype(jnp.bfloat16)
    lane = lax.broadcasted_iota(jnp.int32, mine_ref.shape, 1)
    mine_ref[...] = jnp.where(lane == expert_ref[0], 1.0, 0.0)


def places(pieces):
    start = 0
    for piece in pieces:
        yield slice(start, start + piece.shape[0]), piece
        start += piece.shape[0]


def cotangent_places(pieces):
    rows = pieces[0].shape[0] // 2
    for i, piece in enumerate(pieces):
        for k in range(2):
            at = i // 2 * 4 + (2 * k if i % 2 == 0 else 2 * k + 1)
            yield slice(at * rows, (at + 1) * rows), piece, slice(k * rows, (k + 1) * rows)


def stack_body(*refs):
    for here, piece in places(refs[:-1]):
        refs[-1][here, :] = piece[...]


def forward_body(count, *refs):
    pieces, (wg_ref, wu_ref, x_ref, hidden_ref, gate_ref, up_ref) = refs[:count], refs[count:]
    for here, piece in places(pieces):
        x_ref[here, :] = piece[...]
    x = x_ref[...]
    gate_pre = contract_rows(x, wg_ref[0])
    up_pre = contract_rows(x, wu_ref[0])
    gate_sig = 1.0 / (1.0 + jnp.exp(-gate_pre))
    silu_gate = gate_pre * gate_sig
    hidden_ref[...] = silu_gate * up_pre
    gate_ref[...] = up_pre * (gate_sig * (1.0 + gate_pre * (1.0 - gate_sig)))
    up_ref[...] = silu_gate


def out_body(count, *refs):
    pieces, (hidden_ref, wd_ref, mine_ref, weight_ref, scaled_ref, msg_ref) = (
        refs[:count],
        refs[count:],
    )
    half, width = msg_ref.shape
    for here, piece, there in cotangent_places(pieces):
        route = piece[there, width:].astype(jnp.float32) * mine_ref[:1, :]
        weight = jnp.sum(route, axis=1, keepdims=True)
        weight_ref[here, :] = jnp.broadcast_to(weight, (route.shape[0], weight_ref.shape[1]))
        scaled_ref[here, :] = (weight * hidden_ref[here, :]).astype(jnp.bfloat16)
    msg_ref[...] = jnp.dot(
        scaled_ref[half:, :], wd_ref[0], preferred_element_type=jnp.float32
    ).astype(jnp.bfloat16)


def into_sum(gate_act, up_act, wg_ref, wu_ref):
    return jnp.dot(gate_act, wg_ref[0], preferred_element_type=jnp.float32) + jnp.dot(
        up_act, wu_ref[0], preferred_element_type=jnp.float32
    )


def into_body(count, *refs):
    pieces, rest = refs[:count], refs[count:]
    weight_ref, gate_ref, up_ref, wg_ref, wu_ref, wd_ref = rest[:6]
    dy_ref, gate_act_ref, up_act_ref, msg_ref = rest[6:]
    half, width = msg_ref.shape
    for here, piece, there in cotangent_places(pieces):
        dy_ref[here, :] = piece[there, :width]
    hidden_grad = weight_ref[:, :1] * contract_rows(dy_ref[...], wd_ref[0])
    gate_act_ref[...] = (hidden_grad * gate_ref[...]).astype(jnp.bfloat16)
    up_act_ref[...] = (hidden_grad * up_ref[...]).astype(jnp.bfloat16)
    msg_ref[...] = into_sum(gate_act_ref[half:, :], up_act_ref[half:, :], wg_ref, wu_ref).astype(
        jnp.bfloat16
    )


def scattered(total, outs):
    rows = outs[0].shape[0]
    for i, ref in enumerate(outs):
        ref[...] = total[i * rows : (i + 1) * rows, :].astype(ref.dtype)


def own_out_body(scaled_ref, wd_ref, passed_ref, *outs):
    half = passed_ref.shape[0]
    total = jnp.dot(scaled_ref[:half, :], wd_ref[0], preferred_element_type=jnp.float32)
    scattered(total + passed_ref[...].astype(jnp.float32), outs)


def own_into_body(gate_act_ref, up_act_ref, wg_ref, wu_ref, passed_ref, *outs):
    half = passed_ref.shape[0]
    total = into_sum(gate_act_ref[:half, :], up_act_ref[:half, :], wg_ref, wu_ref)
    scattered(total + passed_ref[...].astype(jnp.float32), outs)


def turn_body(here_ref, came_ref, to_ref):
    to_ref[...] = (here_ref[...] + came_ref[...].astype(jnp.float32)).astype(jnp.bfloat16)


def deal_body(*refs):
    parts, outs = refs[:6], refs[6:]
    width, rows = parts[0].shape[1], outs[0].shape[0]
    for side in range(2):
        at = slice(side * width, (side + 1) * width)
        here = parts[3 * side : 3 * side + 3]
        total = here[0][...]
        for part in here[1:]:
            total = total + part[...].astype(jnp.float32)
        for i, ref in enumerate(outs):
            ref[:, at] = total[i * rows : (i + 1) * rows, :].astype(ref.dtype)


def end_body(own_ref, *refs):
    parts, (out_ref, into_ref) = refs[:-2], refs[-2:]
    total = own_ref[...]
    for part in parts:
        total = total + part[...].astype(jnp.float32)
    width = out_ref.shape[1]
    out_ref[...] = total[:, :width].astype(jnp.bfloat16)
    into_ref[...] = total[:, width:].astype(jnp.bfloat16)


def grad_body(rows_ref, *refs):
    acts, grads = refs[: len(refs) // 2], refs[len(refs) // 2 :]
    for act_ref, ref in zip(acts, grads):
        ref[0] = contract_first(act_ref[...], rows_ref[...]).astype(jnp.bfloat16)


def dense(tokens, expert_ids, route_weights, out_grad, gate_weight, up_weight, down_weight):
    experts = lax.axis_size("expert")
    devices = lax.axis_size("dp") * experts
    expert = lax.axis_index("expert").astype(jnp.int32).reshape(1)
    rows, width = tokens.shape
    ff = gate_weight.shape[1]
    near = tuple(k << 3 for k in range(1, devices >> 3))
    block_rows = rows * (len(near) + 1)
    bf16, f32 = jnp.bfloat16, jnp.float32
    columns = 2 * width + experts + -experts % 128
    unit = 2 * block_rows * ff * width

    def shape(*dims, dtype=bf16):
        return jax.ShapeDtypeStruct(dims, dtype)

    def passed(value, mask):
        return from_xor(value, mask, devices)

    message, mine = kernel_call(
        pack_body,
        (shape(rows, columns), shape(8, columns - 2 * width, dtype=f32)),
        0,
        tokens,
        out_grad,
        expert_ids.T,
        route_weights.T,
        expert,
        scratch=[
            pltpu.VMEM((rows, width), bf16),
            pltpu.VMEM((rows, width), bf16),
            pltpu.VMEM(expert_ids.shape[::-1], jnp.int32),
            pltpu.VMEM(route_weights.shape[::-1], bf16),
            pltpu.SemaphoreType.DMA((4,)),
        ],
        hbm=(0, 1, 2, 3),
    )
    weights = kernel_call(
        load_body,
        (shape(*gate_weight.shape),) * 3,
        0,
        gate_weight,
        up_weight,
        down_weight,
        scratch=[pltpu.SemaphoreType.DMA((3,))],
        hbm=(0, 1, 2),
    )
    arrived = [message] + [passed(message, m) for m in near]
    block_x = jnp.concatenate([piece[:, :width] for piece in arrived], axis=0)
    block_dy = jnp.concatenate([piece[:, width:] for piece in arrived], axis=0)
    block_x, block_dy, *weights = lax.optimization_barrier((block_x, block_dy, *weights))
    w_gate, w_up, w_down = weights

    first, second, _ = FAR
    second_x, first_dy = passed(block_x, second), passed(block_dy, first)
    second_dy, first_x = passed(block_dy, second), passed(block_x, first)
    corner_x, corner_dy = passed(second_x, first), passed(first_dy, second)
    half = (len(FAR) + 1) * block_rows

    def both_cores(*pairs):
        own = [
            kernel_call(stack_body, shape(2 * block_rows, pair[0].shape[1]), 0, *pair)
            for pair in pairs
        ]
        return own + [passed(pair, CORE) for pair in own]

    x_pieces = both_cores((block_x, second_x), (first_x, corner_x))
    early_dy, late_dy, other_early, other_late = both_cores(
        (block_dy, first_dy), (second_dy, corner_dy)
    )
    dy_pieces = [early_dy, late_dy, other_early, other_late]
    all_x, hidden, gate_part, up_part = kernel_call(
        functools.partial(forward_body, len(x_pieces)),
        (shape(2 * half, width),) + (shape(2 * half, ff, dtype=f32),) * 3,
        16 * unit,
        *x_pieces,
        w_gate,
        w_up,
    )
    weight, scaled, message = kernel_call(
        functools.partial(out_body, len(dy_pieces)),
        (
            shape(2 * half, columns - 2 * width, dtype=f32),
            shape(2 * half, ff),
            shape(half, width),
        ),
        4 * unit,
        *dy_pieces,
        hidden,
        w_down,
        mine,
    )
    passed_out = passed(message, CORE)
    all_dy, gate_act, up_act, message = kernel_call(
        functools.partial(into_body, len(dy_pieces)),
        (shape(2 * half, width), shape(2 * half, ff), shape(2 * half, ff), shape(half, width)),
        16 * unit,
        *dy_pieces,
        weight,
        gate_part,
        up_part,
        *weights,
    )
    passed_into = passed(message, CORE)

    piece, full = shape(block_rows, width), shape(block_rows, width, dtype=f32)
    out_here, out_second, out_first, out_corner = kernel_call(
        own_out_body, (full, piece, full, piece), 4 * unit, scaled, w_down, passed_out
    )
    passed_into, out_here = lax.optimization_barrier((passed_into, out_here))
    into_here, into_second, into_first, into_corner = kernel_call(
        own_into_body, (full, full, piece, piece), 8 * unit, gate_act, up_act, w_gate, w_up, passed_into
    )
    out_first = kernel_call(turn_body, piece, 0, out_first, passed(out_corner, second))
    into_second = kernel_call(turn_body, piece, 0, into_second, passed(into_corner, first))
    out_back = [passed(out_second, second), passed(out_first, first)]
    into_back = [passed(into_first, first), passed(into_second, second)]
    into_here, scaled, gate_act, up_act = lax.optimization_barrier(
        (into_here, scaled, gate_act, up_act)
    )
    grad_down = kernel_call(grad_body, shape(*down_weight.shape), 8 * unit, all_dy, scaled)
    into_here, grad_down = lax.optimization_barrier((into_here, grad_down))
    mine_sum, *away = kernel_call(
        deal_body,
        (shape(rows, 2 * width, dtype=f32),) + (shape(rows, 2 * width),) * len(near),
        0,
        out_here,
        *out_back,
        into_here,
        *into_back,
    )
    mine_sum, gate_act, up_act = lax.optimization_barrier((mine_sum, gate_act, up_act))
    grad_gate, grad_up = kernel_call(
        grad_body, (shape(*gate_weight.shape),) * 2, 16 * unit, all_x, gate_act, up_act
    )
    mixed, input_grad = kernel_call(
        end_body,
        (shape(rows, width),) * 2,
        0,
        mine_sum,
        *[passed(piece, m) for m, piece in zip(near, away)],
    )
    return mixed, input_grad, grad_gate, grad_up, grad_down


def shards(tokens, *others):
    experts = lax.axis_size("expert")
    devices = lax.axis_size("dp") * experts
    whole_group = tokens.shape[0] * experts <= ROW_CAP
    if whole_group and devices >= 16 and devices & (devices - 1) == 0:
        return dense(tokens, *others)
    return slotted(tokens, *others)


def solution(mesh):
    return jax.shard_map(
        shards,
        mesh=mesh,
        in_specs=(
            P(("dp", "expert"), None),
            P(("dp", "expert"), None),
            P(("dp", "expert"), None),
            P(("dp", "expert"), None),
            P("expert", "dp", None),
            P("expert", "dp", None),
            P("expert", "dp", None),
        ),
        out_specs=(
            P(("dp", "expert"), None),
            P(("dp", "expert"), None),
            P("expert", "dp", None),
            P("expert", "dp", None),
            P("expert", "dp", None),
        ),
        check_vma=False,
    )
```

```python
import functools

import jax
import jax.numpy as jnp
from jax import lax
from jax.experimental import pallas as pl
from jax.experimental.pallas import tpu as pltpu
from jax.sharding import PartitionSpec as P

ROW_CAP = 16
AXES = ("dp", "expert")


def contract_rows(left, right):
    return lax.dot_general(
        left, right, (((1,), (1,)), ((), ())), preferred_element_type=jnp.float32
    )


def contract_first(left, right):
    return lax.dot_general(
        left, right, (((0,), (0,)), ((), ())), preferred_element_type=jnp.float32
    )


def slotted(tokens, expert_ids, route_weights, out_grad, gate_weight, up_weight, down_weight):
    expert = lax.axis_index("expert")
    width = tokens.shape[1]
    local_tokens = tokens.shape[0]
    group_x, group_dy, group_w = (
        lax.all_gather(tokens, "expert", axis=0, tiled=True),
        lax.all_gather(out_grad, "expert", axis=0, tiled=True),
        lax.all_gather(route_weights, "expert", axis=0, tiled=True),
    )
    group_ids = lax.all_gather(expert_ids, "expert", axis=0, tiled=True)
    matches = group_ids == expert
    routed = jnp.any(matches, axis=1)
    weight = jnp.sum(jnp.where(matches, group_w.astype(jnp.float32), 0.0), axis=1)
    slot_rank = jnp.cumsum(routed.astype(jnp.int32)) - 1
    slot_index = jnp.arange(ROW_CAP, dtype=jnp.int32)
    picker = ((slot_rank[None, :] == slot_index[:, None]) & routed[None, :]).astype(jnp.bfloat16)
    slot_x = jnp.dot(picker, group_x, preferred_element_type=jnp.float32).astype(jnp.bfloat16)
    scaled = (weight[:, None] * group_dy.astype(jnp.float32)).astype(jnp.bfloat16)
    slot_dy = jnp.dot(picker, scaled, preferred_element_type=jnp.float32).astype(jnp.bfloat16)
    w_gate = gate_weight[0]
    w_up = up_weight[0]
    w_down = down_weight[0]
    all_x = lax.all_gather(slot_x, "dp", axis=0, tiled=True)
    gate_pre = contract_rows(w_gate, all_x)
    up_pre = contract_rows(w_up, all_x)
    gate_sig = jax.nn.sigmoid(gate_pre)
    silu_gate = gate_pre * gate_sig
    hidden = (silu_gate * up_pre).astype(jnp.bfloat16)
    expert_out = lax.psum_scatter(
        contract_first(hidden, w_down).astype(jnp.bfloat16), "dp", scatter_dimension=0, tiled=True
    )
    all_dy = lax.all_gather(slot_dy, "dp", axis=0, tiled=True)
    hidden_grad = contract_rows(w_down, all_dy)
    silu_slope = gate_sig * (1.0 + gate_pre * (1.0 - gate_sig))
    gate_act = (hidden_grad * up_pre * silu_slope).astype(jnp.bfloat16)
    up_act = (hidden_grad * silu_gate).astype(jnp.bfloat16)
    grad_down = jnp.dot(hidden, all_dy, preferred_element_type=jnp.float32).astype(jnp.bfloat16)
    grad_gate = jnp.dot(gate_act, all_x, preferred_element_type=jnp.float32).astype(jnp.bfloat16)
    grad_up = jnp.dot(up_act, all_x, preferred_element_type=jnp.float32).astype(jnp.bfloat16)
    expert_in = lax.psum_scatter(
        (contract_first(gate_act, w_gate) + contract_first(up_act, w_up)).astype(jnp.bfloat16),
        "dp",
        scatter_dimension=0,
        tiled=True,
    )
    back_out = contract_first(picker, expert_out).astype(jnp.bfloat16)
    back_in = contract_first(picker, expert_in).astype(jnp.bfloat16)
    got_out, got_in = (
        lax.all_to_all(back_out, "expert", split_axis=0, concat_axis=0, tiled=True),
        lax.all_to_all(back_in, "expert", split_axis=0, concat_axis=0, tiled=True),
    )
    expert_count = lax.axis_size("expert")
    got_out = got_out.reshape(expert_count, local_tokens, width)
    got_in = got_in.reshape(expert_count, local_tokens, width)
    expert_range = jnp.arange(expert_count, dtype=jnp.int32)
    own_match = expert_ids[:, :, None] == expert_range[None, None, :]
    mix_weight = jnp.sum(
        jnp.where(own_match, route_weights.astype(jnp.float32)[:, :, None], 0.0), axis=1
    )
    mixed_out = jnp.sum(jnp.transpose(mix_weight)[:, :, None] * got_out.astype(jnp.float32), axis=0)
    input_total = jnp.sum(got_in.astype(jnp.float32), axis=0)
    return (
        mixed_out.astype(jnp.bfloat16),
        input_total.astype(jnp.bfloat16),
        grad_gate[None],
        grad_up[None],
        grad_down[None],
    )


CORE, FAR = 1, (2, 4, 6)


def from_xor(value, mask, devices):
    return lax.ppermute(value, AXES, [(i, i ^ mask) for i in range(devices)])


def kernel_call(body, out_shape, cost, *operands, scratch=(), hbm=()):
    vmem, smem = pl.BlockSpec(memory_space=pltpu.VMEM), pl.BlockSpec(memory_space=pltpu.SMEM)
    stay = pl.BlockSpec(memory_space=pltpu.HBM)
    specs = [stay if i in hbm else smem if o.ndim == 1 else vmem for i, o in enumerate(operands)]
    operands = [
        pltpu.with_memory_space_constraint(o, pltpu.HBM) if i in hbm else o
        for i, o in enumerate(operands)
    ]
    return pl.pallas_call(
        body,
        out_shape=out_shape,
        in_specs=specs,
        out_specs=jax.tree.map(lambda _: vmem, out_shape),
        scratch_shapes=scratch,
        compiler_params=pltpu.CompilerParams(vmem_limit_bytes=16 << 20),
        cost_estimate=pl.CostEstimate(flops=cost, bytes_accessed=4 << 20, transcendentals=0),
    )(*operands)


def copy_all(pairs, sems):
    copies = [pltpu.make_async_copy(src, dst, sems.at[i]) for i, (src, dst) in enumerate(pairs)]
    for copy in copies:
        copy.start()
    for copy in copies:
        copy.wait()


def load_body(*refs):
    count = len(refs) // 2
    copy_all(list(zip(refs[:count], refs[count:-1])), refs[-1])


def pack_body(x_ref, dy_ref, ids_ref, w_ref, expert_ref, msg_ref, mine_ref, *scratch):
    x_buf, dy_buf, ids_buf, w_buf, sems = scratch
    rows, width = x_ref.shape
    top = ids_ref.shape[0]
    lanes = msg_ref.shape[1] - 2 * width
    copy_all([(x_ref, x_buf), (dy_ref, dy_buf), (ids_ref, ids_buf), (w_ref, w_buf)], sems)
    msg_ref[:, :width] = x_buf[...]
    msg_ref[:, width : 2 * width] = dy_buf[...]
    diagonal = lax.broadcasted_iota(jnp.int32, (rows, rows), 0) == lax.broadcasted_iota(
        jnp.int32, (rows, rows), 1
    )
    expert = lax.broadcasted_iota(jnp.int32, (rows, lanes), 1)
    top_weights = w_buf[...].astype(jnp.float32)
    route = jnp.zeros((rows, lanes), jnp.float32)
    for k in range(top):
        named = jnp.sum(jnp.where(diagonal, ids_buf[k : k + 1, :], 0), axis=1, keepdims=True)
        weight = jnp.sum(jnp.where(diagonal, top_weights[k : k + 1, :], 0.0), axis=1, keepdims=True)
        route = route + jnp.where(expert == named, weight, 0.0)
    msg_ref[:, 2 * width :] = route.astype(jnp.bfloat16)
    lane = lax.broadcasted_iota(jnp.int32, mine_ref.shape, 1)
    mine_ref[...] = jnp.where(lane == expert_ref[0], 1.0, 0.0)


def places(pieces):
    start = 0
    for piece in pieces:
        yield slice(start, start + piece.shape[0]), piece
        start += piece.shape[0]


def cotangent_places(pieces):
    rows = pieces[0].shape[0] // 2
    for i, piece in enumerate(pieces):
        for k in range(2):
            at = i // 2 * 4 + (2 * k if i % 2 == 0 else 2 * k + 1)
            yield slice(at * rows, (at + 1) * rows), piece, slice(k * rows, (k + 1) * rows)


def stack_body(*refs):
    for here, piece in places(refs[:-1]):
        refs[-1][here, :] = piece[...]


def forward_body(count, *refs):
    pieces, (wg_ref, wu_ref, x_ref, hidden_ref, gate_ref, up_ref) = refs[:count], refs[count:]
    for here, piece in places(pieces):
        x_ref[here, :] = piece[...]
    x = x_ref[...]
    gate_pre = contract_rows(x, wg_ref[0])
    up_pre = contract_rows(x, wu_ref[0])
    gate_sig = 1.0 / (1.0 + jnp.exp(-gate_pre))
    silu_gate = gate_pre * gate_sig
    hidden_ref[...] = silu_gate * up_pre
    gate_ref[...] = up_pre * (gate_sig * (1.0 + gate_pre * (1.0 - gate_sig)))
    up_ref[...] = silu_gate


def corner_body(own_ref, came_ref, out_ref, into_ref):
    rows, width = out_ref.shape
    for side, ref in enumerate((out_ref, into_ref)):
        at = slice(side * width, (side + 1) * width)
        ref[...] = (own_ref[-rows:, at] + came_ref[:, at].astype(jnp.float32)).astype(jnp.bfloat16)


def most_body(own_ref, came_ref, *outs):
    rows, width = outs[0].shape
    for i, ref in enumerate(outs):
        here = (slice(i % 3 * rows, (i % 3 + 1) * rows), slice(i // 3 * width, (i // 3 + 1) * width))
        ref[...] = (own_ref[here] + came_ref[here].astype(jnp.float32)).astype(ref.dtype)


def backward_body(count, *refs):
    pieces, rest = refs[:count], refs[count:]
    hidden_ref, gate_ref, up_ref, mine_ref, wg_ref, wu_ref, wd_ref = rest[:7]
    dy_ref, scaled_ref, gate_act_ref, up_act_ref, own_ref, most_ref, corner_ref, weight_ref = rest[7:]
    width = dy_ref.shape[1]
    for here, piece, there in cotangent_places(pieces):
        dy_ref[here, :] = piece[there, :width]
        route = piece[there, width:].astype(jnp.float32) * mine_ref[:1, :]
        weight = jnp.sum(route, axis=1, keepdims=True)
        weight_ref[here, :] = jnp.broadcast_to(weight, (route.shape[0], weight_ref.shape[1]))
    weight = weight_ref[:, :1]
    scaled_ref[...] = (weight * hidden_ref[...]).astype(jnp.bfloat16)
    hidden_grad = weight * contract_rows(dy_ref[...], wd_ref[0])
    gate_act_ref[...] = (hidden_grad * gate_ref[...]).astype(jnp.bfloat16)
    up_act_ref[...] = (hidden_grad * up_ref[...]).astype(jnp.bfloat16)
    out = jnp.dot(scaled_ref[...], wd_ref[0], preferred_element_type=jnp.float32)
    into = jnp.dot(gate_act_ref[...], wg_ref[0], preferred_element_type=jnp.float32) + jnp.dot(
        up_act_ref[...], wu_ref[0], preferred_element_type=jnp.float32
    )
    half, most = own_ref.shape[0], most_ref.shape[0]
    for side, total in enumerate((out, into)):
        at = slice(side * width, (side + 1) * width)
        own_ref[:, at] = total[:half, :]
        corner_ref[:, at] = total[half + most :, :].astype(jnp.bfloat16)
        most_ref[:, at] = total[half : half + most, :].astype(jnp.bfloat16)


def turn_body(here_ref, came_ref, to_ref):
    to_ref[...] = (here_ref[...] + came_ref[...].astype(jnp.float32)).astype(jnp.bfloat16)


def deal_body(*refs):
    parts, outs = refs[:6], refs[6:]
    width, rows = parts[0].shape[1], outs[0].shape[0]
    for side in range(2):
        at = slice(side * width, (side + 1) * width)
        here = parts[3 * side : 3 * side + 3]
        total = here[0][...]
        for part in here[1:]:
            total = total + part[...].astype(jnp.float32)
        for i, ref in enumerate(outs):
            ref[:, at] = total[i * rows : (i + 1) * rows, :].astype(ref.dtype)


def end_body(own_ref, *refs):
    parts, (out_ref, into_ref) = refs[:-2], refs[-2:]
    total = own_ref[...]
    for part in parts:
        total = total + part[...].astype(jnp.float32)
    width = out_ref.shape[1]
    out_ref[...] = total[:, :width].astype(jnp.bfloat16)
    into_ref[...] = total[:, width:].astype(jnp.bfloat16)


def grad_body(rows_ref, *refs):
    acts, grads = refs[: len(refs) // 2], refs[len(refs) // 2 :]
    for act_ref, ref in zip(acts, grads):
        ref[0] = contract_first(act_ref[...], rows_ref[...]).astype(jnp.bfloat16)


def dense(tokens, expert_ids, route_weights, out_grad, gate_weight, up_weight, down_weight):
    experts = lax.axis_size("expert")
    devices = lax.axis_size("dp") * experts
    expert = lax.axis_index("expert").astype(jnp.int32).reshape(1)
    rows, width = tokens.shape
    ff = gate_weight.shape[1]
    near = tuple(k << 3 for k in range(1, devices >> 3))
    block_rows = rows * (len(near) + 1)
    bf16, f32 = jnp.bfloat16, jnp.float32
    columns = 2 * width + experts + -experts % 128
    unit = 2 * block_rows * ff * width

    def shape(*dims, dtype=bf16):
        return jax.ShapeDtypeStruct(dims, dtype)

    def passed(value, mask):
        return from_xor(value, mask, devices)

    message, mine = kernel_call(
        pack_body,
        (shape(rows, columns), shape(8, columns - 2 * width, dtype=f32)),
        0,
        tokens,
        out_grad,
        expert_ids.T,
        route_weights.T,
        expert,
        scratch=[
            pltpu.VMEM((rows, width), bf16),
            pltpu.VMEM((rows, width), bf16),
            pltpu.VMEM(expert_ids.shape[::-1], jnp.int32),
            pltpu.VMEM(route_weights.shape[::-1], bf16),
            pltpu.SemaphoreType.DMA((4,)),
        ],
        hbm=(0, 1, 2, 3),
    )
    weights = kernel_call(
        load_body,
        (shape(*gate_weight.shape),) * 3,
        0,
        gate_weight,
        up_weight,
        down_weight,
        scratch=[pltpu.SemaphoreType.DMA((3,))],
        hbm=(0, 1, 2),
    )
    arrived = [message] + [passed(message, m) for m in near]
    block_x = jnp.concatenate([piece[:, :width] for piece in arrived], axis=0)
    block_dy = jnp.concatenate([piece[:, width:] for piece in arrived], axis=0)
    block_x, block_dy, *weights = lax.optimization_barrier((block_x, block_dy, *weights))
    w_gate, w_up, w_down = weights

    first, second, _ = FAR
    second_x, first_dy = passed(block_x, second), passed(block_dy, first)
    second_dy, first_x = passed(block_dy, second), passed(block_x, first)
    corner_x, corner_dy = passed(second_x, first), passed(first_dy, second)
    half = (len(FAR) + 1) * block_rows

    def both_cores(*pairs):
        own = [
            kernel_call(stack_body, shape(2 * block_rows, pair[0].shape[1]), 0, *pair)
            for pair in pairs
        ]
        return own + [passed(pair, CORE) for pair in own]

    x_pieces = both_cores((block_x, second_x), (first_x, corner_x))
    early_dy, late_dy, other_early, other_late = both_cores(
        (block_dy, first_dy), (second_dy, corner_dy)
    )
    dy_pieces = [early_dy, late_dy, other_early, other_late]
    all_x, hidden, gate_part, up_part = kernel_call(
        functools.partial(forward_body, len(x_pieces)),
        (shape(2 * half, width),) + (shape(2 * half, ff, dtype=f32),) * 3,
        16 * unit,
        *x_pieces,
        w_gate,
        w_up,
    )
    all_dy, scaled, gate_act, up_act, own, message, corner_message = kernel_call(
        functools.partial(backward_body, len(dy_pieces)),
        (
            shape(2 * half, width),
            *(shape(2 * half, ff),) * 3,
            shape(half, 2 * width, dtype=f32),
            shape(half - block_rows, 2 * width),
            shape(block_rows, 2 * width),
        ),
        24 * unit,
        *dy_pieces,
        hidden,
        gate_part,
        up_part,
        mine,
        *weights,
        scratch=[pltpu.VMEM((2 * half, columns - 2 * width), f32)],
    )
    corner_came = passed(corner_message, CORE)
    corner_came, message = lax.optimization_barrier((corner_came, message))
    most_came = passed(message, CORE)

    piece, full = shape(block_rows, width), shape(block_rows, width, dtype=f32)
    out_corner, into_corner = kernel_call(corner_body, (piece, piece), 0, own, corner_came)
    out_here, out_second, out_first, into_here, into_second, into_first = kernel_call(
        most_body, (full, piece, full, full, full, piece), 0, own, most_came
    )
    out_turn, into_turn = passed(out_corner, second), passed(into_corner, first)
    out_second, into_first = passed(out_second, second), passed(into_first, first)
    scaled, out_second, into_first = lax.optimization_barrier((scaled, out_second, into_first))
    out_first = passed(kernel_call(turn_body, piece, 0, out_first, out_turn), first)
    into_second = passed(kernel_call(turn_body, piece, 0, into_second, into_turn), second)
    into_here, scaled, gate_act, up_act = lax.optimization_barrier(
        (into_here, scaled, gate_act, up_act)
    )
    grad_down = kernel_call(grad_body, shape(*down_weight.shape), 8 * unit, all_dy, scaled)
    into_here, grad_down = lax.optimization_barrier((into_here, grad_down))
    mine_sum, *away = kernel_call(
        deal_body,
        (shape(rows, 2 * width, dtype=f32),) + (shape(rows, 2 * width),) * len(near),
        0,
        out_here,
        out_second,
        out_first,
        into_here,
        into_first,
        into_second,
    )
    mine_sum, gate_act, up_act = lax.optimization_barrier((mine_sum, gate_act, up_act))
    grad_gate, grad_up = kernel_call(
        grad_body, (shape(*gate_weight.shape),) * 2, 16 * unit, all_x, gate_act, up_act
    )
    mixed, input_grad = kernel_call(
        end_body,
        (shape(rows, width),) * 2,
        0,
        mine_sum,
        *[passed(piece, m) for m, piece in reversed(list(zip(near, away)))],
    )
    return mixed, input_grad, grad_gate, grad_up, grad_down


def shards(tokens, *others):
    experts = lax.axis_size("expert")
    devices = lax.axis_size("dp") * experts
    whole_group = tokens.shape[0] * experts <= ROW_CAP
    if whole_group and devices >= 16 and devices & (devices - 1) == 0:
        return dense(tokens, *others)
    return slotted(tokens, *others)


def solution(mesh):
    return jax.shard_map(
        shards,
        mesh=mesh,
        in_specs=(
            P(("dp", "expert"), None),
            P(("dp", "expert"), None),
            P(("dp", "expert"), None),
            P(("dp", "expert"), None),
            P("expert", "dp", None),
            P("expert", "dp", None),
            P("expert", "dp", None),
        ),
        out_specs=(
            P(("dp", "expert"), None),
            P(("dp", "expert"), None),
            P("expert", "dp", None),
            P("expert", "dp", None),
            P("expert", "dp", None),
        ),
        check_vma=False,
    )
```

```python
import functools

import jax
import jax.numpy as jnp
from jax import lax
from jax.experimental import pallas as pl
from jax.experimental.pallas import tpu as pltpu
from jax.sharding import PartitionSpec as P

ROW_CAP = 16
AXES = ("dp", "expert")


def contract_rows(left, right):
    return lax.dot_general(
        left, right, (((1,), (1,)), ((), ())), preferred_element_type=jnp.float32
    )


def contract_first(left, right):
    return lax.dot_general(
        left, right, (((0,), (0,)), ((), ())), preferred_element_type=jnp.float32
    )


def slotted(tokens, expert_ids, route_weights, out_grad, gate_weight, up_weight, down_weight):
    expert = lax.axis_index("expert")
    width = tokens.shape[1]
    local_tokens = tokens.shape[0]
    group_x, group_dy, group_w = (
        lax.all_gather(tokens, "expert", axis=0, tiled=True),
        lax.all_gather(out_grad, "expert", axis=0, tiled=True),
        lax.all_gather(route_weights, "expert", axis=0, tiled=True),
    )
    group_ids = lax.all_gather(expert_ids, "expert", axis=0, tiled=True)
    matches = group_ids == expert
    routed = jnp.any(matches, axis=1)
    weight = jnp.sum(jnp.where(matches, group_w.astype(jnp.float32), 0.0), axis=1)
    slot_rank = jnp.cumsum(routed.astype(jnp.int32)) - 1
    slot_index = jnp.arange(ROW_CAP, dtype=jnp.int32)
    picker = ((slot_rank[None, :] == slot_index[:, None]) & routed[None, :]).astype(jnp.bfloat16)
    slot_x = jnp.dot(picker, group_x, preferred_element_type=jnp.float32).astype(jnp.bfloat16)
    scaled = (weight[:, None] * group_dy.astype(jnp.float32)).astype(jnp.bfloat16)
    slot_dy = jnp.dot(picker, scaled, preferred_element_type=jnp.float32).astype(jnp.bfloat16)
    w_gate = gate_weight[0]
    w_up = up_weight[0]
    w_down = down_weight[0]
    all_x = lax.all_gather(slot_x, "dp", axis=0, tiled=True)
    gate_pre = contract_rows(w_gate, all_x)
    up_pre = contract_rows(w_up, all_x)
    gate_sig = jax.nn.sigmoid(gate_pre)
    silu_gate = gate_pre * gate_sig
    hidden = (silu_gate * up_pre).astype(jnp.bfloat16)
    expert_out = lax.psum_scatter(
        contract_first(hidden, w_down).astype(jnp.bfloat16), "dp", scatter_dimension=0, tiled=True
    )
    all_dy = lax.all_gather(slot_dy, "dp", axis=0, tiled=True)
    hidden_grad = contract_rows(w_down, all_dy)
    silu_slope = gate_sig * (1.0 + gate_pre * (1.0 - gate_sig))
    gate_act = (hidden_grad * up_pre * silu_slope).astype(jnp.bfloat16)
    up_act = (hidden_grad * silu_gate).astype(jnp.bfloat16)
    grad_down = jnp.dot(hidden, all_dy, preferred_element_type=jnp.float32).astype(jnp.bfloat16)
    grad_gate = jnp.dot(gate_act, all_x, preferred_element_type=jnp.float32).astype(jnp.bfloat16)
    grad_up = jnp.dot(up_act, all_x, preferred_element_type=jnp.float32).astype(jnp.bfloat16)
    expert_in = lax.psum_scatter(
        (contract_first(gate_act, w_gate) + contract_first(up_act, w_up)).astype(jnp.bfloat16),
        "dp",
        scatter_dimension=0,
        tiled=True,
    )
    back_out = contract_first(picker, expert_out).astype(jnp.bfloat16)
    back_in = contract_first(picker, expert_in).astype(jnp.bfloat16)
    got_out, got_in = (
        lax.all_to_all(back_out, "expert", split_axis=0, concat_axis=0, tiled=True),
        lax.all_to_all(back_in, "expert", split_axis=0, concat_axis=0, tiled=True),
    )
    expert_count = lax.axis_size("expert")
    got_out = got_out.reshape(expert_count, local_tokens, width)
    got_in = got_in.reshape(expert_count, local_tokens, width)
    expert_range = jnp.arange(expert_count, dtype=jnp.int32)
    own_match = expert_ids[:, :, None] == expert_range[None, None, :]
    mix_weight = jnp.sum(
        jnp.where(own_match, route_weights.astype(jnp.float32)[:, :, None], 0.0), axis=1
    )
    mixed_out = jnp.sum(jnp.transpose(mix_weight)[:, :, None] * got_out.astype(jnp.float32), axis=0)
    input_total = jnp.sum(got_in.astype(jnp.float32), axis=0)
    return (
        mixed_out.astype(jnp.bfloat16),
        input_total.astype(jnp.bfloat16),
        grad_gate[None],
        grad_up[None],
        grad_down[None],
    )


CORE, FAR = 1, (2, 4, 6)


def from_xor(value, mask, devices):
    return lax.ppermute(value, AXES, [(i, i ^ mask) for i in range(devices)])


def kernel_call(body, out_shape, cost, *operands, scratch=(), hbm=()):
    vmem, smem = pl.BlockSpec(memory_space=pltpu.VMEM), pl.BlockSpec(memory_space=pltpu.SMEM)
    stay = pl.BlockSpec(memory_space=pltpu.HBM)
    specs = [stay if i in hbm else smem if o.ndim == 1 else vmem for i, o in enumerate(operands)]
    operands = [
        pltpu.with_memory_space_constraint(o, pltpu.HBM) if i in hbm else o
        for i, o in enumerate(operands)
    ]
    return pl.pallas_call(
        body,
        out_shape=out_shape,
        in_specs=specs,
        out_specs=jax.tree.map(lambda _: vmem, out_shape),
        scratch_shapes=scratch,
        compiler_params=pltpu.CompilerParams(vmem_limit_bytes=16 << 20),
        cost_estimate=pl.CostEstimate(flops=cost, bytes_accessed=4 << 20, transcendentals=0),
    )(*operands)


def copy_all(pairs, sems):
    copies = [pltpu.make_async_copy(src, dst, sems.at[i]) for i, (src, dst) in enumerate(pairs)]
    for copy in copies:
        copy.start()
    for copy in copies:
        copy.wait()


def load_body(*refs):
    count = len(refs) // 2
    copy_all(list(zip(refs[:count], refs[count:-1])), refs[-1])


def pack_body(x_ref, dy_ref, ids_ref, w_ref, expert_ref, msg_ref, mine_ref, *scratch):
    x_buf, dy_buf, ids_buf, w_buf, sems = scratch
    rows, width = x_ref.shape
    top = ids_ref.shape[0]
    lanes = msg_ref.shape[1] - 2 * width
    copy_all([(x_ref, x_buf), (dy_ref, dy_buf), (ids_ref, ids_buf), (w_ref, w_buf)], sems)
    msg_ref[:, :width] = x_buf[...]
    msg_ref[:, width : 2 * width] = dy_buf[...]
    diagonal = lax.broadcasted_iota(jnp.int32, (rows, rows), 0) == lax.broadcasted_iota(
        jnp.int32, (rows, rows), 1
    )
    expert = lax.broadcasted_iota(jnp.int32, (rows, lanes), 1)
    top_weights = w_buf[...].astype(jnp.float32)
    route = jnp.zeros((rows, lanes), jnp.float32)
    for k in range(top):
        named = jnp.sum(jnp.where(diagonal, ids_buf[k : k + 1, :], 0), axis=1, keepdims=True)
        weight = jnp.sum(jnp.where(diagonal, top_weights[k : k + 1, :], 0.0), axis=1, keepdims=True)
        route = route + jnp.where(expert == named, weight, 0.0)
    msg_ref[:, 2 * width :] = route.astype(jnp.bfloat16)
    lane = lax.broadcasted_iota(jnp.int32, mine_ref.shape, 1)
    mine_ref[...] = jnp.where(lane == expert_ref[0], 1.0, 0.0)


def places(pieces):
    start = 0
    for piece in pieces:
        yield slice(start, start + piece.shape[0]), piece
        start += piece.shape[0]


def cotangent_places(pieces):
    rows = pieces[0].shape[0] // 2
    for i, piece in enumerate(pieces):
        for k in range(2):
            at = i // 2 * 4 + (2 * k if i % 2 == 0 else 2 * k + 1)
            yield slice(at * rows, (at + 1) * rows), piece, slice(k * rows, (k + 1) * rows)


def stack_body(*refs):
    for here, piece in places(refs[:-1]):
        refs[-1][here, :] = piece[...]


def forward_body(count, *refs):
    pieces, (wg_ref, wu_ref, x_ref, hidden_ref, gate_ref, up_ref) = refs[:count], refs[count:]
    for here, piece in places(pieces):
        x_ref[here, :] = piece[...]
    x = x_ref[...]
    gate_pre = contract_rows(x, wg_ref[0])
    up_pre = contract_rows(x, wu_ref[0])
    gate_sig = 1.0 / (1.0 + jnp.exp(-gate_pre))
    silu_gate = gate_pre * gate_sig
    hidden_ref[...] = silu_gate * up_pre
    gate_ref[...] = up_pre * (gate_sig * (1.0 + gate_pre * (1.0 - gate_sig)))
    up_ref[...] = silu_gate


def corner_body(own_ref, came_ref, out_ref, into_ref):
    rows, width = out_ref.shape
    for side, ref in enumerate((out_ref, into_ref)):
        at = slice(side * width, (side + 1) * width)
        ref[...] = (own_ref[-rows:, at] + came_ref[:, at].astype(jnp.float32)).astype(jnp.bfloat16)


def most_body(own_ref, came_ref, *outs):
    rows, width = outs[0].shape
    for i, ref in enumerate(outs):
        here = (slice(i % 3 * rows, (i % 3 + 1) * rows), slice(i // 3 * width, (i // 3 + 1) * width))
        ref[...] = (own_ref[here] + came_ref[here].astype(jnp.float32)).astype(ref.dtype)


def backward_body(count, *refs):
    pieces, rest = refs[:count], refs[count:]
    hidden_ref, gate_ref, up_ref, mine_ref, wg_ref, wu_ref, wd_ref = rest[:7]
    dy_ref, scaled_ref, gate_act_ref, up_act_ref, own_ref, most_ref, corner_ref, weight_ref = rest[7:]
    width = dy_ref.shape[1]
    for here, piece, there in cotangent_places(pieces):
        dy_ref[here, :] = piece[there, :width]
        route = piece[there, width:].astype(jnp.float32) * mine_ref[:1, :]
        weight = jnp.sum(route, axis=1, keepdims=True)
        weight_ref[here, :] = jnp.broadcast_to(weight, (route.shape[0], weight_ref.shape[1]))
    weight = weight_ref[:, :1]
    scaled_ref[...] = (weight * hidden_ref[...]).astype(jnp.bfloat16)
    hidden_grad = weight * contract_rows(dy_ref[...], wd_ref[0])
    gate_act_ref[...] = (hidden_grad * gate_ref[...]).astype(jnp.bfloat16)
    up_act_ref[...] = (hidden_grad * up_ref[...]).astype(jnp.bfloat16)
    out = jnp.dot(scaled_ref[...], wd_ref[0], preferred_element_type=jnp.float32)
    into = jnp.dot(gate_act_ref[...], wg_ref[0], preferred_element_type=jnp.float32) + jnp.dot(
        up_act_ref[...], wu_ref[0], preferred_element_type=jnp.float32
    )
    half, most = own_ref.shape[0], most_ref.shape[0]
    for side, total in enumerate((out, into)):
        at = slice(side * width, (side + 1) * width)
        own_ref[:, at] = total[:half, :]
        corner_ref[:, at] = total[half + most :, :].astype(jnp.bfloat16)
        most_ref[:, at] = total[half : half + most, :].astype(jnp.bfloat16)


def turn_body(here_ref, came_ref, to_ref):
    to_ref[...] = (here_ref[...] + came_ref[...].astype(jnp.float32)).astype(jnp.bfloat16)


def deal_body(*refs):
    parts, outs = refs[:6], refs[6:]
    width, rows = parts[0].shape[1], outs[0].shape[0]
    for side in range(2):
        at = slice(side * width, (side + 1) * width)
        here = parts[3 * side : 3 * side + 3]
        total = here[0][...]
        for part in here[1:]:
            total = total + part[...].astype(jnp.float32)
        for i, ref in enumerate(outs):
            ref[:, at] = total[i * rows : (i + 1) * rows, :].astype(ref.dtype)


def end_body(own_ref, *refs):
    parts, (out_ref, into_ref) = refs[:-2], refs[-2:]
    total = own_ref[...]
    for part in parts:
        total = total + part[...].astype(jnp.float32)
    width = out_ref.shape[1]
    out_ref[...] = total[:, :width].astype(jnp.bfloat16)
    into_ref[...] = total[:, width:].astype(jnp.bfloat16)


def grad_body(rows_ref, *refs):
    acts, grads = refs[: len(refs) // 2], refs[len(refs) // 2 :]
    for act_ref, ref in zip(acts, grads):
        ref[0] = contract_first(act_ref[...], rows_ref[...]).astype(jnp.bfloat16)


def dense(tokens, expert_ids, route_weights, out_grad, gate_weight, up_weight, down_weight):
    experts = lax.axis_size("expert")
    devices = lax.axis_size("dp") * experts
    expert = lax.axis_index("expert").astype(jnp.int32).reshape(1)
    rows, width = tokens.shape
    ff = gate_weight.shape[1]
    near = tuple(k << 3 for k in range(1, devices >> 3))
    block_rows = rows * (len(near) + 1)
    bf16, f32 = jnp.bfloat16, jnp.float32
    columns = 2 * width + experts + -experts % 128
    unit = 2 * block_rows * ff * width

    def shape(*dims, dtype=bf16):
        return jax.ShapeDtypeStruct(dims, dtype)

    def passed(value, mask):
        return from_xor(value, mask, devices)

    message, mine = kernel_call(
        pack_body,
        (shape(rows, columns), shape(8, columns - 2 * width, dtype=f32)),
        0,
        tokens,
        out_grad,
        expert_ids.T,
        route_weights.T,
        expert,
        scratch=[
            pltpu.VMEM((rows, width), bf16),
            pltpu.VMEM((rows, width), bf16),
            pltpu.VMEM(expert_ids.shape[::-1], jnp.int32),
            pltpu.VMEM(route_weights.shape[::-1], bf16),
            pltpu.SemaphoreType.DMA((4,)),
        ],
        hbm=(0, 1, 2, 3),
    )
    weights = kernel_call(
        load_body,
        (shape(*gate_weight.shape),) * 3,
        0,
        gate_weight,
        up_weight,
        down_weight,
        scratch=[pltpu.SemaphoreType.DMA((3,))],
        hbm=(0, 1, 2),
    )
    arrived = [message] + [passed(message, m) for m in near]
    block_x = jnp.concatenate([piece[:, :width] for piece in arrived], axis=0)
    block_dy = jnp.concatenate([piece[:, width:] for piece in arrived], axis=0)
    block_x, block_dy, *weights = lax.optimization_barrier((block_x, block_dy, *weights))
    w_gate, w_up, w_down = weights

    first, second, _ = FAR
    second_x, first_dy = passed(block_x, second), passed(block_dy, first)
    second_dy, first_x = passed(block_dy, second), passed(block_x, first)
    corner_x, corner_dy = passed(second_x, first), passed(first_dy, second)
    half = (len(FAR) + 1) * block_rows

    def both_cores(*pairs):
        own = [
            kernel_call(stack_body, shape(2 * block_rows, pair[0].shape[1]), 0, *pair)
            for pair in pairs
        ]
        return own + [passed(pair, CORE) for pair in own]

    x_pieces = both_cores((block_x, first_x), (second_x, corner_x))
    early_dy, late_dy, other_early, other_late = both_cores(
        (block_dy, second_dy), (first_dy, corner_dy)
    )
    x_pieces[2], other_early = lax.optimization_barrier((x_pieces[2], other_early))
    dy_pieces = [early_dy, late_dy, other_early, other_late]
    all_x, hidden, gate_part, up_part = kernel_call(
        functools.partial(forward_body, len(x_pieces)),
        (shape(2 * half, width),) + (shape(2 * half, ff, dtype=f32),) * 3,
        16 * unit,
        *x_pieces,
        w_gate,
        w_up,
    )
    all_dy, scaled, gate_act, up_act, own, message, corner_message = kernel_call(
        functools.partial(backward_body, len(dy_pieces)),
        (
            shape(2 * half, width),
            *(shape(2 * half, ff),) * 3,
            shape(half, 2 * width, dtype=f32),
            shape(half - block_rows, 2 * width),
            shape(block_rows, 2 * width),
        ),
        24 * unit,
        *dy_pieces,
        hidden,
        gate_part,
        up_part,
        mine,
        *weights,
        scratch=[pltpu.VMEM((2 * half, columns - 2 * width), f32)],
    )
    corner_came = passed(corner_message, CORE)
    corner_came, message = lax.optimization_barrier((corner_came, message))
    most_came = passed(message, CORE)

    piece, full = shape(block_rows, width), shape(block_rows, width, dtype=f32)
    out_corner, into_corner = kernel_call(corner_body, (piece, piece), 0, own, corner_came)
    out_here, out_first, out_second, into_here, into_first, into_second = kernel_call(
        most_body, (full, full, piece, full, piece, full), 0, own, most_came
    )
    out_turn, into_turn = passed(out_corner, second), passed(into_corner, first)
    out_second, into_first = passed(out_second, second), passed(into_first, first)
    scaled, out_second, into_first = lax.optimization_barrier((scaled, out_second, into_first))
    out_first = passed(kernel_call(turn_body, piece, 0, out_first, out_turn), first)
    into_second = passed(kernel_call(turn_body, piece, 0, into_second, into_turn), second)
    into_here, scaled, gate_act, up_act = lax.optimization_barrier(
        (into_here, scaled, gate_act, up_act)
    )
    grad_down = kernel_call(grad_body, shape(*down_weight.shape), 8 * unit, all_dy, scaled)
    into_here, grad_down = lax.optimization_barrier((into_here, grad_down))
    mine_sum, *away = kernel_call(
        deal_body,
        (shape(rows, 2 * width, dtype=f32),) + (shape(rows, 2 * width),) * len(near),
        0,
        out_here,
        out_second,
        out_first,
        into_here,
        into_first,
        into_second,
    )
    mine_sum, gate_act, up_act = lax.optimization_barrier((mine_sum, gate_act, up_act))
    grad_gate, grad_up = kernel_call(
        grad_body, (shape(*gate_weight.shape),) * 2, 16 * unit, all_x, gate_act, up_act
    )
    mixed, input_grad = kernel_call(
        end_body,
        (shape(rows, width),) * 2,
        0,
        mine_sum,
        *[passed(piece, m) for m, piece in reversed(list(zip(near, away)))],
    )
    return mixed, input_grad, grad_gate, grad_up, grad_down


def shards(tokens, *others):
    experts = lax.axis_size("expert")
    devices = lax.axis_size("dp") * experts
    whole_group = tokens.shape[0] * experts <= ROW_CAP
    if whole_group and devices >= 16 and devices & (devices - 1) == 0:
        return dense(tokens, *others)
    return slotted(tokens, *others)


def solution(mesh):
    return jax.shard_map(
        shards,
        mesh=mesh,
        in_specs=(
            P(("dp", "expert"), None),
            P(("dp", "expert"), None),
            P(("dp", "expert"), None),
            P(("dp", "expert"), None),
            P("expert", "dp", None),
            P("expert", "dp", None),
            P("expert", "dp", None),
        ),
        out_specs=(
            P(("dp", "expert"), None),
            P(("dp", "expert"), None),
            P("expert", "dp", None),
            P("expert", "dp", None),
            P("expert", "dp", None),
        ),
        check_vma=False,
    )
```

```python
import functools

import jax
import jax.numpy as jnp
from jax import lax
from jax.experimental import pallas as pl
from jax.experimental.pallas import tpu as pltpu
from jax.sharding import PartitionSpec as P

ROW_CAP = 16
AXES = ("dp", "expert")


def contract_rows(left, right):
    return lax.dot_general(
        left, right, (((1,), (1,)), ((), ())), preferred_element_type=jnp.float32
    )


def contract_first(left, right):
    return lax.dot_general(
        left, right, (((0,), (0,)), ((), ())), preferred_element_type=jnp.float32
    )


def slotted(tokens, expert_ids, route_weights, out_grad, gate_weight, up_weight, down_weight):
    expert = lax.axis_index("expert")
    width = tokens.shape[1]
    local_tokens = tokens.shape[0]
    group_x, group_dy, group_w = (
        lax.all_gather(tokens, "expert", axis=0, tiled=True),
        lax.all_gather(out_grad, "expert", axis=0, tiled=True),
        lax.all_gather(route_weights, "expert", axis=0, tiled=True),
    )
    group_ids = lax.all_gather(expert_ids, "expert", axis=0, tiled=True)
    matches = group_ids == expert
    routed = jnp.any(matches, axis=1)
    weight = jnp.sum(jnp.where(matches, group_w.astype(jnp.float32), 0.0), axis=1)
    slot_rank = jnp.cumsum(routed.astype(jnp.int32)) - 1
    slot_index = jnp.arange(ROW_CAP, dtype=jnp.int32)
    picker = ((slot_rank[None, :] == slot_index[:, None]) & routed[None, :]).astype(jnp.bfloat16)
    slot_x = jnp.dot(picker, group_x, preferred_element_type=jnp.float32).astype(jnp.bfloat16)
    scaled = (weight[:, None] * group_dy.astype(jnp.float32)).astype(jnp.bfloat16)
    slot_dy = jnp.dot(picker, scaled, preferred_element_type=jnp.float32).astype(jnp.bfloat16)
    w_gate = gate_weight[0]
    w_up = up_weight[0]
    w_down = down_weight[0]
    all_x = lax.all_gather(slot_x, "dp", axis=0, tiled=True)
    gate_pre = contract_rows(w_gate, all_x)
    up_pre = contract_rows(w_up, all_x)
    gate_sig = jax.nn.sigmoid(gate_pre)
    silu_gate = gate_pre * gate_sig
    hidden = (silu_gate * up_pre).astype(jnp.bfloat16)
    expert_out = lax.psum_scatter(
        contract_first(hidden, w_down).astype(jnp.bfloat16), "dp", scatter_dimension=0, tiled=True
    )
    all_dy = lax.all_gather(slot_dy, "dp", axis=0, tiled=True)
    hidden_grad = contract_rows(w_down, all_dy)
    silu_slope = gate_sig * (1.0 + gate_pre * (1.0 - gate_sig))
    gate_act = (hidden_grad * up_pre * silu_slope).astype(jnp.bfloat16)
    up_act = (hidden_grad * silu_gate).astype(jnp.bfloat16)
    grad_down = jnp.dot(hidden, all_dy, preferred_element_type=jnp.float32).astype(jnp.bfloat16)
    grad_gate = jnp.dot(gate_act, all_x, preferred_element_type=jnp.float32).astype(jnp.bfloat16)
    grad_up = jnp.dot(up_act, all_x, preferred_element_type=jnp.float32).astype(jnp.bfloat16)
    expert_in = lax.psum_scatter(
        (contract_first(gate_act, w_gate) + contract_first(up_act, w_up)).astype(jnp.bfloat16),
        "dp",
        scatter_dimension=0,
        tiled=True,
    )
    back_out = contract_first(picker, expert_out).astype(jnp.bfloat16)
    back_in = contract_first(picker, expert_in).astype(jnp.bfloat16)
    got_out, got_in = (
        lax.all_to_all(back_out, "expert", split_axis=0, concat_axis=0, tiled=True),
        lax.all_to_all(back_in, "expert", split_axis=0, concat_axis=0, tiled=True),
    )
    expert_count = lax.axis_size("expert")
    got_out = got_out.reshape(expert_count, local_tokens, width)
    got_in = got_in.reshape(expert_count, local_tokens, width)
    expert_range = jnp.arange(expert_count, dtype=jnp.int32)
    own_match = expert_ids[:, :, None] == expert_range[None, None, :]
    mix_weight = jnp.sum(
        jnp.where(own_match, route_weights.astype(jnp.float32)[:, :, None], 0.0), axis=1
    )
    mixed_out = jnp.sum(jnp.transpose(mix_weight)[:, :, None] * got_out.astype(jnp.float32), axis=0)
    input_total = jnp.sum(got_in.astype(jnp.float32), axis=0)
    return (
        mixed_out.astype(jnp.bfloat16),
        input_total.astype(jnp.bfloat16),
        grad_gate[None],
        grad_up[None],
        grad_down[None],
    )


CORE, ASIDE, ACROSS = (1, 1), (4, 2), (2, 4)


def from_xor(value, masks, devices):
    return lax.ppermute(value, AXES, [(i, i ^ masks[i % 2]) for i in range(devices)])


def kernel_call(body, out_shape, cost, *operands, scratch=(), hbm=()):
    vmem, smem = pl.BlockSpec(memory_space=pltpu.VMEM), pl.BlockSpec(memory_space=pltpu.SMEM)
    stay = pl.BlockSpec(memory_space=pltpu.HBM)
    specs = [stay if i in hbm else smem if o.ndim == 1 else vmem for i, o in enumerate(operands)]
    operands = [
        pltpu.with_memory_space_constraint(o, pltpu.HBM) if i in hbm else o
        for i, o in enumerate(operands)
    ]
    return pl.pallas_call(
        body,
        out_shape=out_shape,
        in_specs=specs,
        out_specs=jax.tree.map(lambda _: vmem, out_shape),
        scratch_shapes=scratch,
        compiler_params=pltpu.CompilerParams(vmem_limit_bytes=16 << 20),
        cost_estimate=pl.CostEstimate(flops=cost, bytes_accessed=4 << 20, transcendentals=0),
    )(*operands)


def copy_all(pairs, sems):
    copies = [pltpu.make_async_copy(src, dst, sems.at[i]) for i, (src, dst) in enumerate(pairs)]
    for copy in copies:
        copy.start()
    for copy in copies:
        copy.wait()


def load_body(*refs):
    count = len(refs) // 2
    copy_all(list(zip(refs[:count], refs[count:-1])), refs[-1])


def pack_body(x_ref, dy_ref, ids_ref, w_ref, expert_ref, msg_ref, mine_ref, *scratch):
    x_buf, dy_buf, ids_buf, w_buf, sems = scratch
    rows, width = x_ref.shape
    top = ids_ref.shape[0]
    lanes = msg_ref.shape[1] - 2 * width
    copy_all([(x_ref, x_buf), (dy_ref, dy_buf), (ids_ref, ids_buf), (w_ref, w_buf)], sems)
    msg_ref[:, :width] = x_buf[...]
    msg_ref[:, width : 2 * width] = dy_buf[...]
    diagonal = lax.broadcasted_iota(jnp.int32, (rows, rows), 0) == lax.broadcasted_iota(
        jnp.int32, (rows, rows), 1
    )
    expert = lax.broadcasted_iota(jnp.int32, (rows, lanes), 1)
    top_weights = w_buf[...].astype(jnp.float32)
    route = jnp.zeros((rows, lanes), jnp.float32)
    for k in range(top):
        named = jnp.sum(jnp.where(diagonal, ids_buf[k : k + 1, :], 0), axis=1, keepdims=True)
        weight = jnp.sum(jnp.where(diagonal, top_weights[k : k + 1, :], 0.0), axis=1, keepdims=True)
        route = route + jnp.where(expert == named, weight, 0.0)
    msg_ref[:, 2 * width :] = route.astype(jnp.bfloat16)
    lane = lax.broadcasted_iota(jnp.int32, mine_ref.shape, 1)
    mine_ref[...] = jnp.where(lane == expert_ref[0], 1.0, 0.0)


def places(pieces):
    start = 0
    for piece in pieces:
        yield slice(start, start + piece.shape[0]), piece
        start += piece.shape[0]


def block_places(pieces, order):
    rows = pieces[0].shape[0] // 2
    for i, piece in enumerate(pieces):
        for k in range(2):
            at = i // 2 * 4 + order[i % 2 * 2 + k]
            yield slice(at * rows, (at + 1) * rows), piece, slice(k * rows, (k + 1) * rows)


def stack_body(*refs):
    for here, piece in places(refs[:-1]):
        refs[-1][here, :] = piece[...]


def forward_body(count, *refs):
    pieces, (wg_ref, wu_ref, x_ref, hidden_ref, gate_ref, up_ref) = refs[:count], refs[count:]
    for here, piece, there in block_places(pieces, (0, 1, 2, 3)):
        x_ref[here, :] = piece[there, :]
    x = x_ref[...]
    gate_pre = contract_rows(x, wg_ref[0])
    up_pre = contract_rows(x, wu_ref[0])
    gate_sig = 1.0 / (1.0 + jnp.exp(-gate_pre))
    silu_gate = gate_pre * gate_sig
    hidden_ref[...] = silu_gate * up_pre
    gate_ref[...] = up_pre * (gate_sig * (1.0 + gate_pre * (1.0 - gate_sig)))
    up_ref[...] = silu_gate


def corner_body(own_ref, came_ref, out_ref, into_ref):
    rows, width = out_ref.shape
    for side, ref in enumerate((out_ref, into_ref)):
        at = slice(side * width, (side + 1) * width)
        ref[...] = (own_ref[-rows:, at] + came_ref[:, at].astype(jnp.float32)).astype(jnp.bfloat16)


def most_body(own_ref, came_ref, here_ref, aside_ref, out_ref, into_ref):
    rows, width = out_ref.shape
    for at, ref in ((0, here_ref), (2, aside_ref)):
        at = slice(at * rows, (at + 1) * rows)
        ref[...] = (own_ref[at, :] + came_ref[at, :].astype(jnp.float32)).astype(ref.dtype)
    for side, ref in enumerate((out_ref, into_ref)):
        at = (slice(rows, 2 * rows), slice(side * width, (side + 1) * width))
        ref[...] = own_ref[at] + came_ref[at].astype(jnp.float32)


def backward_body(count, *refs):
    pieces, rest = refs[:count], refs[count:]
    hidden_ref, gate_ref, up_ref, mine_ref, wg_ref, wu_ref, wd_ref = rest[:7]
    dy_ref, scaled_ref, gate_act_ref, up_act_ref, own_ref, most_ref, corner_ref, weight_ref = rest[7:]
    width = dy_ref.shape[1]
    for here, piece, there in block_places(pieces, (0, 2, 1, 3)):
        dy_ref[here, :] = piece[there, :width]
        route = piece[there, width:].astype(jnp.float32) * mine_ref[:1, :]
        weight = jnp.sum(route, axis=1, keepdims=True)
        weight_ref[here, :] = jnp.broadcast_to(weight, (route.shape[0], weight_ref.shape[1]))
    weight = weight_ref[:, :1]
    scaled_ref[...] = (weight * hidden_ref[...]).astype(jnp.bfloat16)
    hidden_grad = weight * contract_rows(dy_ref[...], wd_ref[0])
    gate_act_ref[...] = (hidden_grad * gate_ref[...]).astype(jnp.bfloat16)
    up_act_ref[...] = (hidden_grad * up_ref[...]).astype(jnp.bfloat16)
    out = jnp.dot(scaled_ref[...], wd_ref[0], preferred_element_type=jnp.float32)
    into = jnp.dot(gate_act_ref[...], wg_ref[0], preferred_element_type=jnp.float32) + jnp.dot(
        up_act_ref[...], wu_ref[0], preferred_element_type=jnp.float32
    )
    half, most = own_ref.shape[0], most_ref.shape[0]
    for side, total in enumerate((out, into)):
        at = slice(side * width, (side + 1) * width)
        own_ref[:, at] = total[:half, :]
        corner_ref[:, at] = total[half + most :, :].astype(jnp.bfloat16)
        most_ref[:, at] = total[half : half + most, :].astype(jnp.bfloat16)


def turn_body(here_ref, came_ref, to_ref):
    to_ref[...] = (here_ref[...] + came_ref[...].astype(jnp.float32)).astype(jnp.bfloat16)


def deal_body(here_ref, aside_ref, *refs):
    parts, outs = refs[:2], refs[2:]
    width, rows = parts[0].shape[1], outs[0].shape[0]
    for side, part in enumerate(parts):
        at = slice(side * width, (side + 1) * width)
        total = here_ref[:, at] + aside_ref[:, at].astype(jnp.float32)
        total = total + part[...].astype(jnp.float32)
        for i, ref in enumerate(outs):
            ref[:, at] = total[i * rows : (i + 1) * rows, :].astype(ref.dtype)


def end_body(own_ref, *refs):
    parts, (out_ref, into_ref) = refs[:-2], refs[-2:]
    total = own_ref[...]
    for part in parts:
        total = total + part[...].astype(jnp.float32)
    width = out_ref.shape[1]
    out_ref[...] = total[:, :width].astype(jnp.bfloat16)
    into_ref[...] = total[:, width:].astype(jnp.bfloat16)


def grad_body(rows_ref, *refs):
    acts, grads = refs[: len(refs) // 2], refs[len(refs) // 2 :]
    for act_ref, ref in zip(acts, grads):
        ref[0] = contract_first(act_ref[...], rows_ref[...]).astype(jnp.bfloat16)


def dense(tokens, expert_ids, route_weights, out_grad, gate_weight, up_weight, down_weight):
    experts = lax.axis_size("expert")
    devices = lax.axis_size("dp") * experts
    expert = lax.axis_index("expert").astype(jnp.int32).reshape(1)
    rows, width = tokens.shape
    ff = gate_weight.shape[1]
    near = tuple((k << 3, k << 3) for k in range(1, devices >> 3))
    block_rows = rows * (len(near) + 1)
    bf16, f32 = jnp.bfloat16, jnp.float32
    columns = 2 * width + experts + -experts % 128
    unit = 2 * block_rows * ff * width

    def shape(*dims, dtype=bf16):
        return jax.ShapeDtypeStruct(dims, dtype)

    def passed(value, masks):
        return from_xor(value, masks, devices)

    message, mine = kernel_call(
        pack_body,
        (shape(rows, columns), shape(8, columns - 2 * width, dtype=f32)),
        0,
        tokens,
        out_grad,
        expert_ids.T,
        route_weights.T,
        expert,
        scratch=[
            pltpu.VMEM((rows, width), bf16),
            pltpu.VMEM((rows, width), bf16),
            pltpu.VMEM(expert_ids.shape[::-1], jnp.int32),
            pltpu.VMEM(route_weights.shape[::-1], bf16),
            pltpu.SemaphoreType.DMA((4,)),
        ],
        hbm=(0, 1, 2, 3),
    )
    weights = kernel_call(
        load_body,
        (shape(*gate_weight.shape),) * 3,
        0,
        gate_weight,
        up_weight,
        down_weight,
        scratch=[pltpu.SemaphoreType.DMA((3,))],
        hbm=(0, 1, 2),
    )
    arrived = [message] + [passed(message, m) for m in near]
    block_x = jnp.concatenate([piece[:, :width] for piece in arrived], axis=0)
    block_dy = jnp.concatenate([piece[:, width:] for piece in arrived], axis=0)
    block_x, block_dy, *weights = lax.optimization_barrier((block_x, block_dy, *weights))
    w_gate, w_up, w_down = weights

    aside_x, across_dy = passed(block_x, ASIDE), passed(block_dy, ACROSS)
    aside_dy, across_x = passed(block_dy, ASIDE), passed(block_x, ACROSS)
    corner_x, corner_dy = passed(aside_x, ACROSS), passed(across_dy, ASIDE)
    half = 4 * block_rows

    def both_cores(*pairs):
        own = [
            kernel_call(stack_body, shape(2 * block_rows, pair[0].shape[1]), 0, *pair)
            for pair in pairs
        ]
        return own + [passed(pair, CORE) for pair in own]

    x_pieces = both_cores((block_x, across_x), (aside_x, corner_x))
    dy_pieces = both_cores((block_dy, aside_dy), (across_dy, corner_dy))
    x_pieces[2], dy_pieces[2] = lax.optimization_barrier((x_pieces[2], dy_pieces[2]))
    all_x, hidden, gate_part, up_part = kernel_call(
        functools.partial(forward_body, len(x_pieces)),
        (shape(2 * half, width),) + (shape(2 * half, ff, dtype=f32),) * 3,
        16 * unit,
        *x_pieces,
        w_gate,
        w_up,
    )
    all_dy, scaled, gate_act, up_act, own, message, corner_message = kernel_call(
        functools.partial(backward_body, len(dy_pieces)),
        (
            shape(2 * half, width),
            *(shape(2 * half, ff),) * 3,
            shape(half, 2 * width, dtype=f32),
            shape(half - block_rows, 2 * width),
            shape(block_rows, 2 * width),
        ),
        24 * unit,
        *dy_pieces,
        hidden,
        gate_part,
        up_part,
        mine,
        *weights,
        scratch=[pltpu.VMEM((2 * half, columns - 2 * width), f32)],
    )
    corner_came = passed(corner_message, CORE)
    corner_came, message = lax.optimization_barrier((corner_came, message))
    most_came = passed(message, CORE)

    piece, full = shape(block_rows, width), shape(block_rows, width, dtype=f32)
    out_corner, into_corner = kernel_call(corner_body, (piece, piece), 0, own, corner_came)
    here, aside, out_across, into_across = kernel_call(
        most_body,
        (shape(block_rows, 2 * width, dtype=f32), shape(block_rows, 2 * width), full, full),
        0,
        own,
        most_came,
    )
    out_turn, into_turn = passed(out_corner, ASIDE), passed(into_corner, ASIDE)
    aside = passed(aside, ASIDE)
    out_across = passed(kernel_call(turn_body, piece, 0, out_across, out_turn), ACROSS)
    into_across = passed(kernel_call(turn_body, piece, 0, into_across, into_turn), ACROSS)
    here, scaled, gate_act, up_act = lax.optimization_barrier((here, scaled, gate_act, up_act))
    grad_gate, grad_up = kernel_call(
        grad_body, (shape(*gate_weight.shape),) * 2, 16 * unit, all_x, gate_act, up_act
    )
    here, grad_gate, grad_up = lax.optimization_barrier((here, grad_gate, grad_up))
    mine_sum, *away = kernel_call(
        deal_body,
        (shape(rows, 2 * width, dtype=f32),) + (shape(rows, 2 * width),) * len(near),
        0,
        here,
        aside,
        out_across,
        into_across,
    )
    mine_sum, scaled = lax.optimization_barrier((mine_sum, scaled))
    grad_down = kernel_call(grad_body, shape(*down_weight.shape), 8 * unit, all_dy, scaled)
    mixed, input_grad = kernel_call(
        end_body,
        (shape(rows, width),) * 2,
        0,
        mine_sum,
        *[passed(piece, m) for m, piece in reversed(list(zip(near, away)))],
    )
    return mixed, input_grad, grad_gate, grad_up, grad_down


def shards(tokens, *others):
    experts = lax.axis_size("expert")
    devices = lax.axis_size("dp") * experts
    whole_group = tokens.shape[0] * experts <= ROW_CAP
    if whole_group and devices >= 16 and devices & (devices - 1) == 0:
        return dense(tokens, *others)
    return slotted(tokens, *others)


def solution(mesh):
    return jax.shard_map(
        shards,
        mesh=mesh,
        in_specs=(
            P(("dp", "expert"), None),
            P(("dp", "expert"), None),
            P(("dp", "expert"), None),
            P(("dp", "expert"), None),
            P("expert", "dp", None),
            P("expert", "dp", None),
            P("expert", "dp", None),
        ),
        out_specs=(
            P(("dp", "expert"), None),
            P(("dp", "expert"), None),
            P("expert", "dp", None),
            P("expert", "dp", None),
            P("expert", "dp", None),
        ),
        check_vma=False,
    )
```

```python
import functools

import jax
import jax.numpy as jnp
from jax import lax
from jax.experimental import pallas as pl
from jax.experimental.pallas import tpu as pltpu
from jax.sharding import PartitionSpec as P

ROW_CAP = 16
AXES = ("dp", "expert")


def contract_rows(left, right):
    return lax.dot_general(
        left, right, (((1,), (1,)), ((), ())), preferred_element_type=jnp.float32
    )


def contract_first(left, right):
    return lax.dot_general(
        left, right, (((0,), (0,)), ((), ())), preferred_element_type=jnp.float32
    )


def slotted(tokens, expert_ids, route_weights, out_grad, gate_weight, up_weight, down_weight):
    expert = lax.axis_index("expert")
    width = tokens.shape[1]
    local_tokens = tokens.shape[0]
    group_x, group_dy, group_w = (
        lax.all_gather(tokens, "expert", axis=0, tiled=True),
        lax.all_gather(out_grad, "expert", axis=0, tiled=True),
        lax.all_gather(route_weights, "expert", axis=0, tiled=True),
    )
    group_ids = lax.all_gather(expert_ids, "expert", axis=0, tiled=True)
    matches = group_ids == expert
    routed = jnp.any(matches, axis=1)
    weight = jnp.sum(jnp.where(matches, group_w.astype(jnp.float32), 0.0), axis=1)
    slot_rank = jnp.cumsum(routed.astype(jnp.int32)) - 1
    slot_index = jnp.arange(ROW_CAP, dtype=jnp.int32)
    picker = ((slot_rank[None, :] == slot_index[:, None]) & routed[None, :]).astype(jnp.bfloat16)
    slot_x = jnp.dot(picker, group_x, preferred_element_type=jnp.float32).astype(jnp.bfloat16)
    scaled = (weight[:, None] * group_dy.astype(jnp.float32)).astype(jnp.bfloat16)
    slot_dy = jnp.dot(picker, scaled, preferred_element_type=jnp.float32).astype(jnp.bfloat16)
    w_gate = gate_weight[0]
    w_up = up_weight[0]
    w_down = down_weight[0]
    all_x = lax.all_gather(slot_x, "dp", axis=0, tiled=True)
    gate_pre = contract_rows(w_gate, all_x)
    up_pre = contract_rows(w_up, all_x)
    gate_sig = jax.nn.sigmoid(gate_pre)
    silu_gate = gate_pre * gate_sig
    hidden = (silu_gate * up_pre).astype(jnp.bfloat16)
    expert_out = lax.psum_scatter(
        contract_first(hidden, w_down).astype(jnp.bfloat16), "dp", scatter_dimension=0, tiled=True
    )
    all_dy = lax.all_gather(slot_dy, "dp", axis=0, tiled=True)
    hidden_grad = contract_rows(w_down, all_dy)
    silu_slope = gate_sig * (1.0 + gate_pre * (1.0 - gate_sig))
    gate_act = (hidden_grad * up_pre * silu_slope).astype(jnp.bfloat16)
    up_act = (hidden_grad * silu_gate).astype(jnp.bfloat16)
    grad_down = jnp.dot(hidden, all_dy, preferred_element_type=jnp.float32).astype(jnp.bfloat16)
    grad_gate = jnp.dot(gate_act, all_x, preferred_element_type=jnp.float32).astype(jnp.bfloat16)
    grad_up = jnp.dot(up_act, all_x, preferred_element_type=jnp.float32).astype(jnp.bfloat16)
    expert_in = lax.psum_scatter(
        (contract_first(gate_act, w_gate) + contract_first(up_act, w_up)).astype(jnp.bfloat16),
        "dp",
        scatter_dimension=0,
        tiled=True,
    )
    back_out = contract_first(picker, expert_out).astype(jnp.bfloat16)
    back_in = contract_first(picker, expert_in).astype(jnp.bfloat16)
    got_out, got_in = (
        lax.all_to_all(back_out, "expert", split_axis=0, concat_axis=0, tiled=True),
        lax.all_to_all(back_in, "expert", split_axis=0, concat_axis=0, tiled=True),
    )
    expert_count = lax.axis_size("expert")
    got_out = got_out.reshape(expert_count, local_tokens, width)
    got_in = got_in.reshape(expert_count, local_tokens, width)
    expert_range = jnp.arange(expert_count, dtype=jnp.int32)
    own_match = expert_ids[:, :, None] == expert_range[None, None, :]
    mix_weight = jnp.sum(
        jnp.where(own_match, route_weights.astype(jnp.float32)[:, :, None], 0.0), axis=1
    )
    mixed_out = jnp.sum(jnp.transpose(mix_weight)[:, :, None] * got_out.astype(jnp.float32), axis=0)
    input_total = jnp.sum(got_in.astype(jnp.float32), axis=0)
    return (
        mixed_out.astype(jnp.bfloat16),
        input_total.astype(jnp.bfloat16),
        grad_gate[None],
        grad_up[None],
        grad_down[None],
    )


CORE, ASIDE, ACROSS = (1, 1), (4, 2), (2, 4)


def from_xor(value, masks, devices):
    return lax.ppermute(value, AXES, [(i, i ^ masks[i % 2]) for i in range(devices)])


def kernel_call(body, out_shape, cost, *operands, scratch=(), hbm=(), blocks=False):
    vmem, smem = pl.BlockSpec(memory_space=pltpu.VMEM), pl.BlockSpec(memory_space=pltpu.SMEM)
    stay = pl.BlockSpec(memory_space=pltpu.HBM)
    specs = [stay if i in hbm else smem if o.ndim == 1 else vmem for i, o in enumerate(operands)]
    operands = [
        pltpu.with_memory_space_constraint(o, pltpu.HBM) if i in hbm else o
        for i, o in enumerate(operands)
    ]
    more = {}
    if blocks:
        specs = [
            smem if o.ndim == 1 else pl.BlockSpec(o.shape, lambda i: (0, 0)) for o in operands
        ]
        operands = [
            o if o.ndim == 1 else pltpu.with_memory_space_constraint(o, pltpu.HBM)
            for o in operands
        ]
        more = {"grid": (1,)}
    return pl.pallas_call(
        body,
        out_shape=out_shape,
        in_specs=specs,
        out_specs=jax.tree.map(lambda _: vmem, out_shape),
        scratch_shapes=scratch,
        compiler_params=pltpu.CompilerParams(vmem_limit_bytes=16 << 20),
        cost_estimate=pl.CostEstimate(flops=cost, bytes_accessed=4 << 20, transcendentals=0),
        **more,
    )(*operands)


def copy_all(pairs, sems):
    copies = [pltpu.make_async_copy(src, dst, sems.at[i]) for i, (src, dst) in enumerate(pairs)]
    for copy in copies:
        copy.start()
    for copy in copies:
        copy.wait()


def load_body(*refs):
    count = len(refs) // 2
    copy_all(list(zip(refs[:count], refs[count:-1])), refs[-1])


def pack_body(x_ref, dy_ref, ids_ref, w_ref, expert_ref, msg_ref, mine_ref):
    rows, width = x_ref.shape
    top = ids_ref.shape[0]
    lanes = msg_ref.shape[1] - 2 * width
    msg_ref[:, :width] = x_ref[...]
    msg_ref[:, width : 2 * width] = dy_ref[...]
    diagonal = lax.broadcasted_iota(jnp.int32, (rows, rows), 0) == lax.broadcasted_iota(
        jnp.int32, (rows, rows), 1
    )
    expert = lax.broadcasted_iota(jnp.int32, (rows, lanes), 1)
    top_weights = w_ref[...].astype(jnp.float32)
    route = jnp.zeros((rows, lanes), jnp.float32)
    for k in range(top):
        named = jnp.sum(jnp.where(diagonal, ids_ref[k : k + 1, :], 0), axis=1, keepdims=True)
        weight = jnp.sum(jnp.where(diagonal, top_weights[k : k + 1, :], 0.0), axis=1, keepdims=True)
        route = route + jnp.where(expert == named, weight, 0.0)
    msg_ref[:, 2 * width :] = route.astype(jnp.bfloat16)
    lane = lax.broadcasted_iota(jnp.int32, mine_ref.shape, 1)
    mine_ref[...] = jnp.where(lane == expert_ref[0], 1.0, 0.0)


def places(pieces):
    start = 0
    for piece in pieces:
        yield slice(start, start + piece.shape[0]), piece
        start += piece.shape[0]


def block_places(pieces, order):
    rows = pieces[0].shape[0] // 2
    for i, piece in enumerate(pieces):
        for k in range(2):
            at = i // 2 * 4 + order[i % 2 * 2 + k]
            yield slice(at * rows, (at + 1) * rows), piece, slice(k * rows, (k + 1) * rows)


def stack_body(*refs):
    for here, piece in places(refs[:-1]):
        refs[-1][here, :] = piece[...]


def forward_body(count, *refs):
    pieces, (wg_ref, wu_ref, x_ref, hidden_ref, gate_ref, up_ref) = refs[:count], refs[count:]
    for here, piece, there in block_places(pieces, (0, 1, 2, 3)):
        x_ref[here, :] = piece[there, :]
    x = x_ref[...]
    gate_pre = contract_rows(x, wg_ref[0])
    up_pre = contract_rows(x, wu_ref[0])
    gate_sig = 1.0 / (1.0 + jnp.exp(-gate_pre))
    silu_gate = gate_pre * gate_sig
    hidden_ref[...] = silu_gate * up_pre
    gate_ref[...] = up_pre * (gate_sig * (1.0 + gate_pre * (1.0 - gate_sig)))
    up_ref[...] = silu_gate


def corner_body(own_ref, came_ref, out_ref, into_ref):
    rows, width = out_ref.shape
    for side, ref in enumerate((out_ref, into_ref)):
        at = slice(side * width, (side + 1) * width)
        ref[...] = (own_ref[-rows:, at] + came_ref[:, at].astype(jnp.float32)).astype(jnp.bfloat16)


def most_body(own_ref, came_ref, here_ref, aside_ref, out_ref, into_ref):
    rows, width = out_ref.shape
    for at, ref in ((0, here_ref), (2, aside_ref)):
        at = slice(at * rows, (at + 1) * rows)
        ref[...] = (own_ref[at, :] + came_ref[at, :].astype(jnp.float32)).astype(ref.dtype)
    for side, ref in enumerate((out_ref, into_ref)):
        at = (slice(rows, 2 * rows), slice(side * width, (side + 1) * width))
        ref[...] = own_ref[at] + came_ref[at].astype(jnp.float32)


def backward_body(count, *refs):
    pieces, rest = refs[:count], refs[count:]
    hidden_ref, gate_ref, up_ref, mine_ref, wg_ref, wu_ref, wd_ref = rest[:7]
    dy_ref, scaled_ref, gate_act_ref, up_act_ref, own_ref, most_ref, corner_ref, weight_ref = rest[7:]
    width = dy_ref.shape[1]
    for here, piece, there in block_places(pieces, (0, 2, 1, 3)):
        dy_ref[here, :] = piece[there, :width]
        route = piece[there, width:].astype(jnp.float32) * mine_ref[:1, :]
        weight = jnp.sum(route, axis=1, keepdims=True)
        weight_ref[here, :] = jnp.broadcast_to(weight, (route.shape[0], weight_ref.shape[1]))
    weight = weight_ref[:, :1]
    scaled_ref[...] = (weight * hidden_ref[...]).astype(jnp.bfloat16)
    hidden_grad = weight * contract_rows(dy_ref[...], wd_ref[0])
    gate_act_ref[...] = (hidden_grad * gate_ref[...]).astype(jnp.bfloat16)
    up_act_ref[...] = (hidden_grad * up_ref[...]).astype(jnp.bfloat16)
    out = jnp.dot(scaled_ref[...], wd_ref[0], preferred_element_type=jnp.float32)
    into = jnp.dot(gate_act_ref[...], wg_ref[0], preferred_element_type=jnp.float32) + jnp.dot(
        up_act_ref[...], wu_ref[0], preferred_element_type=jnp.float32
    )
    half, most = own_ref.shape[0], most_ref.shape[0]
    for side, total in enumerate((out, into)):
        at = slice(side * width, (side + 1) * width)
        own_ref[:, at] = total[:half, :]
        corner_ref[:, at] = total[half + most :, :].astype(jnp.bfloat16)
        most_ref[:, at] = total[half : half + most, :].astype(jnp.bfloat16)


def turn_body(here_ref, came_ref, to_ref):
    to_ref[...] = (here_ref[...] + came_ref[...].astype(jnp.float32)).astype(jnp.bfloat16)


def deal_body(here_ref, aside_ref, *refs):
    parts, outs = refs[:2], refs[2:]
    width, rows = parts[0].shape[1], outs[0].shape[0]
    for side, part in enumerate(parts):
        at = slice(side * width, (side + 1) * width)
        total = here_ref[:, at] + aside_ref[:, at].astype(jnp.float32)
        total = total + part[...].astype(jnp.float32)
        for i, ref in enumerate(outs):
            ref[:, at] = total[i * rows : (i + 1) * rows, :].astype(ref.dtype)


def end_body(own_ref, *refs):
    parts, (out_ref, into_ref) = refs[:-2], refs[-2:]
    total = own_ref[...]
    for part in parts:
        total = total + part[...].astype(jnp.float32)
    width = out_ref.shape[1]
    out_ref[...] = total[:, :width].astype(jnp.bfloat16)
    into_ref[...] = total[:, width:].astype(jnp.bfloat16)


def grad_body(rows_ref, *refs):
    acts, grads = refs[: len(refs) // 2], refs[len(refs) // 2 :]
    for act_ref, ref in zip(acts, grads):
        ref[0] = contract_first(act_ref[...], rows_ref[...]).astype(jnp.bfloat16)


def dense(tokens, expert_ids, route_weights, out_grad, gate_weight, up_weight, down_weight):
    experts = lax.axis_size("expert")
    devices = lax.axis_size("dp") * experts
    expert = lax.axis_index("expert").astype(jnp.int32).reshape(1)
    rows, width = tokens.shape
    ff = gate_weight.shape[1]
    near = tuple((k << 3, k << 3) for k in range(1, devices >> 3))
    block_rows = rows * (len(near) + 1)
    bf16, f32 = jnp.bfloat16, jnp.float32
    columns = 2 * width + experts + -experts % 128
    unit = 2 * block_rows * ff * width

    def shape(*dims, dtype=bf16):
        return jax.ShapeDtypeStruct(dims, dtype)

    def passed(value, masks):
        return from_xor(value, masks, devices)

    message, mine = kernel_call(
        pack_body,
        (shape(rows, columns), shape(8, columns - 2 * width, dtype=f32)),
        0,
        tokens,
        out_grad,
        expert_ids.T,
        route_weights.T,
        expert,
        blocks=True,
    )
    weights = kernel_call(
        load_body,
        (shape(*gate_weight.shape),) * 3,
        0,
        gate_weight,
        up_weight,
        down_weight,
        scratch=[pltpu.SemaphoreType.DMA((3,))],
        hbm=(0, 1, 2),
    )
    arrived = [message] + [passed(message, m) for m in near]
    block_x = jnp.concatenate([piece[:, :width] for piece in arrived], axis=0)
    block_dy = jnp.concatenate([piece[:, width:] for piece in arrived], axis=0)
    block_x, block_dy, *weights = lax.optimization_barrier((block_x, block_dy, *weights))
    w_gate, w_up, w_down = weights

    aside_x, across_dy = passed(block_x, ASIDE), passed(block_dy, ACROSS)
    aside_dy, across_x = passed(block_dy, ASIDE), passed(block_x, ACROSS)
    corner_x, corner_dy = passed(aside_x, ACROSS), passed(across_dy, ASIDE)
    half = 4 * block_rows

    def both_cores(*pairs):
        own = [
            kernel_call(stack_body, shape(2 * block_rows, pair[0].shape[1]), 0, *pair)
            for pair in pairs
        ]
        return own + [passed(pair, CORE) for pair in own]

    x_pieces = both_cores((block_x, across_x), (aside_x, corner_x))
    dy_pieces = both_cores((block_dy, aside_dy), (across_dy, corner_dy))
    x_pieces[2], dy_pieces[2] = lax.optimization_barrier((x_pieces[2], dy_pieces[2]))
    all_x, hidden, gate_part, up_part = kernel_call(
        functools.partial(forward_body, len(x_pieces)),
        (shape(2 * half, width),) + (shape(2 * half, ff, dtype=f32),) * 3,
        16 * unit,
        *x_pieces,
        w_gate,
        w_up,
    )
    all_dy, scaled, gate_act, up_act, own, message, corner_message = kernel_call(
        functools.partial(backward_body, len(dy_pieces)),
        (
            shape(2 * half, width),
            *(shape(2 * half, ff),) * 3,
            shape(half, 2 * width, dtype=f32),
            shape(half - block_rows, 2 * width),
            shape(block_rows, 2 * width),
        ),
        24 * unit,
        *dy_pieces,
        hidden,
        gate_part,
        up_part,
        mine,
        *weights,
        scratch=[pltpu.VMEM((2 * half, columns - 2 * width), f32)],
    )
    corner_came = passed(corner_message, CORE)
    corner_came, message = lax.optimization_barrier((corner_came, message))
    most_came = passed(message, CORE)

    piece, full = shape(block_rows, width), shape(block_rows, width, dtype=f32)
    out_corner, into_corner = kernel_call(corner_body, (piece, piece), 0, own, corner_came)
    here, aside, out_across, into_across = kernel_call(
        most_body,
        (shape(block_rows, 2 * width, dtype=f32), shape(block_rows, 2 * width), full, full),
        0,
        own,
        most_came,
    )
    out_turn, into_turn = passed(out_corner, ASIDE), passed(into_corner, ASIDE)
    aside = passed(aside, ASIDE)
    out_across = passed(kernel_call(turn_body, piece, 0, out_across, out_turn), ACROSS)
    into_across = passed(kernel_call(turn_body, piece, 0, into_across, into_turn), ACROSS)
    here, scaled, gate_act, up_act = lax.optimization_barrier((here, scaled, gate_act, up_act))
    grad_gate, grad_up = kernel_call(
        grad_body, (shape(*gate_weight.shape),) * 2, 16 * unit, all_x, gate_act, up_act
    )
    here, grad_gate, grad_up = lax.optimization_barrier((here, grad_gate, grad_up))
    mine_sum, *away = kernel_call(
        deal_body,
        (shape(rows, 2 * width, dtype=f32),) + (shape(rows, 2 * width),) * len(near),
        0,
        here,
        aside,
        out_across,
        into_across,
    )
    mine_sum, scaled = lax.optimization_barrier((mine_sum, scaled))
    grad_down = kernel_call(grad_body, shape(*down_weight.shape), 8 * unit, all_dy, scaled)
    mixed, input_grad = kernel_call(
        end_body,
        (shape(rows, width),) * 2,
        0,
        mine_sum,
        *[passed(piece, m) for m, piece in reversed(list(zip(near, away)))],
    )
    return mixed, input_grad, grad_gate, grad_up, grad_down


def shards(tokens, *others):
    experts = lax.axis_size("expert")
    devices = lax.axis_size("dp") * experts
    whole_group = tokens.shape[0] * experts <= ROW_CAP
    if whole_group and devices >= 16 and devices & (devices - 1) == 0:
        return dense(tokens, *others)
    return slotted(tokens, *others)


def solution(mesh):
    return jax.shard_map(
        shards,
        mesh=mesh,
        in_specs=(
            P(("dp", "expert"), None),
            P(("dp", "expert"), None),
            P(("dp", "expert"), None),
            P(("dp", "expert"), None),
            P("expert", "dp", None),
            P("expert", "dp", None),
            P("expert", "dp", None),
        ),
        out_specs=(
            P(("dp", "expert"), None),
            P(("dp", "expert"), None),
            P("expert", "dp", None),
            P("expert", "dp", None),
            P("expert", "dp", None),
        ),
        check_vma=False,
    )
```

```python
import functools

import jax
import jax.numpy as jnp
from jax import lax
from jax.experimental import pallas as pl
from jax.experimental.pallas import tpu as pltpu
from jax.sharding import PartitionSpec as P

ROW_CAP = 16
AXES = ("dp", "expert")


def contract_rows(left, right):
    return lax.dot_general(
        left, right, (((1,), (1,)), ((), ())), preferred_element_type=jnp.float32
    )


def contract_first(left, right):
    return lax.dot_general(
        left, right, (((0,), (0,)), ((), ())), preferred_element_type=jnp.float32
    )


def slotted(tokens, expert_ids, route_weights, out_grad, gate_weight, up_weight, down_weight):
    expert = lax.axis_index("expert")
    width = tokens.shape[1]
    local_tokens = tokens.shape[0]
    group_x, group_dy, group_w = (
        lax.all_gather(tokens, "expert", axis=0, tiled=True),
        lax.all_gather(out_grad, "expert", axis=0, tiled=True),
        lax.all_gather(route_weights, "expert", axis=0, tiled=True),
    )
    group_ids = lax.all_gather(expert_ids, "expert", axis=0, tiled=True)
    matches = group_ids == expert
    routed = jnp.any(matches, axis=1)
    weight = jnp.sum(jnp.where(matches, group_w.astype(jnp.float32), 0.0), axis=1)
    slot_rank = jnp.cumsum(routed.astype(jnp.int32)) - 1
    slot_index = jnp.arange(ROW_CAP, dtype=jnp.int32)
    picker = ((slot_rank[None, :] == slot_index[:, None]) & routed[None, :]).astype(jnp.bfloat16)
    slot_x = jnp.dot(picker, group_x, preferred_element_type=jnp.float32).astype(jnp.bfloat16)
    scaled = (weight[:, None] * group_dy.astype(jnp.float32)).astype(jnp.bfloat16)
    slot_dy = jnp.dot(picker, scaled, preferred_element_type=jnp.float32).astype(jnp.bfloat16)
    w_gate = gate_weight[0]
    w_up = up_weight[0]
    w_down = down_weight[0]
    all_x = lax.all_gather(slot_x, "dp", axis=0, tiled=True)
    gate_pre = contract_rows(w_gate, all_x)
    up_pre = contract_rows(w_up, all_x)
    gate_sig = jax.nn.sigmoid(gate_pre)
    silu_gate = gate_pre * gate_sig
    hidden = (silu_gate * up_pre).astype(jnp.bfloat16)
    expert_out = lax.psum_scatter(
        contract_first(hidden, w_down).astype(jnp.bfloat16), "dp", scatter_dimension=0, tiled=True
    )
    all_dy = lax.all_gather(slot_dy, "dp", axis=0, tiled=True)
    hidden_grad = contract_rows(w_down, all_dy)
    silu_slope = gate_sig * (1.0 + gate_pre * (1.0 - gate_sig))
    gate_act = (hidden_grad * up_pre * silu_slope).astype(jnp.bfloat16)
    up_act = (hidden_grad * silu_gate).astype(jnp.bfloat16)
    grad_down = jnp.dot(hidden, all_dy, preferred_element_type=jnp.float32).astype(jnp.bfloat16)
    grad_gate = jnp.dot(gate_act, all_x, preferred_element_type=jnp.float32).astype(jnp.bfloat16)
    grad_up = jnp.dot(up_act, all_x, preferred_element_type=jnp.float32).astype(jnp.bfloat16)
    expert_in = lax.psum_scatter(
        (contract_first(gate_act, w_gate) + contract_first(up_act, w_up)).astype(jnp.bfloat16),
        "dp",
        scatter_dimension=0,
        tiled=True,
    )
    back_out = contract_first(picker, expert_out).astype(jnp.bfloat16)
    back_in = contract_first(picker, expert_in).astype(jnp.bfloat16)
    got_out, got_in = (
        lax.all_to_all(back_out, "expert", split_axis=0, concat_axis=0, tiled=True),
        lax.all_to_all(back_in, "expert", split_axis=0, concat_axis=0, tiled=True),
    )
    expert_count = lax.axis_size("expert")
    got_out = got_out.reshape(expert_count, local_tokens, width)
    got_in = got_in.reshape(expert_count, local_tokens, width)
    expert_range = jnp.arange(expert_count, dtype=jnp.int32)
    own_match = expert_ids[:, :, None] == expert_range[None, None, :]
    mix_weight = jnp.sum(
        jnp.where(own_match, route_weights.astype(jnp.float32)[:, :, None], 0.0), axis=1
    )
    mixed_out = jnp.sum(jnp.transpose(mix_weight)[:, :, None] * got_out.astype(jnp.float32), axis=0)
    input_total = jnp.sum(got_in.astype(jnp.float32), axis=0)
    return (
        mixed_out.astype(jnp.bfloat16),
        input_total.astype(jnp.bfloat16),
        grad_gate[None],
        grad_up[None],
        grad_down[None],
    )


CORE, ASIDE, ACROSS = (1, 1), (4, 2), (2, 4)


def from_xor(value, masks, devices):
    return lax.ppermute(value, AXES, [(i, i ^ masks[i % 2]) for i in range(devices)])


def kernel_call(body, out_shape, cost, *operands, scratch=(), hbm=(), blocks=False):
    vmem, smem = pl.BlockSpec(memory_space=pltpu.VMEM), pl.BlockSpec(memory_space=pltpu.SMEM)
    stay = pl.BlockSpec(memory_space=pltpu.HBM)
    specs = [stay if i in hbm else smem if o.ndim == 1 else vmem for i, o in enumerate(operands)]
    operands = [
        pltpu.with_memory_space_constraint(o, pltpu.HBM) if i in hbm else o
        for i, o in enumerate(operands)
    ]
    more = {}
    if blocks:
        specs = [
            smem if o.ndim == 1 else pl.BlockSpec(o.shape, lambda i: (0, 0)) for o in operands
        ]
        operands = [
            o if o.ndim == 1 else pltpu.with_memory_space_constraint(o, pltpu.HBM)
            for o in operands
        ]
        more = {"grid": (1,)}
    return pl.pallas_call(
        body,
        out_shape=out_shape,
        in_specs=specs,
        out_specs=jax.tree.map(lambda _: vmem, out_shape),
        scratch_shapes=scratch,
        compiler_params=pltpu.CompilerParams(vmem_limit_bytes=16 << 20),
        cost_estimate=pl.CostEstimate(flops=cost, bytes_accessed=4 << 20, transcendentals=0),
        **more,
    )(*operands)


def copy_all(pairs, sems):
    copies = [pltpu.make_async_copy(src, dst, sems.at[i]) for i, (src, dst) in enumerate(pairs)]
    for copy in copies:
        copy.start()
    for copy in copies:
        copy.wait()


def load_body(gate_ref, up_ref, down_ref, pair_ref, down_out_ref, sems):
    ff = gate_ref.shape[1]
    copy_all(
        [
            (gate_ref.at[0], pair_ref.at[pl.ds(0, ff)]),
            (up_ref.at[0], pair_ref.at[pl.ds(ff, ff)]),
            (down_ref.at[0], down_out_ref),
        ],
        sems,
    )


def pack_body(x_ref, dy_ref, ids_ref, w_ref, expert_ref, msg_ref, mine_ref):
    rows, width = x_ref.shape
    top = ids_ref.shape[0]
    lanes = msg_ref.shape[1] - 2 * width
    msg_ref[:, :width] = x_ref[...]
    msg_ref[:, width : 2 * width] = dy_ref[...]
    diagonal = lax.broadcasted_iota(jnp.int32, (rows, rows), 0) == lax.broadcasted_iota(
        jnp.int32, (rows, rows), 1
    )
    expert = lax.broadcasted_iota(jnp.int32, (rows, lanes), 1)
    top_weights = w_ref[...].astype(jnp.float32)
    route = jnp.zeros((rows, lanes), jnp.float32)
    for k in range(top):
        named = jnp.sum(jnp.where(diagonal, ids_ref[k : k + 1, :], 0), axis=1, keepdims=True)
        weight = jnp.sum(jnp.where(diagonal, top_weights[k : k + 1, :], 0.0), axis=1, keepdims=True)
        route = route + jnp.where(expert == named, weight, 0.0)
    msg_ref[:, 2 * width :] = route.astype(jnp.bfloat16)
    lane = lax.broadcasted_iota(jnp.int32, mine_ref.shape, 1)
    mine_ref[...] = jnp.where(lane == expert_ref[0], 1.0, 0.0)


def places(pieces):
    start = 0
    for piece in pieces:
        yield slice(start, start + piece.shape[0]), piece
        start += piece.shape[0]


def block_places(pieces, order):
    rows = pieces[0].shape[0] // 2
    for i, piece in enumerate(pieces):
        for k in range(2):
            at = i // 2 * 4 + order[i % 2 * 2 + k]
            yield slice(at * rows, (at + 1) * rows), piece, slice(k * rows, (k + 1) * rows)


def stack_body(*refs):
    for here, piece in places(refs[:-1]):
        refs[-1][here, :] = piece[...]


def forward_body(count, *refs):
    pieces, (pair_ref, x_ref, hidden_ref, gate_ref, up_ref) = refs[:count], refs[count:]
    for here, piece, there in block_places(pieces, (0, 1, 2, 3)):
        x_ref[here, :] = piece[there, :]
    x = x_ref[...]
    ff = gate_ref.shape[1]
    gate_pre = contract_rows(x, pair_ref[:ff, :])
    up_pre = contract_rows(x, pair_ref[ff:, :])
    gate_sig = 1.0 / (1.0 + jnp.exp(-gate_pre))
    silu_gate = gate_pre * gate_sig
    hidden_ref[...] = silu_gate * up_pre
    gate_ref[...] = up_pre * (gate_sig * (1.0 + gate_pre * (1.0 - gate_sig)))
    up_ref[...] = silu_gate


def corner_body(own_ref, came_ref, out_ref, into_ref):
    rows, width = out_ref.shape
    for side, ref in enumerate((out_ref, into_ref)):
        at = slice(side * width, (side + 1) * width)
        ref[...] = (own_ref[-rows:, at] + came_ref[:, at].astype(jnp.float32)).astype(jnp.bfloat16)


def most_body(own_ref, came_ref, here_ref, aside_ref, out_ref, into_ref):
    rows, width = out_ref.shape
    for at, ref in ((0, here_ref), (2, aside_ref)):
        at = slice(at * rows, (at + 1) * rows)
        ref[...] = (own_ref[at, :] + came_ref[at, :].astype(jnp.float32)).astype(ref.dtype)
    for side, ref in enumerate((out_ref, into_ref)):
        at = (slice(rows, 2 * rows), slice(side * width, (side + 1) * width))
        ref[...] = own_ref[at] + came_ref[at].astype(jnp.float32)


def backward_body(count, *refs):
    pieces, rest = refs[:count], refs[count:]
    hidden_ref, gate_ref, up_ref, mine_ref, pair_ref, wd_ref = rest[:6]
    dy_ref, scaled_ref, acts_ref, own_ref, most_ref, corner_ref, weight_ref = rest[6:]
    ff = wd_ref.shape[0]
    width = dy_ref.shape[1]
    for here, piece, there in block_places(pieces, (0, 2, 1, 3)):
        dy_ref[here, :] = piece[there, :width]
        route = piece[there, width:].astype(jnp.float32) * mine_ref[:1, :]
        weight = jnp.sum(route, axis=1, keepdims=True)
        weight_ref[here, :] = jnp.broadcast_to(weight, (route.shape[0], weight_ref.shape[1]))
    weight = weight_ref[:, :1]
    scaled_ref[...] = (weight * hidden_ref[...]).astype(jnp.bfloat16)
    hidden_grad = weight * contract_rows(dy_ref[...], wd_ref[...])
    acts_ref[:, :ff] = (hidden_grad * gate_ref[...]).astype(jnp.bfloat16)
    acts_ref[:, ff:] = (hidden_grad * up_ref[...]).astype(jnp.bfloat16)
    out = jnp.dot(scaled_ref[...], wd_ref[...], preferred_element_type=jnp.float32)
    into = jnp.dot(acts_ref[...], pair_ref[...], preferred_element_type=jnp.float32)
    half, most = own_ref.shape[0], most_ref.shape[0]
    for side, total in enumerate((out, into)):
        at = slice(side * width, (side + 1) * width)
        own_ref[:, at] = total[:half, :]
        corner_ref[:, at] = total[half + most :, :].astype(jnp.bfloat16)
        most_ref[:, at] = total[half : half + most, :].astype(jnp.bfloat16)


def turn_body(here_ref, came_ref, to_ref):
    to_ref[...] = (here_ref[...] + came_ref[...].astype(jnp.float32)).astype(jnp.bfloat16)


def deal_body(here_ref, aside_ref, *refs):
    parts, outs = refs[:2], refs[2:]
    width, rows = parts[0].shape[1], outs[0].shape[0]
    for side, part in enumerate(parts):
        at = slice(side * width, (side + 1) * width)
        total = here_ref[:, at] + aside_ref[:, at].astype(jnp.float32)
        total = total + part[...].astype(jnp.float32)
        for i, ref in enumerate(outs):
            ref[:, at] = total[i * rows : (i + 1) * rows, :].astype(ref.dtype)


def end_body(own_ref, *refs):
    parts, (out_ref, into_ref) = refs[:-2], refs[-2:]
    total = own_ref[...]
    for part in parts:
        total = total + part[...].astype(jnp.float32)
    width = out_ref.shape[1]
    out_ref[...] = total[:, :width].astype(jnp.bfloat16)
    into_ref[...] = total[:, width:].astype(jnp.bfloat16)


def grad_body(rows_ref, acts_ref, *grads):
    ff = grads[0].shape[1]
    for i, ref in enumerate(grads):
        acts = acts_ref[:, i * ff : (i + 1) * ff]
        ref[0] = contract_first(acts, rows_ref[...]).astype(jnp.bfloat16)


def dense(tokens, expert_ids, route_weights, out_grad, gate_weight, up_weight, down_weight):
    experts = lax.axis_size("expert")
    devices = lax.axis_size("dp") * experts
    expert = lax.axis_index("expert").astype(jnp.int32).reshape(1)
    rows, width = tokens.shape
    ff = gate_weight.shape[1]
    near = tuple((k << 3, k << 3) for k in range(1, devices >> 3))
    block_rows = rows * (len(near) + 1)
    bf16, f32 = jnp.bfloat16, jnp.float32
    columns = 2 * width + experts + -experts % 128
    unit = 2 * block_rows * ff * width

    def shape(*dims, dtype=bf16):
        return jax.ShapeDtypeStruct(dims, dtype)

    def passed(value, masks):
        return from_xor(value, masks, devices)

    message, mine = kernel_call(
        pack_body,
        (shape(rows, columns), shape(8, columns - 2 * width, dtype=f32)),
        0,
        tokens,
        out_grad,
        expert_ids.T,
        route_weights.T,
        expert,
        blocks=True,
    )
    weights = kernel_call(
        load_body,
        (shape(2 * ff, width), shape(ff, width)),
        0,
        gate_weight,
        up_weight,
        down_weight,
        scratch=[pltpu.SemaphoreType.DMA((3,))],
        hbm=(0, 1, 2),
    )
    arrived = [message] + [passed(message, m) for m in near]
    block_x = jnp.concatenate([piece[:, :width] for piece in arrived], axis=0)
    block_dy = jnp.concatenate([piece[:, width:] for piece in arrived], axis=0)
    block_dy, *weights = lax.optimization_barrier((block_dy, *weights))

    aside_x, across_dy = passed(block_x, ASIDE), passed(block_dy, ACROSS)
    aside_dy, across_x = passed(block_dy, ASIDE), passed(block_x, ACROSS)
    corner_x, corner_dy = passed(aside_x, ACROSS), passed(across_dy, ASIDE)
    half = 4 * block_rows

    def both_cores(*pairs):
        own = [
            kernel_call(stack_body, shape(2 * block_rows, pair[0].shape[1]), 0, *pair)
            for pair in pairs
        ]
        return own + [passed(pair, CORE) for pair in own]

    x_pieces = both_cores((block_x, across_x), (aside_x, corner_x))
    dy_pieces = both_cores((block_dy, aside_dy), (across_dy, corner_dy))
    x_pieces[2], dy_pieces[2] = lax.optimization_barrier((x_pieces[2], dy_pieces[2]))
    all_x, hidden, gate_part, up_part = kernel_call(
        functools.partial(forward_body, len(x_pieces)),
        (shape(2 * half, width),) + (shape(2 * half, ff, dtype=f32),) * 3,
        16 * unit,
        *x_pieces,
        weights[0],
    )
    all_dy, scaled, acts, own, message, corner_message = kernel_call(
        functools.partial(backward_body, len(dy_pieces)),
        (
            shape(2 * half, width),
            shape(2 * half, ff),
            shape(2 * half, 2 * ff),
            shape(half, 2 * width, dtype=f32),
            shape(half - block_rows, 2 * width),
            shape(block_rows, 2 * width),
        ),
        24 * unit,
        *dy_pieces,
        hidden,
        gate_part,
        up_part,
        mine,
        *weights,
        scratch=[pltpu.VMEM((2 * half, columns - 2 * width), f32)],
    )
    corner_came = passed(corner_message, CORE)
    corner_came, message = lax.optimization_barrier((corner_came, message))
    most_came = passed(message, CORE)

    piece, full = shape(block_rows, width), shape(block_rows, width, dtype=f32)
    out_corner, into_corner = kernel_call(corner_body, (piece, piece), 0, own, corner_came)
    here, aside, out_across, into_across = kernel_call(
        most_body,
        (shape(block_rows, 2 * width, dtype=f32), shape(block_rows, 2 * width), full, full),
        0,
        own,
        most_came,
    )
    out_turn, into_turn = passed(out_corner, ASIDE), passed(into_corner, ASIDE)
    aside = passed(aside, ASIDE)
    out_across = passed(kernel_call(turn_body, piece, 0, out_across, out_turn), ACROSS)
    into_across = passed(kernel_call(turn_body, piece, 0, into_across, into_turn), ACROSS)
    here, scaled, acts = lax.optimization_barrier((here, scaled, acts))
    grad_gate, grad_up = kernel_call(
        grad_body, (shape(*gate_weight.shape),) * 2, 16 * unit, all_x, acts
    )
    here, grad_gate, grad_up = lax.optimization_barrier((here, grad_gate, grad_up))
    mine_sum, *away = kernel_call(
        deal_body,
        (shape(rows, 2 * width, dtype=f32),) + (shape(rows, 2 * width),) * len(near),
        0,
        here,
        aside,
        out_across,
        into_across,
    )
    mine_sum, scaled = lax.optimization_barrier((mine_sum, scaled))
    grad_down = kernel_call(grad_body, shape(*down_weight.shape), 8 * unit, all_dy, scaled)
    mixed, input_grad = kernel_call(
        end_body,
        (shape(rows, width),) * 2,
        0,
        mine_sum,
        *[passed(piece, m) for m, piece in reversed(list(zip(near, away)))],
    )
    return mixed, input_grad, grad_gate, grad_up, grad_down


def shards(tokens, *others):
    experts = lax.axis_size("expert")
    devices = lax.axis_size("dp") * experts
    whole_group = tokens.shape[0] * experts <= ROW_CAP
    if whole_group and devices >= 16 and devices & (devices - 1) == 0:
        return dense(tokens, *others)
    return slotted(tokens, *others)


def solution(mesh):
    return jax.shard_map(
        shards,
        mesh=mesh,
        in_specs=(
            P(("dp", "expert"), None),
            P(("dp", "expert"), None),
            P(("dp", "expert"), None),
            P(("dp", "expert"), None),
            P("expert", "dp", None),
            P("expert", "dp", None),
            P("expert", "dp", None),
        ),
        out_specs=(
            P(("dp", "expert"), None),
            P(("dp", "expert"), None),
            P("expert", "dp", None),
            P("expert", "dp", None),
            P("expert", "dp", None),
        ),
        check_vma=False,
    )
```

```python
import functools

import jax
import jax.numpy as jnp
from jax import lax
from jax.experimental import pallas as pl
from jax.experimental.pallas import tpu as pltpu
from jax.sharding import PartitionSpec as P

ROW_CAP = 16
AXES = ("dp", "expert")


def contract_rows(left, right):
    return lax.dot_general(
        left, right, (((1,), (1,)), ((), ())), preferred_element_type=jnp.float32
    )


def contract_first(left, right):
    return lax.dot_general(
        left, right, (((0,), (0,)), ((), ())), preferred_element_type=jnp.float32
    )


def slotted(tokens, expert_ids, route_weights, out_grad, gate_weight, up_weight, down_weight):
    expert = lax.axis_index("expert")
    width = tokens.shape[1]
    local_tokens = tokens.shape[0]
    group_x, group_dy, group_w = (
        lax.all_gather(tokens, "expert", axis=0, tiled=True),
        lax.all_gather(out_grad, "expert", axis=0, tiled=True),
        lax.all_gather(route_weights, "expert", axis=0, tiled=True),
    )
    group_ids = lax.all_gather(expert_ids, "expert", axis=0, tiled=True)
    matches = group_ids == expert
    routed = jnp.any(matches, axis=1)
    weight = jnp.sum(jnp.where(matches, group_w.astype(jnp.float32), 0.0), axis=1)
    slot_rank = jnp.cumsum(routed.astype(jnp.int32)) - 1
    slot_index = jnp.arange(ROW_CAP, dtype=jnp.int32)
    picker = ((slot_rank[None, :] == slot_index[:, None]) & routed[None, :]).astype(jnp.bfloat16)
    slot_x = jnp.dot(picker, group_x, preferred_element_type=jnp.float32).astype(jnp.bfloat16)
    scaled = (weight[:, None] * group_dy.astype(jnp.float32)).astype(jnp.bfloat16)
    slot_dy = jnp.dot(picker, scaled, preferred_element_type=jnp.float32).astype(jnp.bfloat16)
    w_gate = gate_weight[0]
    w_up = up_weight[0]
    w_down = down_weight[0]
    all_x = lax.all_gather(slot_x, "dp", axis=0, tiled=True)
    gate_pre = contract_rows(w_gate, all_x)
    up_pre = contract_rows(w_up, all_x)
    gate_sig = jax.nn.sigmoid(gate_pre)
    silu_gate = gate_pre * gate_sig
    hidden = (silu_gate * up_pre).astype(jnp.bfloat16)
    expert_out = lax.psum_scatter(
        contract_first(hidden, w_down).astype(jnp.bfloat16), "dp", scatter_dimension=0, tiled=True
    )
    all_dy = lax.all_gather(slot_dy, "dp", axis=0, tiled=True)
    hidden_grad = contract_rows(w_down, all_dy)
    silu_slope = gate_sig * (1.0 + gate_pre * (1.0 - gate_sig))
    gate_act = (hidden_grad * up_pre * silu_slope).astype(jnp.bfloat16)
    up_act = (hidden_grad * silu_gate).astype(jnp.bfloat16)
    grad_down = jnp.dot(hidden, all_dy, preferred_element_type=jnp.float32).astype(jnp.bfloat16)
    grad_gate = jnp.dot(gate_act, all_x, preferred_element_type=jnp.float32).astype(jnp.bfloat16)
    grad_up = jnp.dot(up_act, all_x, preferred_element_type=jnp.float32).astype(jnp.bfloat16)
    expert_in = lax.psum_scatter(
        (contract_first(gate_act, w_gate) + contract_first(up_act, w_up)).astype(jnp.bfloat16),
        "dp",
        scatter_dimension=0,
        tiled=True,
    )
    back_out = contract_first(picker, expert_out).astype(jnp.bfloat16)
    back_in = contract_first(picker, expert_in).astype(jnp.bfloat16)
    got_out, got_in = (
        lax.all_to_all(back_out, "expert", split_axis=0, concat_axis=0, tiled=True),
        lax.all_to_all(back_in, "expert", split_axis=0, concat_axis=0, tiled=True),
    )
    expert_count = lax.axis_size("expert")
    got_out = got_out.reshape(expert_count, local_tokens, width)
    got_in = got_in.reshape(expert_count, local_tokens, width)
    expert_range = jnp.arange(expert_count, dtype=jnp.int32)
    own_match = expert_ids[:, :, None] == expert_range[None, None, :]
    mix_weight = jnp.sum(
        jnp.where(own_match, route_weights.astype(jnp.float32)[:, :, None], 0.0), axis=1
    )
    mixed_out = jnp.sum(jnp.transpose(mix_weight)[:, :, None] * got_out.astype(jnp.float32), axis=0)
    input_total = jnp.sum(got_in.astype(jnp.float32), axis=0)
    return (
        mixed_out.astype(jnp.bfloat16),
        input_total.astype(jnp.bfloat16),
        grad_gate[None],
        grad_up[None],
        grad_down[None],
    )


CORE, ASIDE, ACROSS = (1, 1), (4, 2), (2, 4)


def from_xor(value, masks, devices):
    return lax.ppermute(value, AXES, [(i, i ^ masks[i % 2]) for i in range(devices)])


def kernel_call(body, out_shape, cost, *operands, scratch=(), hbm=(), blocks=False):
    vmem, smem = pl.BlockSpec(memory_space=pltpu.VMEM), pl.BlockSpec(memory_space=pltpu.SMEM)
    stay = pl.BlockSpec(memory_space=pltpu.HBM)
    specs = [stay if i in hbm else smem if o.ndim == 1 else vmem for i, o in enumerate(operands)]
    operands = [
        pltpu.with_memory_space_constraint(o, pltpu.HBM) if i in hbm else o
        for i, o in enumerate(operands)
    ]
    more = {}
    if blocks:
        specs = [
            smem if o.ndim == 1 else pl.BlockSpec(o.shape, lambda i: (0, 0)) for o in operands
        ]
        operands = [
            o if o.ndim == 1 else pltpu.with_memory_space_constraint(o, pltpu.HBM)
            for o in operands
        ]
        more = {"grid": (1,)}
    return pl.pallas_call(
        body,
        out_shape=out_shape,
        in_specs=specs,
        out_specs=jax.tree.map(lambda _: vmem, out_shape),
        scratch_shapes=scratch,
        compiler_params=pltpu.CompilerParams(vmem_limit_bytes=16 << 20),
        cost_estimate=pl.CostEstimate(flops=cost, bytes_accessed=4 << 20, transcendentals=0),
        **more,
    )(*operands)


def copy_all(pairs, sems):
    copies = [pltpu.make_async_copy(src, dst, sems.at[i]) for i, (src, dst) in enumerate(pairs)]
    for copy in copies:
        copy.start()
    for copy in copies:
        copy.wait()


def load_body(gate_ref, up_ref, down_ref, pair_ref, down_out_ref, sems):
    ff = gate_ref.shape[1]
    copy_all(
        [
            (gate_ref.at[0], pair_ref.at[pl.ds(0, ff)]),
            (up_ref.at[0], pair_ref.at[pl.ds(ff, ff)]),
            (down_ref.at[0], down_out_ref),
        ],
        sems,
    )


def pack_body(x_ref, dy_ref, ids_ref, w_ref, expert_ref, msg_ref, mine_ref):
    rows, width = x_ref.shape
    top = ids_ref.shape[0]
    lanes = msg_ref.shape[1] - 2 * width
    msg_ref[:, :width] = x_ref[...]
    msg_ref[:, width : 2 * width] = dy_ref[...]
    diagonal = lax.broadcasted_iota(jnp.int32, (rows, rows), 0) == lax.broadcasted_iota(
        jnp.int32, (rows, rows), 1
    )
    expert = lax.broadcasted_iota(jnp.int32, (rows, lanes), 1)
    top_weights = w_ref[...].astype(jnp.float32)
    route = jnp.zeros((rows, lanes), jnp.float32)
    for k in range(top):
        named = jnp.sum(jnp.where(diagonal, ids_ref[k : k + 1, :], 0), axis=1, keepdims=True)
        weight = jnp.sum(jnp.where(diagonal, top_weights[k : k + 1, :], 0.0), axis=1, keepdims=True)
        route = route + jnp.where(expert == named, weight, 0.0)
    msg_ref[:, 2 * width :] = route.astype(jnp.bfloat16)
    lane = lax.broadcasted_iota(jnp.int32, mine_ref.shape, 1)
    mine_ref[...] = jnp.where(lane == expert_ref[0], 1.0, 0.0)


def places(pieces):
    start = 0
    for piece in pieces:
        yield slice(start, start + piece.shape[0]), piece
        start += piece.shape[0]


def block_places(pieces, order):
    rows = pieces[0].shape[0] // 2
    for i, piece in enumerate(pieces):
        for k in range(2):
            at = i // 2 * 4 + order[i % 2 * 2 + k]
            yield slice(at * rows, (at + 1) * rows), piece, slice(k * rows, (k + 1) * rows)


def stack_body(*refs):
    for here, piece in places(refs[:-1]):
        refs[-1][here, :] = piece[...]


def forward_body(count, *refs):
    pieces, (pair_ref, x_ref, hidden_ref, gate_ref, up_ref) = refs[:count], refs[count:]
    for here, piece, there in block_places(pieces, (0, 1, 2, 3)):
        x_ref[here, :] = piece[there, :]
    x = x_ref[...]
    ff = gate_ref.shape[1]
    gate_pre = contract_rows(x, pair_ref[:ff, :])
    up_pre = contract_rows(x, pair_ref[ff:, :])
    gate_sig = 1.0 / (1.0 + jnp.exp(-gate_pre))
    silu_gate = gate_pre * gate_sig
    hidden_ref[...] = silu_gate * up_pre
    gate_ref[...] = up_pre * (gate_sig * (1.0 + gate_pre * (1.0 - gate_sig)))
    up_ref[...] = silu_gate


def corner_body(own_ref, came_ref, out_ref, into_ref):
    rows, width = out_ref.shape
    for side, ref in enumerate((out_ref, into_ref)):
        at = slice(side * width, (side + 1) * width)
        ref[...] = (own_ref[-rows:, at].astype(jnp.float32) + came_ref[:, at].astype(jnp.float32)).astype(jnp.bfloat16)


def most_body(own_ref, came_ref, here_ref, aside_ref, out_ref, into_ref):
    rows, width = out_ref.shape
    for at, ref in ((0, here_ref), (2, aside_ref)):
        at = slice(at * rows, (at + 1) * rows)
        ref[...] = (own_ref[at, :].astype(jnp.float32) + came_ref[at, :].astype(jnp.float32)).astype(ref.dtype)
    for side, ref in enumerate((out_ref, into_ref)):
        at = (slice(rows, 2 * rows), slice(side * width, (side + 1) * width))
        ref[...] = own_ref[at].astype(jnp.float32) + came_ref[at].astype(jnp.float32)


def backward_body(count, *refs):
    pieces, rest = refs[:count], refs[count:]
    hidden_ref, gate_ref, up_ref, mine_ref, pair_ref, wd_ref = rest[:6]
    dy_ref, scaled_ref, acts_ref, own_ref, most_ref, corner_ref, weight_ref = rest[6:]
    ff = wd_ref.shape[0]
    width = dy_ref.shape[1]
    for here, piece, there in block_places(pieces, (0, 2, 1, 3)):
        dy_ref[here, :] = piece[there, :width]
        route = piece[there, width:].astype(jnp.float32) * mine_ref[:1, :]
        weight = jnp.sum(route, axis=1, keepdims=True)
        weight_ref[here, :] = jnp.broadcast_to(weight, (route.shape[0], weight_ref.shape[1]))
    weight = weight_ref[:, :1]
    scaled_ref[...] = (weight * hidden_ref[...]).astype(jnp.bfloat16)
    hidden_grad = weight * contract_rows(dy_ref[...], wd_ref[...])
    acts_ref[:, :ff] = (hidden_grad * gate_ref[...]).astype(jnp.bfloat16)
    acts_ref[:, ff:] = (hidden_grad * up_ref[...]).astype(jnp.bfloat16)
    out = jnp.dot(scaled_ref[...], wd_ref[...], preferred_element_type=jnp.float32)
    into = jnp.dot(acts_ref[...], pair_ref[...], preferred_element_type=jnp.float32)
    half, most = own_ref.shape[0], most_ref.shape[0]
    for side, total in enumerate((out, into)):
        at = slice(side * width, (side + 1) * width)
        own_ref[:, at] = total[:half, :].astype(jnp.bfloat16)
        corner_ref[:, at] = total[half + most :, :].astype(jnp.bfloat16)
        most_ref[:, at] = total[half : half + most, :].astype(jnp.bfloat16)


def turn_body(here_ref, came_ref, to_ref):
    to_ref[...] = (here_ref[...] + came_ref[...].astype(jnp.float32)).astype(jnp.bfloat16)


def deal_body(here_ref, aside_ref, *refs):
    parts, outs = refs[:2], refs[2:]
    width, rows = parts[0].shape[1], outs[0].shape[0]
    for side, part in enumerate(parts):
        at = slice(side * width, (side + 1) * width)
        total = here_ref[:, at] + aside_ref[:, at].astype(jnp.float32)
        total = total + part[...].astype(jnp.float32)
        for i, ref in enumerate(outs):
            ref[:, at] = total[i * rows : (i + 1) * rows, :].astype(ref.dtype)


def end_body(own_ref, *refs):
    parts, (out_ref, into_ref) = refs[:-2], refs[-2:]
    total = own_ref[...]
    for part in parts:
        total = total + part[...].astype(jnp.float32)
    width = out_ref.shape[1]
    out_ref[...] = total[:, :width].astype(jnp.bfloat16)
    into_ref[...] = total[:, width:].astype(jnp.bfloat16)


def grad_body(rows_ref, acts_ref, *grads):
    ff = grads[0].shape[1]
    for i, ref in enumerate(grads):
        acts = acts_ref[:, i * ff : (i + 1) * ff]
        ref[0] = contract_first(acts, rows_ref[...]).astype(jnp.bfloat16)


def dense(tokens, expert_ids, route_weights, out_grad, gate_weight, up_weight, down_weight):
    experts = lax.axis_size("expert")
    devices = lax.axis_size("dp") * experts
    expert = lax.axis_index("expert").astype(jnp.int32).reshape(1)
    rows, width = tokens.shape
    ff = gate_weight.shape[1]
    near = tuple((k << 3, k << 3) for k in range(1, devices >> 3))
    block_rows = rows * (len(near) + 1)
    bf16, f32 = jnp.bfloat16, jnp.float32
    columns = 2 * width + experts + -experts % 128
    unit = 2 * block_rows * ff * width

    def shape(*dims, dtype=bf16):
        return jax.ShapeDtypeStruct(dims, dtype)

    def passed(value, masks):
        return from_xor(value, masks, devices)

    message, mine = kernel_call(
        pack_body,
        (shape(rows, columns), shape(8, columns - 2 * width, dtype=f32)),
        0,
        tokens,
        out_grad,
        expert_ids.T,
        route_weights.T,
        expert,
        blocks=True,
    )
    weights = kernel_call(
        load_body,
        (shape(2 * ff, width), shape(ff, width)),
        0,
        gate_weight,
        up_weight,
        down_weight,
        scratch=[pltpu.SemaphoreType.DMA((3,))],
        hbm=(0, 1, 2),
    )
    arrived = [message] + [passed(message, m) for m in near]
    block_x = jnp.concatenate([piece[:, :width] for piece in arrived], axis=0)
    block_dy = jnp.concatenate([piece[:, width:] for piece in arrived], axis=0)
    block_dy, *weights = lax.optimization_barrier((block_dy, *weights))

    aside_x, across_dy = passed(block_x, ASIDE), passed(block_dy, ACROSS)
    aside_dy, across_x = passed(block_dy, ASIDE), passed(block_x, ACROSS)
    corner_x, corner_dy = passed(aside_x, ACROSS), passed(across_dy, ASIDE)
    half = 4 * block_rows

    def both_cores(*pairs):
        own = [
            kernel_call(stack_body, shape(2 * block_rows, pair[0].shape[1]), 0, *pair)
            for pair in pairs
        ]
        return own + [passed(pair, CORE) for pair in own]

    x_pieces = both_cores((block_x, across_x), (aside_x, corner_x))
    dy_pieces = both_cores((block_dy, aside_dy), (across_dy, corner_dy))
    x_pieces[2], dy_pieces[2] = lax.optimization_barrier((x_pieces[2], dy_pieces[2]))
    all_x, hidden, gate_part, up_part = kernel_call(
        functools.partial(forward_body, len(x_pieces)),
        (shape(2 * half, width),) + (shape(2 * half, ff, dtype=f32),) * 3,
        16 * unit,
        *x_pieces,
        weights[0],
    )
    all_dy, scaled, acts, own, message, corner_message = kernel_call(
        functools.partial(backward_body, len(dy_pieces)),
        (
            shape(2 * half, width),
            shape(2 * half, ff),
            shape(2 * half, 2 * ff),
            shape(half, 2 * width),
            shape(half - block_rows, 2 * width),
            shape(block_rows, 2 * width),
        ),
        24 * unit,
        *dy_pieces,
        hidden,
        gate_part,
        up_part,
        mine,
        *weights,
        scratch=[pltpu.VMEM((2 * half, columns - 2 * width), f32)],
    )
    corner_came = passed(corner_message, CORE)
    corner_came, message = lax.optimization_barrier((corner_came, message))
    most_came = passed(message, CORE)

    piece, full = shape(block_rows, width), shape(block_rows, width, dtype=f32)
    out_corner, into_corner = kernel_call(corner_body, (piece, piece), 0, own, corner_came)
    here, aside, out_across, into_across = kernel_call(
        most_body,
        (shape(block_rows, 2 * width, dtype=f32), shape(block_rows, 2 * width), full, full),
        0,
        own,
        most_came,
    )
    out_turn, into_turn = passed(out_corner, ASIDE), passed(into_corner, ASIDE)
    aside = passed(aside, ASIDE)
    out_across = passed(kernel_call(turn_body, piece, 0, out_across, out_turn), ACROSS)
    into_across = passed(kernel_call(turn_body, piece, 0, into_across, into_turn), ACROSS)
    here, scaled, acts = lax.optimization_barrier((here, scaled, acts))
    grad_gate, grad_up = kernel_call(
        grad_body, (shape(*gate_weight.shape),) * 2, 16 * unit, all_x, acts
    )
    here, grad_gate, grad_up = lax.optimization_barrier((here, grad_gate, grad_up))
    mine_sum, *away = kernel_call(
        deal_body,
        (shape(rows, 2 * width, dtype=f32),) + (shape(rows, 2 * width),) * len(near),
        0,
        here,
        aside,
        out_across,
        into_across,
    )
    mine_sum, scaled = lax.optimization_barrier((mine_sum, scaled))
    grad_down = kernel_call(grad_body, shape(*down_weight.shape), 8 * unit, all_dy, scaled)
    mixed, input_grad = kernel_call(
        end_body,
        (shape(rows, width),) * 2,
        0,
        mine_sum,
        *[passed(piece, m) for m, piece in reversed(list(zip(near, away)))],
    )
    return mixed, input_grad, grad_gate, grad_up, grad_down


def shards(tokens, *others):
    experts = lax.axis_size("expert")
    devices = lax.axis_size("dp") * experts
    whole_group = tokens.shape[0] * experts <= ROW_CAP
    if whole_group and devices >= 16 and devices & (devices - 1) == 0:
        return dense(tokens, *others)
    return slotted(tokens, *others)


def solution(mesh):
    return jax.shard_map(
        shards,
        mesh=mesh,
        in_specs=(
            P(("dp", "expert"), None),
            P(("dp", "expert"), None),
            P(("dp", "expert"), None),
            P(("dp", "expert"), None),
            P("expert", "dp", None),
            P("expert", "dp", None),
            P("expert", "dp", None),
        ),
        out_specs=(
            P(("dp", "expert"), None),
            P(("dp", "expert"), None),
            P("expert", "dp", None),
            P("expert", "dp", None),
            P("expert", "dp", None),
        ),
        check_vma=False,
    )
```

```python
import functools

import jax
import jax.numpy as jnp
from jax import lax
from jax.experimental import pallas as pl
from jax.experimental.pallas import tpu as pltpu
from jax.sharding import PartitionSpec as P

ROW_CAP = 16
AXES = ("dp", "expert")


def contract_rows(left, right):
    return lax.dot_general(
        left, right, (((1,), (1,)), ((), ())), preferred_element_type=jnp.float32
    )


def contract_first(left, right):
    return lax.dot_general(
        left, right, (((0,), (0,)), ((), ())), preferred_element_type=jnp.float32
    )


def slotted(tokens, expert_ids, route_weights, out_grad, gate_weight, up_weight, down_weight):
    expert = lax.axis_index("expert")
    width = tokens.shape[1]
    local_tokens = tokens.shape[0]
    group_x, group_dy, group_w = (
        lax.all_gather(tokens, "expert", axis=0, tiled=True),
        lax.all_gather(out_grad, "expert", axis=0, tiled=True),
        lax.all_gather(route_weights, "expert", axis=0, tiled=True),
    )
    group_ids = lax.all_gather(expert_ids, "expert", axis=0, tiled=True)
    matches = group_ids == expert
    routed = jnp.any(matches, axis=1)
    weight = jnp.sum(jnp.where(matches, group_w.astype(jnp.float32), 0.0), axis=1)
    slot_rank = jnp.cumsum(routed.astype(jnp.int32)) - 1
    slot_index = jnp.arange(ROW_CAP, dtype=jnp.int32)
    picker = ((slot_rank[None, :] == slot_index[:, None]) & routed[None, :]).astype(jnp.bfloat16)
    slot_x = jnp.dot(picker, group_x, preferred_element_type=jnp.float32).astype(jnp.bfloat16)
    scaled = (weight[:, None] * group_dy.astype(jnp.float32)).astype(jnp.bfloat16)
    slot_dy = jnp.dot(picker, scaled, preferred_element_type=jnp.float32).astype(jnp.bfloat16)
    w_gate = gate_weight[0]
    w_up = up_weight[0]
    w_down = down_weight[0]
    all_x = lax.all_gather(slot_x, "dp", axis=0, tiled=True)
    gate_pre = contract_rows(w_gate, all_x)
    up_pre = contract_rows(w_up, all_x)
    gate_sig = jax.nn.sigmoid(gate_pre)
    silu_gate = gate_pre * gate_sig
    hidden = (silu_gate * up_pre).astype(jnp.bfloat16)
    expert_out = lax.psum_scatter(
        contract_first(hidden, w_down).astype(jnp.bfloat16), "dp", scatter_dimension=0, tiled=True
    )
    all_dy = lax.all_gather(slot_dy, "dp", axis=0, tiled=True)
    hidden_grad = contract_rows(w_down, all_dy)
    silu_slope = gate_sig * (1.0 + gate_pre * (1.0 - gate_sig))
    gate_act = (hidden_grad * up_pre * silu_slope).astype(jnp.bfloat16)
    up_act = (hidden_grad * silu_gate).astype(jnp.bfloat16)
    grad_down = jnp.dot(hidden, all_dy, preferred_element_type=jnp.float32).astype(jnp.bfloat16)
    grad_gate = jnp.dot(gate_act, all_x, preferred_element_type=jnp.float32).astype(jnp.bfloat16)
    grad_up = jnp.dot(up_act, all_x, preferred_element_type=jnp.float32).astype(jnp.bfloat16)
    expert_in = lax.psum_scatter(
        (contract_first(gate_act, w_gate) + contract_first(up_act, w_up)).astype(jnp.bfloat16),
        "dp",
        scatter_dimension=0,
        tiled=True,
    )
    back_out = contract_first(picker, expert_out).astype(jnp.bfloat16)
    back_in = contract_first(picker, expert_in).astype(jnp.bfloat16)
    got_out, got_in = (
        lax.all_to_all(back_out, "expert", split_axis=0, concat_axis=0, tiled=True),
        lax.all_to_all(back_in, "expert", split_axis=0, concat_axis=0, tiled=True),
    )
    expert_count = lax.axis_size("expert")
    got_out = got_out.reshape(expert_count, local_tokens, width)
    got_in = got_in.reshape(expert_count, local_tokens, width)
    expert_range = jnp.arange(expert_count, dtype=jnp.int32)
    own_match = expert_ids[:, :, None] == expert_range[None, None, :]
    mix_weight = jnp.sum(
        jnp.where(own_match, route_weights.astype(jnp.float32)[:, :, None], 0.0), axis=1
    )
    mixed_out = jnp.sum(jnp.transpose(mix_weight)[:, :, None] * got_out.astype(jnp.float32), axis=0)
    input_total = jnp.sum(got_in.astype(jnp.float32), axis=0)
    return (
        mixed_out.astype(jnp.bfloat16),
        input_total.astype(jnp.bfloat16),
        grad_gate[None],
        grad_up[None],
        grad_down[None],
    )


CORE, ASIDE, ACROSS = (1, 1), (4, 2), (2, 4)


def from_xor(value, masks, devices):
    return lax.ppermute(value, AXES, [(i, i ^ masks[i % 2]) for i in range(devices)])


def kernel_call(body, out_shape, cost, *operands, scratch=(), hbm=(), blocks=False):
    vmem, smem = pl.BlockSpec(memory_space=pltpu.VMEM), pl.BlockSpec(memory_space=pltpu.SMEM)
    stay = pl.BlockSpec(memory_space=pltpu.HBM)
    specs = [stay if i in hbm else smem if o.ndim == 1 else vmem for i, o in enumerate(operands)]
    operands = [
        pltpu.with_memory_space_constraint(o, pltpu.HBM) if i in hbm else o
        for i, o in enumerate(operands)
    ]
    more = {}
    if blocks:
        specs = [
            smem if o.ndim == 1 else pl.BlockSpec(o.shape, lambda i: (0, 0)) for o in operands
        ]
        operands = [
            o if o.ndim == 1 else pltpu.with_memory_space_constraint(o, pltpu.HBM)
            for o in operands
        ]
        more = {"grid": (1,)}
    return pl.pallas_call(
        body,
        out_shape=out_shape,
        in_specs=specs,
        out_specs=jax.tree.map(lambda _: vmem, out_shape),
        scratch_shapes=scratch,
        compiler_params=pltpu.CompilerParams(vmem_limit_bytes=16 << 20),
        cost_estimate=pl.CostEstimate(flops=cost, bytes_accessed=4 << 20, transcendentals=0),
        **more,
    )(*operands)


def copy_all(pairs, sems):
    copies = [pltpu.make_async_copy(src, dst, sems.at[i]) for i, (src, dst) in enumerate(pairs)]
    for copy in copies:
        copy.start()
    for copy in copies:
        copy.wait()


LOAD_PARTS = 4


def load_body(gate_ref, up_ref, down_ref, pair_ref, down_out_ref, sems):
    ff = gate_ref.shape[1]
    part = ff // LOAD_PARTS
    pairs = []
    for k in range(LOAD_PARTS):
        here = pl.ds(k * part, part)
        pairs.append((gate_ref.at[0, here], pair_ref.at[here]))
        pairs.append((up_ref.at[0, here], pair_ref.at[pl.ds(ff + k * part, part)]))
        pairs.append((down_ref.at[0, here], down_out_ref.at[here]))
    copy_all(pairs, sems)


def pack_body(x_ref, dy_ref, ids_ref, w_ref, expert_ref, msg_ref, mine_ref):
    rows, width = x_ref.shape
    top = ids_ref.shape[0]
    lanes = msg_ref.shape[1] - 2 * width
    msg_ref[:, :width] = x_ref[...]
    msg_ref[:, width : 2 * width] = dy_ref[...]
    diagonal = lax.broadcasted_iota(jnp.int32, (rows, rows), 0) == lax.broadcasted_iota(
        jnp.int32, (rows, rows), 1
    )
    expert = lax.broadcasted_iota(jnp.int32, (rows, lanes), 1)
    top_weights = w_ref[...].astype(jnp.float32)
    route = jnp.zeros((rows, lanes), jnp.float32)
    for k in range(top):
        named = jnp.sum(jnp.where(diagonal, ids_ref[k : k + 1, :], 0), axis=1, keepdims=True)
        weight = jnp.sum(jnp.where(diagonal, top_weights[k : k + 1, :], 0.0), axis=1, keepdims=True)
        route = route + jnp.where(expert == named, weight, 0.0)
    msg_ref[:, 2 * width :] = route.astype(jnp.bfloat16)
    lane = lax.broadcasted_iota(jnp.int32, mine_ref.shape, 1)
    mine_ref[...] = jnp.where(lane == expert_ref[0], 1.0, 0.0)


def places(pieces):
    start = 0
    for piece in pieces:
        yield slice(start, start + piece.shape[0]), piece
        start += piece.shape[0]


def block_places(pieces, order):
    rows = pieces[0].shape[0] // 2
    for i, piece in enumerate(pieces):
        for k in range(2):
            at = i // 2 * 4 + order[i % 2 * 2 + k]
            yield slice(at * rows, (at + 1) * rows), piece, slice(k * rows, (k + 1) * rows)


def stack_body(*refs):
    for here, piece in places(refs[:-1]):
        refs[-1][here, :] = piece[...]


def forward_body(count, *refs):
    pieces, (pair_ref, x_ref, hidden_ref, gate_ref, up_ref) = refs[:count], refs[count:]
    for here, piece, there in block_places(pieces, (0, 1, 2, 3)):
        x_ref[here, :] = piece[there, :]
    x = x_ref[...]
    ff = gate_ref.shape[1]
    gate_pre = contract_rows(x, pair_ref[:ff, :])
    up_pre = contract_rows(x, pair_ref[ff:, :])
    gate_sig = 1.0 / (1.0 + jnp.exp(-gate_pre))
    silu_gate = gate_pre * gate_sig
    hidden_ref[...] = silu_gate * up_pre
    gate_ref[...] = up_pre * (gate_sig * (1.0 + gate_pre * (1.0 - gate_sig)))
    up_ref[...] = silu_gate


def corner_body(own_ref, came_ref, out_ref, into_ref):
    rows, width = out_ref.shape
    for side, ref in enumerate((out_ref, into_ref)):
        at = slice(side * width, (side + 1) * width)
        ref[...] = (own_ref[-rows:, at] + came_ref[:, at].astype(jnp.float32)).astype(jnp.bfloat16)


def most_body(own_ref, came_ref, here_ref, aside_ref, out_ref, into_ref):
    rows, width = out_ref.shape
    for at, ref in ((0, here_ref), (2, aside_ref)):
        at = slice(at * rows, (at + 1) * rows)
        ref[...] = (own_ref[at, :] + came_ref[at, :].astype(jnp.float32)).astype(ref.dtype)
    for side, ref in enumerate((out_ref, into_ref)):
        at = (slice(rows, 2 * rows), slice(side * width, (side + 1) * width))
        ref[...] = own_ref[at] + came_ref[at].astype(jnp.float32)


def backward_body(count, *refs):
    pieces, rest = refs[:count], refs[count:]
    hidden_ref, gate_ref, up_ref, mine_ref, pair_ref, wd_ref = rest[:6]
    dy_ref, scaled_ref, acts_ref, own_ref, most_ref, corner_ref, weight_ref = rest[6:]
    ff = wd_ref.shape[0]
    width = dy_ref.shape[1]
    for here, piece, there in block_places(pieces, (0, 2, 1, 3)):
        dy_ref[here, :] = piece[there, :width]
        route = piece[there, width:].astype(jnp.float32) * mine_ref[:1, :]
        weight = jnp.sum(route, axis=1, keepdims=True)
        weight_ref[here, :] = jnp.broadcast_to(weight, (route.shape[0], weight_ref.shape[1]))
    weight = weight_ref[:, :1]
    scaled_ref[...] = (weight * hidden_ref[...]).astype(jnp.bfloat16)
    hidden_grad = weight * contract_rows(dy_ref[...], wd_ref[...])
    acts_ref[:, :ff] = (hidden_grad * gate_ref[...]).astype(jnp.bfloat16)
    acts_ref[:, ff:] = (hidden_grad * up_ref[...]).astype(jnp.bfloat16)
    out = jnp.dot(scaled_ref[...], wd_ref[...], preferred_element_type=jnp.float32)
    into = jnp.dot(acts_ref[...], pair_ref[...], preferred_element_type=jnp.float32)
    half, most = own_ref.shape[0], most_ref.shape[0]
    for side, total in enumerate((out, into)):
        at = slice(side * width, (side + 1) * width)
        own_ref[:, at] = total[:half, :]
        corner_ref[:, at] = total[half + most :, :].astype(jnp.bfloat16)
        most_ref[:, at] = total[half : half + most, :].astype(jnp.bfloat16)


def turn_body(here_ref, came_ref, to_ref):
    to_ref[...] = (here_ref[...] + came_ref[...].astype(jnp.float32)).astype(jnp.bfloat16)


def deal_body(here_ref, aside_ref, *refs):
    parts, outs = refs[:2], refs[2:]
    width, rows = parts[0].shape[1], outs[0].shape[0]
    for side, part in enumerate(parts):
        at = slice(side * width, (side + 1) * width)
        total = here_ref[:, at] + aside_ref[:, at].astype(jnp.float32)
        total = total + part[...].astype(jnp.float32)
        for i, ref in enumerate(outs):
            ref[:, at] = total[i * rows : (i + 1) * rows, :].astype(ref.dtype)


def end_body(own_ref, *refs):
    parts, (out_ref, into_ref) = refs[:-2], refs[-2:]
    total = own_ref[...]
    for part in parts:
        total = total + part[...].astype(jnp.float32)
    width = out_ref.shape[1]
    out_ref[...] = total[:, :width].astype(jnp.bfloat16)
    into_ref[...] = total[:, width:].astype(jnp.bfloat16)


def grad_body(rows_ref, acts_ref, *grads):
    ff = grads[0].shape[1]
    for i, ref in enumerate(grads):
        acts = acts_ref[:, i * ff : (i + 1) * ff]
        ref[0] = contract_first(acts, rows_ref[...]).astype(jnp.bfloat16)


def dense(tokens, expert_ids, route_weights, out_grad, gate_weight, up_weight, down_weight):
    experts = lax.axis_size("expert")
    devices = lax.axis_size("dp") * experts
    expert = lax.axis_index("expert").astype(jnp.int32).reshape(1)
    rows, width = tokens.shape
    ff = gate_weight.shape[1]
    near = tuple((k << 3, k << 3) for k in range(1, devices >> 3))
    block_rows = rows * (len(near) + 1)
    bf16, f32 = jnp.bfloat16, jnp.float32
    columns = 2 * width + experts + -experts % 128
    unit = 2 * block_rows * ff * width

    def shape(*dims, dtype=bf16):
        return jax.ShapeDtypeStruct(dims, dtype)

    def passed(value, masks):
        return from_xor(value, masks, devices)

    message, mine = kernel_call(
        pack_body,
        (shape(rows, columns), shape(8, columns - 2 * width, dtype=f32)),
        0,
        tokens,
        out_grad,
        expert_ids.T,
        route_weights.T,
        expert,
        blocks=True,
    )
    weights = kernel_call(
        load_body,
        (shape(2 * ff, width), shape(ff, width)),
        0,
        gate_weight,
        up_weight,
        down_weight,
        scratch=[pltpu.SemaphoreType.DMA((3 * LOAD_PARTS,))],
        hbm=(0, 1, 2),
    )
    arrived = [message] + [passed(message, m) for m in near]
    block_x = jnp.concatenate([piece[:, :width] for piece in arrived], axis=0)
    block_dy = jnp.concatenate([piece[:, width:] for piece in arrived], axis=0)
    block_dy, *weights = lax.optimization_barrier((block_dy, *weights))

    aside_x, across_dy = passed(block_x, ASIDE), passed(block_dy, ACROSS)
    aside_dy, across_x = passed(block_dy, ASIDE), passed(block_x, ACROSS)
    corner_x, corner_dy = passed(aside_x, ACROSS), passed(across_dy, ASIDE)
    half = 4 * block_rows

    def both_cores(*pairs):
        own = [
            kernel_call(stack_body, shape(2 * block_rows, pair[0].shape[1]), 0, *pair)
            for pair in pairs
        ]
        return own + [passed(pair, CORE) for pair in own]

    x_pieces = both_cores((block_x, across_x), (aside_x, corner_x))
    dy_pieces = both_cores((block_dy, aside_dy), (across_dy, corner_dy))
    x_pieces[2], dy_pieces[2] = lax.optimization_barrier((x_pieces[2], dy_pieces[2]))
    all_x, hidden, gate_part, up_part = kernel_call(
        functools.partial(forward_body, len(x_pieces)),
        (shape(2 * half, width),) + (shape(2 * half, ff, dtype=f32),) * 3,
        16 * unit,
        *x_pieces,
        weights[0],
    )
    all_dy, scaled, acts, own, message, corner_message = kernel_call(
        functools.partial(backward_body, len(dy_pieces)),
        (
            shape(2 * half, width),
            shape(2 * half, ff),
            shape(2 * half, 2 * ff),
            shape(half, 2 * width, dtype=f32),
            shape(half - block_rows, 2 * width),
            shape(block_rows, 2 * width),
        ),
        24 * unit,
        *dy_pieces,
        hidden,
        gate_part,
        up_part,
        mine,
        *weights,
        scratch=[pltpu.VMEM((2 * half, columns - 2 * width), f32)],
    )
    corner_came = passed(corner_message, CORE)
    corner_came, message = lax.optimization_barrier((corner_came, message))
    most_came = passed(message, CORE)

    piece, full = shape(block_rows, width), shape(block_rows, width, dtype=f32)
    out_corner, into_corner = kernel_call(corner_body, (piece, piece), 0, own, corner_came)
    here, aside, out_across, into_across = kernel_call(
        most_body,
        (shape(block_rows, 2 * width, dtype=f32), shape(block_rows, 2 * width), full, full),
        0,
        own,
        most_came,
    )
    out_turn, into_turn = passed(out_corner, ASIDE), passed(into_corner, ASIDE)
    aside = passed(aside, ASIDE)
    out_across = passed(kernel_call(turn_body, piece, 0, out_across, out_turn), ACROSS)
    into_across = passed(kernel_call(turn_body, piece, 0, into_across, into_turn), ACROSS)
    here, scaled, acts = lax.optimization_barrier((here, scaled, acts))
    grad_gate, grad_up = kernel_call(
        grad_body, (shape(*gate_weight.shape),) * 2, 16 * unit, all_x, acts
    )
    here, grad_gate, grad_up = lax.optimization_barrier((here, grad_gate, grad_up))
    mine_sum, *away = kernel_call(
        deal_body,
        (shape(rows, 2 * width, dtype=f32),) + (shape(rows, 2 * width),) * len(near),
        0,
        here,
        aside,
        out_across,
        into_across,
    )
    mine_sum, scaled = lax.optimization_barrier((mine_sum, scaled))
    grad_down = kernel_call(grad_body, shape(*down_weight.shape), 8 * unit, all_dy, scaled)
    mixed, input_grad = kernel_call(
        end_body,
        (shape(rows, width),) * 2,
        0,
        mine_sum,
        *[passed(piece, m) for m, piece in reversed(list(zip(near, away)))],
    )
    return mixed, input_grad, grad_gate, grad_up, grad_down


def shards(tokens, *others):
    experts = lax.axis_size("expert")
    devices = lax.axis_size("dp") * experts
    whole_group = tokens.shape[0] * experts <= ROW_CAP
    if whole_group and devices >= 16 and devices & (devices - 1) == 0:
        return dense(tokens, *others)
    return slotted(tokens, *others)


def solution(mesh):
    return jax.shard_map(
        shards,
        mesh=mesh,
        in_specs=(
            P(("dp", "expert"), None),
            P(("dp", "expert"), None),
            P(("dp", "expert"), None),
            P(("dp", "expert"), None),
            P("expert", "dp", None),
            P("expert", "dp", None),
            P("expert", "dp", None),
        ),
        out_specs=(
            P(("dp", "expert"), None),
            P(("dp", "expert"), None),
            P("expert", "dp", None),
            P("expert", "dp", None),
            P("expert", "dp", None),
        ),
        check_vma=False,
    )
```

```python
import functools

import jax
import jax.numpy as jnp
from jax import lax
from jax.experimental import pallas as pl
from jax.experimental.pallas import tpu as pltpu
from jax.sharding import PartitionSpec as P

ROW_CAP = 16
AXES = ("dp", "expert")


def contract_rows(left, right):
    return lax.dot_general(
        left, right, (((1,), (1,)), ((), ())), preferred_element_type=jnp.float32
    )


def contract_first(left, right):
    return lax.dot_general(
        left, right, (((0,), (0,)), ((), ())), preferred_element_type=jnp.float32
    )


def slotted(tokens, expert_ids, route_weights, out_grad, gate_weight, up_weight, down_weight):
    expert = lax.axis_index("expert")
    width = tokens.shape[1]
    local_tokens = tokens.shape[0]
    group_x, group_dy, group_w = (
        lax.all_gather(tokens, "expert", axis=0, tiled=True),
        lax.all_gather(out_grad, "expert", axis=0, tiled=True),
        lax.all_gather(route_weights, "expert", axis=0, tiled=True),
    )
    group_ids = lax.all_gather(expert_ids, "expert", axis=0, tiled=True)
    matches = group_ids == expert
    routed = jnp.any(matches, axis=1)
    weight = jnp.sum(jnp.where(matches, group_w.astype(jnp.float32), 0.0), axis=1)
    slot_rank = jnp.cumsum(routed.astype(jnp.int32)) - 1
    slot_index = jnp.arange(ROW_CAP, dtype=jnp.int32)
    picker = ((slot_rank[None, :] == slot_index[:, None]) & routed[None, :]).astype(jnp.bfloat16)
    slot_x = jnp.dot(picker, group_x, preferred_element_type=jnp.float32).astype(jnp.bfloat16)
    scaled = (weight[:, None] * group_dy.astype(jnp.float32)).astype(jnp.bfloat16)
    slot_dy = jnp.dot(picker, scaled, preferred_element_type=jnp.float32).astype(jnp.bfloat16)
    w_gate = gate_weight[0]
    w_up = up_weight[0]
    w_down = down_weight[0]
    all_x = lax.all_gather(slot_x, "dp", axis=0, tiled=True)
    gate_pre = contract_rows(w_gate, all_x)
    up_pre = contract_rows(w_up, all_x)
    gate_sig = jax.nn.sigmoid(gate_pre)
    silu_gate = gate_pre * gate_sig
    hidden = (silu_gate * up_pre).astype(jnp.bfloat16)
    expert_out = lax.psum_scatter(
        contract_first(hidden, w_down).astype(jnp.bfloat16), "dp", scatter_dimension=0, tiled=True
    )
    all_dy = lax.all_gather(slot_dy, "dp", axis=0, tiled=True)
    hidden_grad = contract_rows(w_down, all_dy)
    silu_slope = gate_sig * (1.0 + gate_pre * (1.0 - gate_sig))
    gate_act = (hidden_grad * up_pre * silu_slope).astype(jnp.bfloat16)
    up_act = (hidden_grad * silu_gate).astype(jnp.bfloat16)
    grad_down = jnp.dot(hidden, all_dy, preferred_element_type=jnp.float32).astype(jnp.bfloat16)
    grad_gate = jnp.dot(gate_act, all_x, preferred_element_type=jnp.float32).astype(jnp.bfloat16)
    grad_up = jnp.dot(up_act, all_x, preferred_element_type=jnp.float32).astype(jnp.bfloat16)
    expert_in = lax.psum_scatter(
        (contract_first(gate_act, w_gate) + contract_first(up_act, w_up)).astype(jnp.bfloat16),
        "dp",
        scatter_dimension=0,
        tiled=True,
    )
    back_out = contract_first(picker, expert_out).astype(jnp.bfloat16)
    back_in = contract_first(picker, expert_in).astype(jnp.bfloat16)
    got_out, got_in = (
        lax.all_to_all(back_out, "expert", split_axis=0, concat_axis=0, tiled=True),
        lax.all_to_all(back_in, "expert", split_axis=0, concat_axis=0, tiled=True),
    )
    expert_count = lax.axis_size("expert")
    got_out = got_out.reshape(expert_count, local_tokens, width)
    got_in = got_in.reshape(expert_count, local_tokens, width)
    expert_range = jnp.arange(expert_count, dtype=jnp.int32)
    own_match = expert_ids[:, :, None] == expert_range[None, None, :]
    mix_weight = jnp.sum(
        jnp.where(own_match, route_weights.astype(jnp.float32)[:, :, None], 0.0), axis=1
    )
    mixed_out = jnp.sum(jnp.transpose(mix_weight)[:, :, None] * got_out.astype(jnp.float32), axis=0)
    input_total = jnp.sum(got_in.astype(jnp.float32), axis=0)
    return (
        mixed_out.astype(jnp.bfloat16),
        input_total.astype(jnp.bfloat16),
        grad_gate[None],
        grad_up[None],
        grad_down[None],
    )


CORE, ASIDE, ACROSS = (1, 1), (4, 2), (2, 4)


def from_xor(value, masks, devices):
    return lax.ppermute(value, AXES, [(i, i ^ masks[i % 2]) for i in range(devices)])


def kernel_call(body, out_shape, cost, *operands, scratch=(), hbm=(), blocks=False):
    vmem, smem = pl.BlockSpec(memory_space=pltpu.VMEM), pl.BlockSpec(memory_space=pltpu.SMEM)
    stay = pl.BlockSpec(memory_space=pltpu.HBM)
    specs = [stay if i in hbm else smem if o.ndim == 1 else vmem for i, o in enumerate(operands)]
    operands = [
        pltpu.with_memory_space_constraint(o, pltpu.HBM) if i in hbm else o
        for i, o in enumerate(operands)
    ]
    more = {}
    if blocks:
        specs = [
            smem if o.ndim == 1 else pl.BlockSpec(o.shape, lambda i: (0, 0)) for o in operands
        ]
        operands = [
            o if o.ndim == 1 else pltpu.with_memory_space_constraint(o, pltpu.HBM)
            for o in operands
        ]
        more = {"grid": (1,)}
    return pl.pallas_call(
        body,
        out_shape=out_shape,
        in_specs=specs,
        out_specs=jax.tree.map(lambda _: vmem, out_shape),
        scratch_shapes=scratch,
        compiler_params=pltpu.CompilerParams(vmem_limit_bytes=16 << 20),
        cost_estimate=pl.CostEstimate(flops=cost, bytes_accessed=4 << 20, transcendentals=0),
        **more,
    )(*operands)


def copy_all(pairs, sems):
    copies = [pltpu.make_async_copy(src, dst, sems.at[i]) for i, (src, dst) in enumerate(pairs)]
    for copy in copies:
        copy.start()
    for copy in copies:
        copy.wait()


def load_body(gate_ref, up_ref, down_ref, pair_ref, down_out_ref, sems):
    ff = gate_ref.shape[1]
    copy_all(
        [
            (gate_ref.at[0], pair_ref.at[pl.ds(0, ff)]),
            (up_ref.at[0], pair_ref.at[pl.ds(ff, ff)]),
            (down_ref.at[0], down_out_ref),
        ],
        sems,
    )


def pack_body(x_ref, dy_ref, ids_ref, w_ref, expert_ref, msg_ref, mine_ref):
    rows, width = x_ref.shape
    top = ids_ref.shape[0]
    lanes = msg_ref.shape[1] - 2 * width
    msg_ref[:, :width] = x_ref[...]
    msg_ref[:, width : 2 * width] = dy_ref[...]
    diagonal = lax.broadcasted_iota(jnp.int32, (rows, rows), 0) == lax.broadcasted_iota(
        jnp.int32, (rows, rows), 1
    )
    expert = lax.broadcasted_iota(jnp.int32, (rows, lanes), 1)
    top_weights = w_ref[...].astype(jnp.float32)
    route = jnp.zeros((rows, lanes), jnp.float32)
    for k in range(top):
        named = jnp.sum(jnp.where(diagonal, ids_ref[k : k + 1, :], 0), axis=1, keepdims=True)
        weight = jnp.sum(jnp.where(diagonal, top_weights[k : k + 1, :], 0.0), axis=1, keepdims=True)
        route = route + jnp.where(expert == named, weight, 0.0)
    msg_ref[:, 2 * width :] = route.astype(jnp.bfloat16)
    lane = lax.broadcasted_iota(jnp.int32, mine_ref.shape, 1)
    mine_ref[...] = jnp.where(lane == expert_ref[0], 1.0, 0.0)


def places(pieces):
    start = 0
    for piece in pieces:
        yield slice(start, start + piece.shape[0]), piece
        start += piece.shape[0]


def block_places(pieces, order):
    rows = pieces[0].shape[0] // 2
    for i, piece in enumerate(pieces):
        for k in range(2):
            at = i // 2 * 4 + order[i % 2 * 2 + k]
            yield slice(at * rows, (at + 1) * rows), piece, slice(k * rows, (k + 1) * rows)


def stack_body(*refs):
    for here, piece in places(refs[:-1]):
        refs[-1][here, :] = piece[...]


def forward_body(count, *refs):
    pieces, (pair_ref, x_ref, hidden_ref, gate_ref, up_ref) = refs[:count], refs[count:]
    for here, piece, there in block_places(pieces, (0, 1, 2, 3)):
        x_ref[here, :] = piece[there, :]
    x = x_ref[...]
    ff = gate_ref.shape[1]
    gate_pre = contract_rows(x, pair_ref[:ff, :])
    up_pre = contract_rows(x, pair_ref[ff:, :])
    gate_sig = 1.0 / (1.0 + jnp.exp(-gate_pre))
    silu_gate = gate_pre * gate_sig
    hidden_ref[...] = silu_gate * up_pre
    gate_ref[...] = up_pre * (gate_sig * (1.0 + gate_pre * (1.0 - gate_sig)))
    up_ref[...] = silu_gate


def corner_body(own_ref, came_ref, out_ref, into_ref):
    rows, width = out_ref.shape
    for side, ref in enumerate((out_ref, into_ref)):
        at = slice(side * width, (side + 1) * width)
        ref[...] = (own_ref[-rows:, at] + came_ref[:, at].astype(jnp.float32)).astype(jnp.bfloat16)


def most_body(own_ref, came_ref, here_ref, aside_ref, out_ref, into_ref):
    rows, width = out_ref.shape
    for at, ref in ((0, here_ref), (2, aside_ref)):
        at = slice(at * rows, (at + 1) * rows)
        ref[...] = (own_ref[at, :] + came_ref[at, :].astype(jnp.float32)).astype(ref.dtype)
    for side, ref in enumerate((out_ref, into_ref)):
        at = (slice(rows, 2 * rows), slice(side * width, (side + 1) * width))
        ref[...] = own_ref[at] + came_ref[at].astype(jnp.float32)


def backward_body(count, *refs):
    pieces, rest = refs[:count], refs[count:]
    hidden_ref, gate_ref, up_ref, mine_ref, pair_ref, wd_ref = rest[:6]
    dy_ref, scaled_ref, acts_ref, own_ref, most_ref, corner_ref, weight_ref = rest[6:]
    ff = wd_ref.shape[0]
    width = dy_ref.shape[1]
    for here, piece, there in block_places(pieces, (0, 2, 1, 3)):
        dy_ref[here, :] = piece[there, :width]
        route = piece[there, width:].astype(jnp.float32) * mine_ref[:1, :]
        weight = jnp.sum(route, axis=1, keepdims=True)
        weight_ref[here, :] = jnp.broadcast_to(weight, (route.shape[0], weight_ref.shape[1]))
    weight = weight_ref[:, :1]
    scaled_ref[...] = (weight * hidden_ref[...]).astype(jnp.bfloat16)
    hidden_grad = weight * contract_rows(dy_ref[...], wd_ref[...])
    acts_ref[:, :ff] = (hidden_grad * gate_ref[...]).astype(jnp.bfloat16)
    acts_ref[:, ff:] = (hidden_grad * up_ref[...]).astype(jnp.bfloat16)
    out = jnp.dot(scaled_ref[...], wd_ref[...], preferred_element_type=jnp.float32)
    into = jnp.dot(acts_ref[...], pair_ref[...], preferred_element_type=jnp.float32)
    half, most = own_ref.shape[0], most_ref.shape[0]
    for side, total in enumerate((out, into)):
        at = slice(side * width, (side + 1) * width)
        own_ref[:, at] = total[:half, :]
        corner_ref[:, at] = total[half + most :, :].astype(jnp.bfloat16)
        most_ref[:, at] = total[half : half + most, :].astype(jnp.bfloat16)


def turn_body(here_ref, came_ref, to_ref):
    to_ref[...] = (here_ref[...] + came_ref[...].astype(jnp.float32)).astype(jnp.bfloat16)


def deal_body(here_ref, aside_ref, *refs):
    parts, outs = refs[:2], refs[2:]
    width, rows = parts[0].shape[1], outs[0].shape[0]
    for side, part in enumerate(parts):
        at = slice(side * width, (side + 1) * width)
        total = here_ref[:, at] + aside_ref[:, at].astype(jnp.float32)
        total = total + part[...].astype(jnp.float32)
        for i, ref in enumerate(outs):
            ref[:, at] = total[i * rows : (i + 1) * rows, :].astype(ref.dtype)


def end_body(own_ref, *refs):
    parts, (out_ref, into_ref) = refs[:-2], refs[-2:]
    total = own_ref[...]
    for part in parts:
        total = total + part[...].astype(jnp.float32)
    width = out_ref.shape[1]
    out_ref[...] = total[:, :width].astype(jnp.bfloat16)
    into_ref[...] = total[:, width:].astype(jnp.bfloat16)


def grad_body(rows_ref, acts_ref, *grads):
    ff = grads[0].shape[1]
    for i, ref in enumerate(grads):
        acts = acts_ref[:, i * ff : (i + 1) * ff]
        ref[0] = contract_first(acts, rows_ref[...]).astype(jnp.bfloat16)


def dense(tokens, expert_ids, route_weights, out_grad, gate_weight, up_weight, down_weight):
    experts = lax.axis_size("expert")
    devices = lax.axis_size("dp") * experts
    expert = lax.axis_index("expert").astype(jnp.int32).reshape(1)
    rows, width = tokens.shape
    ff = gate_weight.shape[1]
    near = tuple((k << 3, k << 3) for k in range(1, devices >> 3))
    block_rows = rows * (len(near) + 1)
    bf16, f32 = jnp.bfloat16, jnp.float32
    columns = 2 * width + experts + -experts % 128
    unit = 2 * block_rows * ff * width

    def shape(*dims, dtype=bf16):
        return jax.ShapeDtypeStruct(dims, dtype)

    def passed(value, masks):
        return from_xor(value, masks, devices)

    message, mine = kernel_call(
        pack_body,
        (shape(rows, columns), shape(8, columns - 2 * width, dtype=f32)),
        0,
        tokens,
        out_grad,
        expert_ids.T,
        route_weights.T,
        expert,
        blocks=True,
    )
    weights = kernel_call(
        load_body,
        (shape(2 * ff, width), shape(ff, width)),
        0,
        gate_weight,
        up_weight,
        down_weight,
        scratch=[pltpu.SemaphoreType.DMA((3,))],
        hbm=(0, 1, 2),
    )
    arrived = [message] + [passed(message, m) for m in near]
    block_x = jnp.concatenate([piece[:, :width] for piece in arrived], axis=0)
    block_dy = jnp.concatenate([piece[:, width:] for piece in arrived], axis=0)
    block_dy, *weights = lax.optimization_barrier((block_dy, *weights))

    aside_x, across_dy = passed(block_x, ASIDE), passed(block_dy, ACROSS)
    aside_dy, across_x = passed(block_dy, ASIDE), passed(block_x, ACROSS)
    corner_x, corner_dy = passed(aside_x, ACROSS), passed(across_dy, ASIDE)
    half = 4 * block_rows

    def both_cores(*pairs):
        own = [
            kernel_call(stack_body, shape(2 * block_rows, pair[0].shape[1]), 0, *pair)
            for pair in pairs
        ]
        return own + [passed(pair, CORE) for pair in own]

    x_pieces = both_cores((block_x, across_x), (aside_x, corner_x))
    dy_pieces = both_cores((block_dy, aside_dy), (across_dy, corner_dy))
    x_pieces[2], dy_pieces[2], dy_pieces[1] = lax.optimization_barrier(
        (x_pieces[2], dy_pieces[2], dy_pieces[1])
    )
    all_x, hidden, gate_part, up_part = kernel_call(
        functools.partial(forward_body, len(x_pieces)),
        (shape(2 * half, width),) + (shape(2 * half, ff, dtype=f32),) * 3,
        16 * unit,
        *x_pieces,
        weights[0],
    )
    all_dy, scaled, acts, own, message, corner_message = kernel_call(
        functools.partial(backward_body, len(dy_pieces)),
        (
            shape(2 * half, width),
            shape(2 * half, ff),
            shape(2 * half, 2 * ff),
            shape(half, 2 * width, dtype=f32),
            shape(half - block_rows, 2 * width),
            shape(block_rows, 2 * width),
        ),
        24 * unit,
        *dy_pieces,
        hidden,
        gate_part,
        up_part,
        mine,
        *weights,
        scratch=[pltpu.VMEM((2 * half, columns - 2 * width), f32)],
    )
    corner_came = passed(corner_message, CORE)
    corner_came, message = lax.optimization_barrier((corner_came, message))
    most_came = passed(message, CORE)

    piece, full = shape(block_rows, width), shape(block_rows, width, dtype=f32)
    out_corner, into_corner = kernel_call(corner_body, (piece, piece), 0, own, corner_came)
    here, aside, out_across, into_across = kernel_call(
        most_body,
        (shape(block_rows, 2 * width, dtype=f32), shape(block_rows, 2 * width), full, full),
        0,
        own,
        most_came,
    )
    out_turn, into_turn = passed(out_corner, ASIDE), passed(into_corner, ASIDE)
    aside = passed(aside, ASIDE)
    out_across = passed(kernel_call(turn_body, piece, 0, out_across, out_turn), ACROSS)
    into_across = passed(kernel_call(turn_body, piece, 0, into_across, into_turn), ACROSS)
    here, scaled, acts = lax.optimization_barrier((here, scaled, acts))
    grad_gate, grad_up = kernel_call(
        grad_body, (shape(*gate_weight.shape),) * 2, 16 * unit, all_x, acts
    )
    here, grad_gate, grad_up = lax.optimization_barrier((here, grad_gate, grad_up))
    mine_sum, *away = kernel_call(
        deal_body,
        (shape(rows, 2 * width, dtype=f32),) + (shape(rows, 2 * width),) * len(near),
        0,
        here,
        aside,
        out_across,
        into_across,
    )
    mine_sum, scaled = lax.optimization_barrier((mine_sum, scaled))
    grad_down = kernel_call(grad_body, shape(*down_weight.shape), 8 * unit, all_dy, scaled)
    mixed, input_grad = kernel_call(
        end_body,
        (shape(rows, width),) * 2,
        0,
        mine_sum,
        *[passed(piece, m) for m, piece in reversed(list(zip(near, away)))],
    )
    return mixed, input_grad, grad_gate, grad_up, grad_down


def shards(tokens, *others):
    experts = lax.axis_size("expert")
    devices = lax.axis_size("dp") * experts
    whole_group = tokens.shape[0] * experts <= ROW_CAP
    if whole_group and devices >= 16 and devices & (devices - 1) == 0:
        return dense(tokens, *others)
    return slotted(tokens, *others)


def solution(mesh):
    return jax.shard_map(
        shards,
        mesh=mesh,
        in_specs=(
            P(("dp", "expert"), None),
            P(("dp", "expert"), None),
            P(("dp", "expert"), None),
            P(("dp", "expert"), None),
            P("expert", "dp", None),
            P("expert", "dp", None),
            P("expert", "dp", None),
        ),
        out_specs=(
            P(("dp", "expert"), None),
            P(("dp", "expert"), None),
            P("expert", "dp", None),
            P("expert", "dp", None),
            P("expert", "dp", None),
        ),
        check_vma=False,
    )
```
